32 devices in a mesh: seq: 16 (over z, y, x), dp: 2 (over core).
Axes of the slice: x: 2, y: 2, z: 4, core: 2. Of those that a mesh axis runs over, the one named last changes fastest.
Arguments:
- queries: bfloat16 [2, 4096, 1024], P('dp', 'seq'), may hold values from -6 to 6
- keys: bfloat16 [2, 4096, 1024], P('dp', 'seq'), may hold values from -6 to 6
- values: bfloat16 [2, 4096, 1024], P('dp', 'seq'), may hold values from -36 to 36, as said below
- out_gain: float32 [1024], replicated, may hold values from 0.5 to 1.5
- grad_out: bfloat16 [2, 4096, 1024], P('dp', 'seq'), may hold values from -16 to 16, as said below
Outputs:
- grad_q: bfloat16 [2, 4096, 1024], P('dp', 'seq')
- grad_k: bfloat16 [2, 4096, 1024], P('dp', 'seq')
- grad_v: bfloat16 [2, 4096, 1024], P('dp', 'seq')
- grad_gain: float32 [1024], replicated
The draws below stay inside these ranges and needn't reach their ends.
Inputs may be any that keep to these rules, and one draw needn't show every extreme that they name: `values`: Real-valued entries. `grad_out`: Real-valued entries.
All inputs are finite; a program needn't handle non-finite values.
Results may differ from the reference program's by a relative error of at most 0.0075.
Values sent between devices are 32-bit elements; how exact they have to be, the bound alone decides.
No kernel may reach another device: no remote copies, remote signals or barrier semaphores. Data moves between devices by JAX's collectives and lax.ppermute only.
A program may use at most 128 MiB of HBM per device.

```python
import math
import jax
import jax.numpy as jnp
from jax import lax

HEADS = 8
DH = 128
BLOCK = 256
HD = 1024
LENGTH = 4096
DOCS = 2


def draw_values(key, part):
    first, second, third = jax.random.split(jax.random.fold_in(key, 11), 3)
    shape = (DOCS, LENGTH, HD)
    column_scale = 0.3 * 10.0 ** jax.random.uniform(second, (HD,), jnp.float32)
    row_scale = 0.3 * 10.0 ** jax.random.uniform(third, (DOCS, LENGTH, 1), jnp.float32)
    base = jnp.clip(jax.random.normal(first, shape, jnp.float32), -4.0, 4.0)
    return (base * column_scale * row_scale).astype(jnp.bfloat16)


def draw_grad_out(key, part):
    first = jax.random.fold_in(key, 23)
    shape = (DOCS, LENGTH, HD)
    position = jnp.arange(LENGTH, dtype=jnp.float32) / LENGTH
    rising = (1.0 + 2.0 * position)[None, :, None]
    base = jnp.clip(jax.random.normal(first, shape, jnp.float32), -4.0, 4.0) * rising
    return base.astype(jnp.bfloat16)


def shard_levels(key, extent, pieces, smallest, top_value):
    gain, own = 1.0, jax.random.fold_in(key, 6)
    for axis_at, parts in pieces:
        heights = jnp.exp(jax.random.uniform(jax.random.fold_in(own, axis_at), (parts,), jnp.float32, smallest / len(pieces), top_value / len(pieces)))
        gain = gain * jnp.repeat(heights, extent[axis_at] // parts).reshape([-1 if axis == axis_at else 1 for axis in range(len(extent))])
    return gain


def normal_values(rng, dims, spread, reach, cuts=(), kind=jnp.bfloat16):
    gain = shard_levels(rng, dims, cuts, -0.22, 0.18) if cuts else 1.0
    drawn = jax.random.normal(rng, dims, jnp.float32) * spread * gain
    return jnp.minimum(jnp.maximum(drawn, -reach), reach).astype(kind)


def setup_inputs(seed: int = 0) -> dict:
    seeds = jax.random.split(jax.random.key(seed), 6)
    queries = normal_values(seeds[0], (DOCS, LENGTH, HD), 1.0, 6.0, ((0, 2), (1, 16)))
    keys = normal_values(seeds[1], (DOCS, LENGTH, HD), 1.0, 6.0, ((0, 2), (1, 16)))
    values = draw_values(jax.random.fold_in(seeds[5], 71), 0)
    out_gain = jnp.clip(jax.random.uniform(seeds[3], (HD,), jnp.float32, 0.5, 1.5), 0.5, 1.5)
    grad_out = draw_grad_out(jax.random.fold_in(seeds[5], 71), 0)
    return dict(queries=queries, keys=keys, values=values, out_gain=out_gain, grad_out=grad_out)


EPSILON = 1e-06

def one_document(inputs_doc):
    queries_doc, keys_doc, values_doc, cotangent_doc, channel_gain = inputs_doc
    block_count = LENGTH // BLOCK
    shape_four = (block_count, BLOCK, HEADS, DH)
    query_blocks = queries_doc.reshape(shape_four).astype(jnp.float32)
    key_blocks = keys_doc.reshape(shape_four).astype(jnp.float32)
    value_blocks = values_doc.reshape(shape_four).astype(jnp.float32)
    cotangent = cotangent_doc.reshape(shape_four).astype(jnp.float32)
    causal = lax.broadcasted_iota(jnp.int32, (BLOCK, BLOCK), 0) >= lax.broadcasted_iota(jnp.int32, (BLOCK, BLOCK), 1)
    raw_scores = jnp.einsum('cthd,cshd->chts', query_blocks, key_blocks)
    scores_low = jnp.where(causal, raw_scores, jnp.float32(0.0)).astype(jnp.bfloat16).astype(jnp.float32)
    deltas = jnp.einsum('cshd,cshe->chde', key_blocks, value_blocks)
    prefix_state = (jnp.cumsum(deltas, axis=0) - deltas).astype(jnp.bfloat16).astype(jnp.float32)
    attention = jnp.einsum('chts,cshe->cthe', scores_low, value_blocks) + jnp.einsum('cthd,chde->cthe', query_blocks, prefix_state)
    root_mean = jnp.sqrt(lax.optimization_barrier(jnp.mean(attention * attention, axis=-1, keepdims=True)) + EPSILON)
    normed = attention / root_mean
    gain_terms = lax.optimization_barrier(jnp.sum(normed * cotangent, axis=(0, 1))).reshape(-1)
    scaled = channel_gain.reshape(HEADS, DH) * cotangent
    grad_attn = ((scaled - normed * lax.optimization_barrier(jnp.mean(normed * scaled, axis=-1, keepdims=True))) / root_mean).astype(jnp.bfloat16).astype(jnp.float32)
    grad_deltas = jnp.einsum('cthd,cthe->chde', query_blocks, grad_attn)
    grad_state = (lax.optimization_barrier(jnp.sum(grad_deltas, axis=0))[None] - jnp.cumsum(grad_deltas, axis=0)).astype(jnp.bfloat16).astype(jnp.float32)
    raw_grad = jnp.einsum('cthe,cshe->chts', grad_attn, value_blocks)
    grad_scores = jnp.where(causal, raw_grad, jnp.float32(0.0)).astype(jnp.bfloat16).astype(jnp.float32)
    grad_query = jnp.einsum('chts,cshd->cthd', grad_scores, key_blocks) + jnp.einsum('cthe,chde->cthd', grad_attn, prefix_state)
    grad_key = jnp.einsum('chts,cthd->cshd', grad_scores, query_blocks) + jnp.einsum('cshe,chde->cshd', value_blocks, grad_state)
    grad_value = jnp.einsum('chts,cthe->cshe', scores_low, grad_attn) + jnp.einsum('cshd,chde->cshe', key_blocks, grad_state)
    flat = (LENGTH, HD)
    return (grad_query.reshape(flat).astype(jnp.bfloat16), grad_key.reshape(flat).astype(jnp.bfloat16), grad_value.reshape(flat).astype(jnp.bfloat16), gain_terms)

def reference(queries, keys, values, out_gain, grad_out):
    gains = jnp.broadcast_to(out_gain[None], (DOCS, HD))
    grad_query, grad_key, grad_value, gain_terms = lax.map(one_document, (queries, keys, values, grad_out, gains))
    grad_gain = lax.optimization_barrier(jnp.sum(gain_terms, axis=0)) / math.sqrt(DOCS * LENGTH)
    return (grad_query, grad_key, grad_value, grad_gain)
```

```python
import math

import jax
import jax.numpy as jnp
from jax import lax
from jax.sharding import PartitionSpec as P

HEADS = 8
DH = 128
BLOCK = 256


EPSILON = 1e-06


def carried_in(part, axis, reverse):
    count = lax.axis_size(axis)
    place = lax.axis_index(axis)
    group = math.gcd(count, 4)
    member = lax.rem(place, group)
    quarters = part.reshape((group, HEADS // group) + part.shape[1:])

    def swap(array, mask):
        if mask == 0:
            return array
        return lax.ppermute(array, axis, [(s, s ^ mask) for s in range(count)])

    def before(first, second):
        return first > second if reverse else first < second

    def pick(array, at):
        return lax.dynamic_index_in_dim(array, at, 0, False)

    held = [swap(pick(quarters, member ^ mask), mask) for mask in range(group)]
    total = sum(held[1:], held[0])
    carried = jnp.zeros_like(total)
    reach = 1
    while reach * group < count:
        step = -reach * group if reverse else reach * group
        pairs = [(s, s + step) for s in range(count) if 0 <= s + step < count]
        arrived = lax.ppermute(total, axis, pairs)
        carried = carried + arrived
        total = total + arrived
        reach *= 2
    back = []
    for mask in range(group):
        target = member ^ mask
        own = carried
        for other in range(group):
            own = own + jnp.where(before(member ^ other, target), held[other], 0.0)
        back.append(swap(own, mask))
    back = jnp.stack(back)
    return jnp.concatenate([pick(back, member ^ quarter) for quarter in range(group)])


def head_major(array, blocks_dev):
    seq_rows = array.shape[1]
    return (
        array.reshape(seq_rows, HEADS, DH).transpose(1, 0, 2).reshape(HEADS, blocks_dev, BLOCK, DH)
    )


def row_major(array, full_shape):
    seq_rows = full_shape[1]
    return array.reshape(HEADS, seq_rows, DH).transpose(1, 0, 2).reshape(full_shape)


def local(queries, keys, values, out_gain, grad_out):
    seq_rows = queries.shape[1]
    blocks_dev = seq_rows // BLOCK
    query_blocks = head_major(queries, blocks_dev)
    key_blocks = head_major(keys, blocks_dev)
    value_blocks = head_major(values, blocks_dev)
    causal = lax.broadcasted_iota(jnp.int32, (BLOCK, BLOCK), 0) >= lax.broadcasted_iota(
        jnp.int32, (BLOCK, BLOCK), 1
    )
    raw_scores = jnp.einsum(
        "hctd,hcsd->hcts", query_blocks, key_blocks, preferred_element_type=jnp.float32
    )
    scores_low = jnp.where(causal, raw_scores, 0.0).astype(jnp.bfloat16)
    deltas = jnp.einsum(
        "hcsd,hcse->hcde", key_blocks, value_blocks, preferred_element_type=jnp.float32
    )
    local_total = jnp.sum(deltas, axis=1)
    carried = carried_in(local_total, "seq", False)
    prefix_state = (carried[:, None] + jnp.cumsum(deltas, axis=1) - deltas).astype(jnp.bfloat16)
    attention = jnp.einsum(
        "hcts,hcse->hcte", scores_low, value_blocks, preferred_element_type=jnp.float32
    )
    attention = attention + jnp.einsum(
        "hctd,hcde->hcte", query_blocks, prefix_state, preferred_element_type=jnp.float32
    )
    root_mean = jnp.sqrt(jnp.mean(attention * attention, axis=-1, keepdims=True) + EPSILON)
    normed = attention / root_mean
    cotangent = head_major(grad_out, blocks_dev).astype(jnp.float32)
    gain_terms = jnp.sum(normed * cotangent, axis=(1, 2)).reshape(-1)
    scaled = out_gain.reshape(HEADS, 1, 1, DH) * cotangent
    grad_attn = (
        (scaled - normed * jnp.mean(normed * scaled, axis=-1, keepdims=True)) / root_mean
    ).astype(jnp.bfloat16)
    grad_deltas = jnp.einsum(
        "hctd,hcte->hcde", query_blocks, grad_attn, preferred_element_type=jnp.float32
    )
    grad_total = jnp.sum(grad_deltas, axis=1)
    after_local = grad_total[:, None] - jnp.cumsum(grad_deltas, axis=1)
    later_sum = carried_in(grad_total, "seq", True)
    grad_state = (later_sum[:, None] + after_local).astype(jnp.bfloat16)
    raw_grad = jnp.einsum(
        "hcte,hcse->hcts", grad_attn, value_blocks, preferred_element_type=jnp.float32
    )
    grad_scores = jnp.where(causal, raw_grad, 0.0).astype(jnp.bfloat16)
    grad_query = jnp.einsum(
        "hcts,hcsd->hctd", grad_scores, key_blocks, preferred_element_type=jnp.float32
    )
    grad_query = grad_query + jnp.einsum(
        "hcte,hcde->hctd", grad_attn, prefix_state, preferred_element_type=jnp.float32
    )
    grad_key = jnp.einsum(
        "hcts,hctd->hcsd", grad_scores, query_blocks, preferred_element_type=jnp.float32
    )
    grad_key = grad_key + jnp.einsum(
        "hcse,hcde->hcsd", value_blocks, grad_state, preferred_element_type=jnp.float32
    )
    grad_value = jnp.einsum(
        "hcts,hcte->hcse", scores_low, grad_attn, preferred_element_type=jnp.float32
    )
    grad_value = grad_value + jnp.einsum(
        "hcsd,hcde->hcse", key_blocks, grad_state, preferred_element_type=jnp.float32
    )
    gain_total = lax.psum(gain_terms, ("seq", "dp"))
    position_count = lax.axis_size("seq") * lax.axis_size("dp") * seq_rows
    grad_gain = gain_total / math.sqrt(position_count)
    return (
        row_major(grad_query.astype(jnp.bfloat16), queries.shape),
        row_major(grad_key.astype(jnp.bfloat16), queries.shape),
        row_major(grad_value.astype(jnp.bfloat16), queries.shape),
        grad_gain,
    )


def solution(mesh):
    return jax.shard_map(
        local,
        mesh=mesh,
        in_specs=(
            P("dp", "seq", None),
            P("dp", "seq", None),
            P("dp", "seq", None),
            P(),
            P("dp", "seq", None),
        ),
        out_specs=(P("dp", "seq", None), P("dp", "seq", None), P("dp", "seq", None), P()),
        check_vma=False,
    )
```

```python
import math

import jax
import jax.numpy as jnp
from jax import lax
from jax.sharding import PartitionSpec as P

HEADS = 8
DH = 128
BLOCK = 256


EPSILON = 1e-06


def carried_in(part, axis, reverse):
    count = lax.axis_size(axis)
    place = lax.axis_index(axis)
    group = math.gcd(count, HEADS)
    owned = HEADS // group
    rows = part.shape[1]
    teams = [list(range(first, first + group)) for first in range(0, count, group)]

    def spread(array):
        return lax.all_to_all(array, axis, 0, 0, axis_index_groups=teams)

    held = spread(part.reshape(group, owned, rows, DH))
    order = range(group - 1, -1, -1) if reverse else range(group)
    total = jnp.zeros_like(held[0])
    ahead = [None] * group
    for member in order:
        ahead[member] = total
        total = total + held[member]
    carried = jnp.zeros_like(total)
    mask = group
    while mask < count:
        arrived = lax.ppermute(total, axis, [(s, s ^ mask) for s in range(count)])
        later = (place & mask) != 0
        carried = carried + jnp.where(later != reverse, arrived, 0.0)
        total = total + arrived
        mask *= 2
    summed = jnp.stack([ahead[member] + carried for member in range(group)])
    if rows > DH:
        summed = jnp.concatenate(
            [summed[:, :, :DH], jnp.broadcast_to(total[:, DH:], (group, owned, rows - DH, DH))], axis=2
        )
    return spread(summed).reshape(part.shape)


def head_major(array, blocks_dev):
    seq_rows = array.shape[1]
    return (
        array.reshape(seq_rows, HEADS, DH).transpose(1, 0, 2).reshape(HEADS, blocks_dev, BLOCK, DH)
    )


def row_major(array, full_shape):
    seq_rows = full_shape[1]
    return array.reshape(HEADS, seq_rows, DH).transpose(1, 0, 2).reshape(full_shape)


def local(queries, keys, values, out_gain, grad_out):
    seq_rows = queries.shape[1]
    blocks_dev = seq_rows // BLOCK
    query_blocks = head_major(queries, blocks_dev)
    key_blocks = head_major(keys, blocks_dev)
    value_blocks = head_major(values, blocks_dev)
    causal = lax.broadcasted_iota(jnp.int32, (BLOCK, BLOCK), 0) >= lax.broadcasted_iota(
        jnp.int32, (BLOCK, BLOCK), 1
    )
    raw_scores = jnp.einsum(
        "hctd,hcsd->hcts", query_blocks, key_blocks, preferred_element_type=jnp.float32
    )
    scores_low = jnp.where(causal, raw_scores, 0.0).astype(jnp.bfloat16)
    deltas = jnp.einsum(
        "hcsd,hcse->hcde", key_blocks, value_blocks, preferred_element_type=jnp.float32
    )
    local_total = jnp.sum(deltas, axis=1)
    carried = carried_in(local_total, "seq", False)
    prefix_state = (carried[:, None] + jnp.cumsum(deltas, axis=1) - deltas).astype(jnp.bfloat16)
    attention = jnp.einsum(
        "hcts,hcse->hcte", scores_low, value_blocks, preferred_element_type=jnp.float32
    )
    attention = attention + jnp.einsum(
        "hctd,hcde->hcte", query_blocks, prefix_state, preferred_element_type=jnp.float32
    )
    root_mean = jnp.sqrt(jnp.mean(attention * attention, axis=-1, keepdims=True) + EPSILON)
    normed = attention / root_mean
    cotangent = head_major(grad_out, blocks_dev).astype(jnp.float32)
    gain_terms = jnp.sum(normed * cotangent, axis=(1, 2)).reshape(-1)
    scaled = out_gain.reshape(HEADS, 1, 1, DH) * cotangent
    grad_attn = (
        (scaled - normed * jnp.mean(normed * scaled, axis=-1, keepdims=True)) / root_mean
    ).astype(jnp.bfloat16)
    grad_deltas = jnp.einsum(
        "hctd,hcte->hcde", query_blocks, grad_attn, preferred_element_type=jnp.float32
    )
    grad_total = jnp.sum(grad_deltas, axis=1)
    after_local = grad_total[:, None] - jnp.cumsum(grad_deltas, axis=1)
    extra = jnp.broadcast_to(gain_terms.reshape(HEADS, 1, DH), (HEADS, 8, DH))
    later_all = carried_in(jnp.concatenate([grad_total, extra], axis=1), "seq", True)
    later_sum = later_all[:, :DH]
    gain_total = later_all[:, DH].reshape(-1)
    mask = 1
    while mask < lax.axis_size("dp"):
        pairs = [(d, d ^ mask) for d in range(lax.axis_size("dp"))]
        gain_total = gain_total + lax.ppermute(gain_total, "dp", pairs)
        mask *= 2
    grad_state = (later_sum[:, None] + after_local).astype(jnp.bfloat16)
    raw_grad = jnp.einsum(
        "hcte,hcse->hcts", grad_attn, value_blocks, preferred_element_type=jnp.float32
    )
    grad_scores = jnp.where(causal, raw_grad, 0.0).astype(jnp.bfloat16)
    grad_query = jnp.einsum(
        "hcts,hcsd->hctd", grad_scores, key_blocks, preferred_element_type=jnp.float32
    )
    grad_query = grad_query + jnp.einsum(
        "hcte,hcde->hctd", grad_attn, prefix_state, preferred_element_type=jnp.float32
    )
    grad_key = jnp.einsum(
        "hcts,hctd->hcsd", grad_scores, query_blocks, preferred_element_type=jnp.float32
    )
    grad_key = grad_key + jnp.einsum(
        "hcse,hcde->hcsd", value_blocks, grad_state, preferred_element_type=jnp.float32
    )
    grad_value = jnp.einsum(
        "hcts,hcte->hcse", scores_low, grad_attn, preferred_element_type=jnp.float32
    )
    grad_value = grad_value + jnp.einsum(
        "hcsd,hcde->hcse", key_blocks, grad_state, preferred_element_type=jnp.float32
    )
    position_count = lax.axis_size("seq") * lax.axis_size("dp") * seq_rows
    grad_gain = gain_total / math.sqrt(position_count)
    return (
        row_major(grad_query.astype(jnp.bfloat16), queries.shape),
        row_major(grad_key.astype(jnp.bfloat16), queries.shape),
        row_major(grad_value.astype(jnp.bfloat16), queries.shape),
        grad_gain,
    )


def solution(mesh):
    return jax.shard_map(
        local,
        mesh=mesh,
        in_specs=(
            P("dp", "seq", None),
            P("dp", "seq", None),
            P("dp", "seq", None),
            P(),
            P("dp", "seq", None),
        ),
        out_specs=(P("dp", "seq", None), P("dp", "seq", None), P("dp", "seq", None), P()),
        check_vma=False,
    )
```

```python
import functools
import math

import jax
import jax.numpy as jnp
from jax import lax
from jax.experimental import pallas as pl
from jax.experimental.pallas import tpu as pltpu
from jax.sharding import PartitionSpec as P

HEADS = 8
DH = 128
BLOCK = 256
CHAINS = 2
CHAIN_HEADS = HEADS // CHAINS
WIDE = CHAIN_HEADS * DH
GAIN_ROWS = 8
EPSILON = 1e-06

NT = (((1,), (1,)), ((), ()))
TN = (((0,), (0,)), ((), ()))
NN = (((1,), (0,)), ((), ()))


def dot(left, right, dims):
    return lax.dot_general(left, right, dims, preferred_element_type=jnp.float32)


def columns(member, mask):
    return pl.ds(pl.multiple_of((member ^ mask) * DH, DH), DH)


def causal():
    shape = (BLOCK, BLOCK)
    return lax.broadcasted_iota(jnp.int32, shape, 0) >= lax.broadcasted_iota(jnp.int32, shape, 1)


def delta_body(member_ref, key_ref, value_ref, *delta_refs):
    for mask, delta_ref in enumerate(delta_refs):
        at = columns(member_ref[0], mask)
        delta_ref[...] = dot(key_ref[:, at], value_ref[:, at], TN)


def inner_body(query_ref, key_ref, value_ref, inner_ref):
    keep = causal()
    for head in range(CHAIN_HEADS):
        at = pl.ds(head * DH, DH)
        raw = dot(query_ref[:, at], key_ref[:, at], NT)
        scores = jnp.where(keep, raw, 0.0).astype(jnp.bfloat16)
        inner_ref[:, at] = dot(scores, value_ref[:, at], NN)


def norm_body(member_ref, query_ref, grad_ref, inner_ref, gain_ref, *refs):
    state_refs, (attn_ref, *delta_refs) = refs[:CHAIN_HEADS], refs[CHAIN_HEADS:]
    for mask, state_ref in enumerate(state_refs):
        at = columns(member_ref[0], mask)
        query = query_ref[:, at]
        attn = inner_ref[:, at] + dot(query, state_ref[...].astype(jnp.bfloat16), NN)
        root = jnp.sqrt(jnp.mean(attn * attn, axis=-1, keepdims=True) + EPSILON)
        normed = attn / root
        cotangent = grad_ref[:, at].astype(jnp.float32)
        product = normed * cotangent
        gain = gain_ref[:, at]
        scaled = gain * cotangent
        shared = jnp.mean(normed * scaled, axis=-1, keepdims=True)
        grad_attn = ((scaled - normed * shared) / root).astype(jnp.bfloat16)
        attn_ref[:, at] = grad_attn
        delta_refs[mask][:DH] = dot(query, grad_attn, TN)
        delta_refs[mask][DH:] = jnp.broadcast_to(jnp.sum(product, axis=0, keepdims=True), (GAIN_ROWS, DH))


def partial_body(member_ref, query_ref, key_ref, value_ref, attn_ref, *refs):
    state_refs, (grad_query_ref, key_part_ref, value_part_ref) = refs[:CHAIN_HEADS], refs[-3:]
    keep = causal()
    for mask, state_ref in enumerate(state_refs):
        at = columns(member_ref[0], mask)
        query, key, value, grad_attn = query_ref[:, at], key_ref[:, at], value_ref[:, at], attn_ref[:, at]
        scores = jnp.where(keep, dot(query, key, NT), 0.0).astype(jnp.bfloat16)
        grad_scores = jnp.where(keep, dot(grad_attn, value, NT), 0.0).astype(jnp.bfloat16)
        carried = dot(grad_attn, state_ref[...].astype(jnp.bfloat16), NT)
        grad_query_ref[:, at] = (dot(grad_scores, key, NN) + carried).astype(jnp.bfloat16)
        key_part_ref[:, at] = dot(grad_scores, query, TN)
        value_part_ref[:, at] = dot(scores, grad_attn, TN)


def final_body(member_ref, key_ref, value_ref, *refs):
    parts, states = refs[: 2 * CHAINS], refs[2 * CHAINS : -2]
    grad_key_ref, grad_value_ref = refs[-2:]
    for chain in range(CHAINS):
        for mask in range(CHAIN_HEADS):
            at = columns(member_ref[0], mask)
            wide = pl.ds(pl.multiple_of(chain * WIDE + (member_ref[0] ^ mask) * DH, DH), DH)
            state = states[chain * CHAIN_HEADS + mask][:DH].astype(jnp.bfloat16)
            key_part, value_part = parts[2 * chain][:, at], parts[2 * chain + 1][:, at]
            grad_key_ref[:, wide] = (key_part + dot(value_ref[:, wide], state, NT)).astype(jnp.bfloat16)
            grad_value_ref[:, wide] = (value_part + dot(key_ref[:, wide], state, NN)).astype(jnp.bfloat16)


def whole(*shape):
    return pl.BlockSpec(shape, lambda step: (0,) * len(shape))


def part_of(chain):
    return pl.BlockSpec((BLOCK, WIDE), lambda step: (0, chain))


MEMBER = pl.BlockSpec(memory_space=pltpu.SMEM)


def call(body, in_specs, out_specs, outs, flops, name, aliases=None):
    return pl.pallas_call(
        body,
        grid=(1,),
        in_specs=in_specs,
        out_specs=out_specs,
        out_shape=outs,
        input_output_aliases=aliases or {},
        compiler_params=pltpu.CompilerParams(vmem_limit_bytes=32 * 1024 * 1024),
        cost_estimate=pl.CostEstimate(flops=flops, bytes_accessed=2 << 20, transcendentals=0),
        name=name,
    )


def swap(array, axis, mask):
    if mask == 0:
        return array
    return lax.ppermute(array, axis, [(s, s ^ mask) for s in range(lax.axis_size(axis))])


def carried_in(held, axis, reverse):
    count, place = lax.axis_size(axis), lax.axis_index(axis)
    group = len(held)
    member = lax.rem(place, group)

    def later(first, second):
        return first < second if reverse else first > second

    held = [swap(piece, axis, mask) for mask, piece in enumerate(held)]
    total = functools.reduce(jnp.add, held)
    carried = jnp.zeros_like(total)
    mask = group
    while mask < count:
        arrived = swap(total, axis, mask)
        carried = carried + jnp.where(later(place, place ^ mask), arrived, 0.0)
        total = total + arrived
        mask *= 2
    back = []
    for mask in range(group):
        own = carried
        for other in range(group):
            own = own + jnp.where(later(member ^ mask, member ^ other), held[other], 0.0)
        if own.shape[0] > DH:
            own = jnp.concatenate([own[:DH], total[DH:]])
        back.append(swap(own, axis, mask))
    return back


def local(queries, keys, values, out_gain, grad_out):
    full = queries.shape
    flat = (full[0] * full[1], full[2])
    assert flat == (BLOCK, HEADS * DH)
    query, key, value, grad = (a.reshape(flat) for a in (queries, keys, values, grad_out))
    gain = out_gain.reshape(1, HEADS * DH)
    member = lax.rem(lax.axis_index("seq"), CHAIN_HEADS)
    member_in = member.astype(jnp.int32).reshape(1)
    square = jax.ShapeDtypeStruct((DH, DH), jnp.float32)
    taller = jax.ShapeDtypeStruct((DH + GAIN_ROWS, DH), jnp.float32)
    wide_float = jax.ShapeDtypeStruct((BLOCK, WIDE), jnp.float32)
    wide_low = jax.ShapeDtypeStruct((BLOCK, WIDE), jnp.bfloat16)
    full_low = jax.ShapeDtypeStruct(flat, jnp.bfloat16)
    squares = [whole(DH, DH)] * CHAIN_HEADS
    tallers = [whole(DH + GAIN_ROWS, DH)] * CHAIN_HEADS
    unit = 2 * BLOCK * DH * DH * CHAIN_HEADS

    states, inner = [], []
    for chain in range(CHAINS):
        cols = part_of(chain)
        deltas = call(
            delta_body, [MEMBER, cols, cols], squares, [square] * CHAIN_HEADS, unit, "delta"
        )(member_in, key, value)
        states.append(carried_in(deltas, "seq", False))
        inner.append(
            call(inner_body, [cols] * 3, whole(BLOCK, WIDE), wide_float, 4 * unit, "inner")(query, key, value)
        )

    later, parts, grad_query = [], [], None
    for chain in range(CHAINS):
        cols = part_of(chain)
        attn, *deltas = call(
            norm_body,
            [MEMBER, cols, cols, whole(BLOCK, WIDE), pl.BlockSpec((1, WIDE), lambda step, c=chain: (0, c))] + squares,
            [whole(BLOCK, WIDE)] + tallers,
            [wide_low] + [taller] * CHAIN_HEADS,
            2 * unit,
            "norm",
        )(member_in, query, grad, inner[chain], gain, *states[chain])
        later.append(carried_in(deltas, "seq", True))
        held = [] if grad_query is None else [grad_query]
        grad_query, key_part, value_part = call(
            partial_body,
            [MEMBER, cols, cols, cols, whole(BLOCK, WIDE)] + squares + [pl.BlockSpec(memory_space=pl.ANY)] * len(held),
            [cols, whole(BLOCK, WIDE), whole(BLOCK, WIDE)],
            [full_low, wide_float, wide_float],
            11 * unit,
            "partial",
            {5 + CHAIN_HEADS: 0} if held else None,
        )(member_in, query, key, value, attn, *states[chain], *held)
        parts += [key_part, value_part]

    gain_terms = jnp.stack([piece[DH] for chain in later for piece in chain])
    mask = 1
    while mask < lax.axis_size("dp"):
        gain_terms = gain_terms + swap(gain_terms, "dp", mask)
        mask *= 2
    grad_key, grad_value = call(
        final_body,
        [MEMBER] + [whole(*flat)] * 2 + [whole(BLOCK, WIDE)] * (2 * CHAINS) + tallers * CHAINS,
        [whole(*flat)] * 2,
        [full_low] * 2,
        4 * unit,
        "final",
    )(member_in, key, value, *parts, *[piece for chain in later for piece in chain])
    gain_terms = gain_terms.reshape(CHAINS, CHAIN_HEADS, DH)
    ordered = []
    for head in range(CHAIN_HEADS):
        picked = jnp.zeros((CHAINS, DH), jnp.float32)
        for mask in range(CHAIN_HEADS):
            picked = picked + jnp.where((member ^ mask) == head, gain_terms[:, mask], 0.0)
        ordered.append(picked)
    positions = lax.axis_size("seq") * lax.axis_size("dp") * BLOCK
    grad_gain = jnp.stack(ordered, axis=1).reshape(HEADS * DH) / math.sqrt(positions)
    return (grad_query.reshape(full), grad_key.reshape(full), grad_value.reshape(full), grad_gain)


def solution(mesh):
    sharded = P("dp", "seq", None)
    return jax.shard_map(
        local,
        mesh=mesh,
        in_specs=(sharded, sharded, sharded, P(), sharded),
        out_specs=(sharded, sharded, sharded, P()),
        check_vma=False,
    )
```

```python
import math

import jax
import jax.numpy as jnp
from jax import lax
from jax.experimental import pallas as pl
from jax.experimental.pallas import tpu as pltpu
from jax.sharding import PartitionSpec as P

HEADS = 8
DH = 128
BLOCK = 256
CHAINS = 2
CHAIN_HEADS = HEADS // CHAINS
WIDE = CHAIN_HEADS * DH
GAIN_ROWS = 8
HALF = CHAIN_HEADS // 2
EPSILON = 1e-06

NT = (((1,), (1,)), ((), ()))
TN = (((0,), (0,)), ((), ()))
NN = (((1,), (0,)), ((), ()))


def dot(left, right, dims):
    return lax.dot_general(left, right, dims, preferred_element_type=jnp.float32)


def columns(member, mask):
    return pl.ds(pl.multiple_of((member ^ mask) * DH, DH), DH)


def causal():
    shape = (BLOCK, BLOCK)
    return lax.broadcasted_iota(jnp.int32, shape, 0) >= lax.broadcasted_iota(jnp.int32, shape, 1)


def delta_body(member_ref, key_ref, value_ref, *delta_refs):
    for mask in range(CHAIN_HEADS):
        at = columns(member_ref[0], mask)
        delta_refs[mask // HALF][mask % HALF] = dot(key_ref[:, at], value_ref[:, at], TN)


def inner_body(query_ref, key_ref, value_ref, inner_ref):
    keep = causal()
    for head in range(CHAIN_HEADS):
        at = pl.ds(head * DH, DH)
        raw = dot(query_ref[:, at], key_ref[:, at], NT)
        scores = jnp.where(keep, raw, 0.0).astype(jnp.bfloat16)
        inner_ref[:, at] = dot(scores, value_ref[:, at], NN)


def norm_body(member_ref, query_ref, grad_ref, inner_ref, gain_ref, *refs):
    state_refs, (attn_ref, *delta_refs) = refs[:2], refs[2:]
    for mask in range(CHAIN_HEADS):
        at = columns(member_ref[0], mask)
        state_ref, delta_ref = state_refs[mask // HALF].at[mask % HALF], delta_refs[mask // HALF].at[mask % HALF]
        query = query_ref[:, at]
        attn = inner_ref[:, at] + dot(query, state_ref[...].astype(jnp.bfloat16), NN)
        root = jnp.sqrt(jnp.mean(attn * attn, axis=-1, keepdims=True) + EPSILON)
        normed = attn / root
        cotangent = grad_ref[:, at].astype(jnp.float32)
        scaled = gain_ref[:, at] * cotangent
        shared = jnp.mean(normed * scaled, axis=-1, keepdims=True)
        grad_attn = ((scaled - normed * shared) / root).astype(jnp.bfloat16)
        attn_ref[:, at] = grad_attn
        terms = jnp.sum(normed * cotangent, axis=0, keepdims=True)
        delta_ref[:DH] = dot(query, grad_attn, TN)
        delta_ref[DH:] = jnp.broadcast_to(terms, (GAIN_ROWS, DH))


def partial_body(member_ref, query_ref, key_ref, value_ref, attn_ref, *refs):
    state_refs, (grad_query_ref, key_part_ref, value_part_ref) = refs[:2], refs[-3:]
    keep = causal()
    for mask in range(CHAIN_HEADS):
        at = columns(member_ref[0], mask)
        query, key, value, grad_attn = query_ref[:, at], key_ref[:, at], value_ref[:, at], attn_ref[:, at]
        state = state_refs[mask // HALF][mask % HALF].astype(jnp.bfloat16)
        scores = jnp.where(keep, dot(query, key, NT), 0.0).astype(jnp.bfloat16)
        grad_scores = jnp.where(keep, dot(grad_attn, value, NT), 0.0).astype(jnp.bfloat16)
        grad_query_ref[:, at] = (dot(grad_scores, key, NN) + dot(grad_attn, state, NT)).astype(jnp.bfloat16)
        key_part_ref[:, at] = dot(grad_scores, query, TN)
        value_part_ref[:, at] = dot(scores, grad_attn, TN)


def final_body(member_ref, key_ref, value_ref, key_part_ref, value_part_ref, *refs):
    state_refs, (grad_key_ref, grad_value_ref) = refs[:2], refs[-2:]
    for mask in range(CHAIN_HEADS):
        at = columns(member_ref[0], mask)
        state = state_refs[mask // HALF][mask % HALF, :DH].astype(jnp.bfloat16)
        grad_key_ref[:, at] = (key_part_ref[:, at] + dot(value_ref[:, at], state, NT)).astype(jnp.bfloat16)
        grad_value_ref[:, at] = (value_part_ref[:, at] + dot(key_ref[:, at], state, NN)).astype(jnp.bfloat16)


def gain_body(member_ref, *refs):
    piece_refs, gain_ref = refs[:-1], refs[-1]
    for chain in range(CHAINS):
        for mask in range(CHAIN_HEADS):
            row = chain * CHAIN_HEADS + (member_ref[0] ^ mask)
            piece_ref = piece_refs[2 * chain + mask // HALF]
            gain_ref[pl.ds(row, 1), :] = piece_ref[mask % HALF, DH : DH + 1, :]


def whole(*shape):
    return pl.BlockSpec(shape, lambda step: (0,) * len(shape))


def part_of(chain):
    return pl.BlockSpec((BLOCK, WIDE), lambda step: (0, chain))


MEMBER = pl.BlockSpec(memory_space=pltpu.SMEM)


def call(body, in_specs, out_specs, outs, flops, name, aliases=None):
    return pl.pallas_call(
        body,
        grid=(1,),
        in_specs=in_specs,
        out_specs=out_specs,
        out_shape=outs,
        input_output_aliases=aliases or {},
        compiler_params=pltpu.CompilerParams(vmem_limit_bytes=16 * 1024 * 1024),
        cost_estimate=pl.CostEstimate(flops=flops, bytes_accessed=2 << 20, transcendentals=0),
        name=name,
    )


def swap(array, axis, mask):
    if mask == 0:
        return array
    return lax.ppermute(array, axis, [(s, s ^ mask) for s in range(lax.axis_size(axis))])


def carried_in(kept, sent, axis, reverse):
    count, place = lax.axis_size(axis), lax.axis_index(axis)
    is_state = lax.broadcasted_iota(jnp.int32, kept.shape[1:], 0) < DH

    def later(mask):
        bit = (place & mask) != 0
        return bit != reverse

    other = swap(sent, axis, 1)
    row = kept + other
    beside = swap(row[1], axis, 2)
    total = row[0] + beside
    carried = jnp.where(is_state, 0.0, total)
    mask = 4
    while mask < count:
        arrived = swap(total, axis, mask)
        carried = carried + jnp.where(is_state & ~later(mask), 0.0, arrived)
        total = total + arrived
        mask *= 2
    back = swap(carried + jnp.where(is_state & ~later(2), row[0], 0.0), axis, 2)
    before = jnp.stack([carried + jnp.where(is_state & later(2), beside, 0.0), back])
    mine = before + jnp.where(is_state & later(1), other, 0.0)
    return mine, swap(before + jnp.where(is_state & ~later(1), kept, 0.0), axis, 1)


def local(queries, keys, values, out_gain, grad_out):
    full = queries.shape
    flat = (full[0] * full[1], full[2])
    assert flat == (BLOCK, HEADS * DH)
    query, key, value, grad = (a.reshape(flat) for a in (queries, keys, values, grad_out))
    gain = out_gain.reshape(1, HEADS * DH)
    assert lax.axis_size("seq") % CHAIN_HEADS == 0
    place = lax.axis_index("seq")
    member = ((place & 1) * 2 + ((place >> 1) & 1)).astype(jnp.int32).reshape(1)
    half = jax.ShapeDtypeStruct((HALF, DH, DH), jnp.float32)
    taller = jax.ShapeDtypeStruct((HALF, DH + GAIN_ROWS, DH), jnp.float32)
    wide_float = jax.ShapeDtypeStruct((BLOCK, WIDE), jnp.float32)
    wide_low = jax.ShapeDtypeStruct((BLOCK, WIDE), jnp.bfloat16)
    full_low = jax.ShapeDtypeStruct(flat, jnp.bfloat16)
    halves = [whole(*half.shape)] * 2
    tallers = [whole(*taller.shape)] * 2
    wide = whole(BLOCK, WIDE)
    spot = pl.BlockSpec(memory_space=pl.ANY)
    unit = 2 * BLOCK * DH * DH * CHAIN_HEADS

    states, inner = [], []
    for chain in range(CHAINS):
        cols = part_of(chain)
        kept, sent = call(delta_body, [MEMBER, cols, cols], halves, [half] * 2, 6 * unit, "delta")(member, key, value)
        states.append(carried_in(kept, sent, "seq", False))
        inner.append(call(inner_body, [cols] * 3, wide, wide_float, 16 * unit, "inner")(query, key, value))

    later, parts, grad_query = [], [], []
    for chain in range(CHAINS):
        cols = part_of(chain)
        attn, kept, sent = call(
            norm_body,
            [MEMBER, cols, cols, wide, pl.BlockSpec((1, WIDE), lambda step, c=chain: (0, c))] + halves,
            [wide] + tallers,
            [wide_low] + [taller] * 2,
            16 * unit,
            "norm",
        )(member, query, grad, inner[chain], gain, *states[chain])
        later.append(carried_in(kept, sent, "seq", True))
        *grad_query, key_part, value_part = call(
            partial_body,
            [MEMBER, cols, cols, cols, wide] + halves + [spot] * len(grad_query),
            [cols, wide, wide],
            [full_low, wide_float, wide_float],
            48 * unit,
            "partial",
            {7: 0} if grad_query else None,
        )(member, query, key, value, attn, *states[chain], *grad_query)
        parts.append((key_part, value_part))

    gain_terms = call(
        gain_body, [MEMBER] + tallers * CHAINS, whole(HEADS, DH),
        jax.ShapeDtypeStruct((HEADS, DH), jnp.float32), unit, "gain",
    )(member, *[piece for chain in later for piece in chain])
    mask = 1
    while mask < lax.axis_size("dp"):
        gain_terms = gain_terms + swap(gain_terms, "dp", mask)
        mask *= 2
    grads = []
    for chain in range(CHAINS):
        cols = part_of(chain)
        grads = call(
            final_body,
            [MEMBER, cols, cols, wide, wide] + tallers + [spot] * len(grads),
            [cols] * 2,
            [full_low] * 2,
            16 * unit,
            "final",
            {7: 0, 8: 1} if grads else None,
        )(member, key, value, *parts[chain], *later[chain], *grads)
    grad_key, grad_value = grads
    positions = lax.axis_size("seq") * lax.axis_size("dp") * BLOCK
    grad_gain = gain_terms.reshape(HEADS * DH) / math.sqrt(positions)
    return (grad_query[0].reshape(full), grad_key.reshape(full), grad_value.reshape(full), grad_gain)


def solution(mesh):
    sharded = P("dp", "seq", None)
    return jax.shard_map(
        local,
        mesh=mesh,
        in_specs=(sharded, sharded, sharded, P(), sharded),
        out_specs=(sharded, sharded, sharded, P()),
        check_vma=False,
    )
```

```python
import functools
import math

import jax
import jax.numpy as jnp
from jax import lax
from jax.experimental import pallas as pl
from jax.experimental.pallas import tpu as pltpu
from jax.sharding import PartitionSpec as P

HEADS = 8
DH = 128
BLOCK = 256
GROUP = 8
CHUNKS = 2
CHUNK_HEADS = HEADS // CHUNKS
WIDE = CHUNK_HEADS * DH
GAIN_ROWS = 8
EPSILON = 1e-06

NT = (((1,), (1,)), ((), ()))
TN = (((0,), (0,)), ((), ()))
NN = (((1,), (0,)), ((), ()))


def dot(left, right, dims):
    return lax.dot_general(left, right, dims, preferred_element_type=jnp.float32)


def columns(member, mask):
    return pl.ds(pl.multiple_of((member ^ mask) * DH, DH), DH)


def causal():
    shape = (BLOCK, BLOCK)
    return lax.broadcasted_iota(jnp.int32, shape, 0) >= lax.broadcasted_iota(jnp.int32, shape, 1)


def delta_body(member_ref, key_ref, value_ref, *delta_refs):
    for mask, delta_ref in enumerate(delta_refs):
        at = columns(member_ref[0], mask)
        delta_ref[...] = dot(key_ref[:, at], value_ref[:, at], TN)


def inner_body(query_ref, key_ref, value_ref, inner_ref):
    keep = causal()
    for head in range(HEADS):
        at = pl.ds(head * DH, DH)
        raw = dot(query_ref[:, at], key_ref[:, at], NT)
        scores = jnp.where(keep, raw, 0.0).astype(jnp.bfloat16)
        inner_ref[:, at] = dot(scores, value_ref[:, at], NN)


def norm_body(member_ref, query_ref, grad_ref, inner_ref, gain_ref, *refs):
    state_refs, (attn_ref, low_ref, *delta_refs) = refs[:GROUP], refs[GROUP:]
    for mask, (state_ref, delta_ref) in enumerate(zip(state_refs, delta_refs)):
        at = columns(member_ref[0], mask)
        query = query_ref[:, at]
        state = state_ref[...].astype(jnp.bfloat16)
        low_ref[pl.ds(member_ref[0] ^ mask, 1)] = state[None]
        attn = inner_ref[:, at] + dot(query, state, NN)
        root = jnp.sqrt(jnp.mean(attn * attn, axis=-1, keepdims=True) + EPSILON)
        normed = attn / root
        cotangent = grad_ref[:, at].astype(jnp.float32)
        scaled = gain_ref[:, at] * cotangent
        shared = jnp.mean(normed * scaled, axis=-1, keepdims=True)
        grad_attn = ((scaled - normed * shared) / root).astype(jnp.bfloat16)
        attn_ref[:, at] = grad_attn
        terms = jnp.sum(normed * cotangent, axis=0, keepdims=True)
        delta_ref[:DH] = dot(query, grad_attn, TN)
        delta_ref[DH:] = jnp.broadcast_to(terms, (GAIN_ROWS, DH))


def partial_body(query_ref, key_ref, value_ref, attn_ref, state_ref, *refs):
    grad_query_ref, key_part_ref, value_part_ref = refs[-3:]
    keep = causal()
    for head in range(CHUNK_HEADS):
        at = pl.ds(head * DH, DH)
        query, key, value, grad_attn = query_ref[:, at], key_ref[:, at], value_ref[:, at], attn_ref[:, at]
        scores = jnp.where(keep, dot(query, key, NT), 0.0).astype(jnp.bfloat16)
        grad_scores = jnp.where(keep, dot(grad_attn, value, NT), 0.0).astype(jnp.bfloat16)
        carried = dot(grad_attn, state_ref[head], NT)
        grad_query_ref[:, at] = (dot(grad_scores, key, NN) + carried).astype(jnp.bfloat16)
        key_part_ref[:, at] = dot(grad_scores, query, TN)
        value_part_ref[:, at] = dot(scores, grad_attn, TN)


def final_body(member_ref, key_ref, value_ref, key_part_ref, value_part_ref, *refs):
    state_refs, (grad_key_ref, grad_value_ref) = refs[:GROUP], refs[GROUP:]
    for mask, state_ref in enumerate(state_refs):
        at = columns(member_ref[0], mask)
        state = state_ref[:DH].astype(jnp.bfloat16)
        grad_key_ref[:, at] = (key_part_ref[:, at] + dot(value_ref[:, at], state, NT)).astype(jnp.bfloat16)
        grad_value_ref[:, at] = (value_part_ref[:, at] + dot(key_ref[:, at], state, NN)).astype(jnp.bfloat16)


def prefix_body(reverse, member_ref, carried_ref, total_ref, *refs):
    held_refs, back_refs, ahead = refs[:GROUP], refs[GROUP:-1], refs[-1]
    for mask, held_ref in enumerate(held_refs):
        ahead[pl.ds(member_ref[0] ^ mask, 1)] = held_ref[:DH][None]
    running = carried_ref[:DH]
    for member in reversed(range(GROUP)) if reverse else range(GROUP):
        own = ahead[member]
        ahead[member] = running
        running = running + own
    for mask, back_ref in enumerate(back_refs):
        back_ref[:DH] = ahead[pl.ds(member_ref[0] ^ mask, 1)][0]
        if back_ref.shape[0] > DH:
            back_ref[DH:] = total_ref[DH:]


def gain_body(member_ref, *refs):
    for mask, piece_ref in enumerate(refs[:-1]):
        refs[-1][pl.ds(member_ref[0] ^ mask, 1), :] = piece_ref[DH : DH + 1, :]


def whole(*shape):
    return pl.BlockSpec(shape, lambda step: (0,) * len(shape))


def part_of(chain):
    return pl.BlockSpec((BLOCK, WIDE), lambda step: (0, chain))


MEMBER = pl.BlockSpec(memory_space=pltpu.SMEM)


def call(body, in_specs, out_specs, outs, flops, name, aliases=None, scratch=()):
    return pl.pallas_call(
        body,
        grid=(1,),
        in_specs=in_specs,
        out_specs=out_specs,
        out_shape=outs,
        input_output_aliases=aliases or {},
        scratch_shapes=scratch,
        compiler_params=pltpu.CompilerParams(vmem_limit_bytes=16 * 1024 * 1024),
        cost_estimate=pl.CostEstimate(flops=flops, bytes_accessed=2 << 20, transcendentals=0),
        name=name,
    )


def swap(array, axis, mask):
    if mask == 0:
        return array
    return lax.ppermute(array, axis, [(s, s ^ mask) for s in range(lax.axis_size(axis))])


def carried_in(held, axis, member, reverse):
    count, place = lax.axis_size(axis), lax.axis_index(axis)
    held = [swap(piece, axis, mask) for mask, piece in enumerate(held)]
    total = sum(held[1:], held[0])
    carried = jnp.zeros_like(total)
    mask = GROUP
    while mask < count:
        arrived = swap(total, axis, mask)
        later = ((place & mask) != 0) != reverse
        carried = carried + jnp.where(later, arrived, 0.0)
        total = total + arrived
        mask *= 2
    specs = [whole(*total.shape)] * GROUP
    back = call(
        functools.partial(prefix_body, reverse),
        [MEMBER] + specs[:2] + specs,
        specs,
        [jax.ShapeDtypeStruct(total.shape, jnp.float32)] * GROUP,
        1 << 24,
        "prefix",
        scratch=[pltpu.VMEM((GROUP, DH, DH), jnp.float32)],
    )(member, carried, total, *held)
    return [swap(piece, axis, mask) for mask, piece in enumerate(back)]


def local(queries, keys, values, out_gain, grad_out):
    full = queries.shape
    flat = (full[0] * full[1], full[2])
    assert flat == (BLOCK, HEADS * DH)
    query, key, value, grad = (a.reshape(flat) for a in (queries, keys, values, grad_out))
    gain = out_gain.reshape(1, HEADS * DH)
    assert lax.axis_size("seq") % GROUP == 0
    member = lax.rem(lax.axis_index("seq"), GROUP).astype(jnp.int32).reshape(1)
    square = jax.ShapeDtypeStruct((DH, DH), jnp.float32)
    taller = jax.ShapeDtypeStruct((DH + GAIN_ROWS, DH), jnp.float32)
    full_float = jax.ShapeDtypeStruct(flat, jnp.float32)
    full_low = jax.ShapeDtypeStruct(flat, jnp.bfloat16)
    states_low = jax.ShapeDtypeStruct((HEADS, DH, DH), jnp.bfloat16)
    squares = [whole(*square.shape)] * GROUP
    tallers = [whole(*taller.shape)] * GROUP
    wide = whole(*flat)
    spot = pl.BlockSpec(memory_space=pl.ANY)
    unit = 2 * BLOCK * DH * DH * HEADS

    deltas = call(delta_body, [MEMBER, wide, wide], squares, [square] * GROUP, 6 * unit, "delta")(member, key, value)
    states = carried_in(deltas, "seq", member, False)
    inner = call(inner_body, [wide] * 3, wide, full_float, 16 * unit, "inner")(query, key, value)
    attn, low, *deltas = call(
        norm_body,
        [MEMBER, wide, wide, wide, whole(1, HEADS * DH)] + squares,
        [wide, whole(*states_low.shape)] + tallers,
        [full_low, states_low] + [taller] * GROUP,
        16 * unit,
        "norm",
    )(member, query, grad, inner, gain, *states)
    later = carried_in(deltas, "seq", member, True)
    parts = []
    for chunk in range(CHUNKS):
        cols = part_of(chunk)
        parts = call(
            partial_body,
            [cols] * 4 + [pl.BlockSpec((CHUNK_HEADS, DH, DH), lambda step, c=chunk: (c, 0, 0))] + [spot] * len(parts),
            [cols] * 3,
            [full_low, full_float, full_float],
            24 * unit,
            "partial",
            {5: 0, 6: 1, 7: 2} if parts else None,
        )(query, key, value, attn, low, *parts)
    grad_query, *parts = parts

    gain_terms = call(
        gain_body, [MEMBER] + tallers, whole(HEADS, DH), jax.ShapeDtypeStruct((HEADS, DH), jnp.float32), unit, "gain"
    )(member, *later)
    mask = 1
    while mask < lax.axis_size("dp"):
        gain_terms = gain_terms + swap(gain_terms, "dp", mask)
        mask *= 2
    grad_key, grad_value = call(
        final_body, [MEMBER] + [wide] * 4 + tallers, [wide] * 2, [full_low] * 2, 16 * unit, "final"
    )(member, key, value, *parts, *later)
    positions = lax.axis_size("seq") * lax.axis_size("dp") * BLOCK
    grad_gain = gain_terms.reshape(HEADS * DH) / math.sqrt(positions)
    return (grad_query.reshape(full), grad_key.reshape(full), grad_value.reshape(full), grad_gain)


def solution(mesh):
    sharded = P("dp", "seq", None)
    return jax.shard_map(
        local,
        mesh=mesh,
        in_specs=(sharded, sharded, sharded, P(), sharded),
        out_specs=(sharded, sharded, sharded, P()),
        check_vma=False,
    )
```

```python
import functools
import math

import jax
import jax.numpy as jnp
from jax import lax
from jax.experimental import pallas as pl
from jax.experimental.pallas import tpu as pltpu
from jax.sharding import PartitionSpec as P

HEADS = 8
DH = 128
BLOCK = 256
GROUP = 8
CHAINS = 2
CHAIN_HEADS = HEADS // CHAINS
WIDE = CHAIN_HEADS * DH
OWNED = WIDE // GROUP
SHARES = DH // OWNED
GAIN_ROWS = 8
EPSILON = 1e-06

NT = (((1,), (1,)), ((), ()))
TN = (((0,), (0,)), ((), ()))
NN = (((1,), (0,)), ((), ()))


def dot(left, right, dims):
    return lax.dot_general(left, right, dims, preferred_element_type=jnp.float32)


def columns(head):
    return pl.ds(head * DH, DH)


def causal():
    shape = (BLOCK, BLOCK)
    return lax.broadcasted_iota(jnp.int32, shape, 0) >= lax.broadcasted_iota(jnp.int32, shape, 1)


def put(delta_ref, head, delta):
    for share in range(SHARES):
        delta_ref[head * SHARES + share, :OWNED] = delta[share * OWNED : (share + 1) * OWNED]


def delta_body(key_ref, value_ref, delta_ref):
    for head in range(CHAIN_HEADS):
        at = columns(head)
        put(delta_ref, head, dot(key_ref[:, at], value_ref[:, at], TN))


def state_of(state_ref, head):
    shares = [state_ref[head * SHARES + share, :OWNED] for share in range(SHARES)]
    return jnp.concatenate(shares, axis=0).astype(jnp.bfloat16)


def inner_body(query_ref, key_ref, value_ref, inner_ref):
    keep = causal()
    for head in range(CHAIN_HEADS):
        at = columns(head)
        raw = dot(query_ref[:, at], key_ref[:, at], NT)
        scores = jnp.where(keep, raw, 0.0).astype(jnp.bfloat16)
        inner_ref[:, at] = dot(scores, value_ref[:, at], NN)


def norm_body(query_ref, grad_ref, inner_ref, gain_ref, state_ref, attn_ref, delta_ref):
    for head in range(CHAIN_HEADS):
        at = columns(head)
        query = query_ref[:, at]
        attn = inner_ref[:, at] + dot(query, state_of(state_ref, head), NN)
        root = jnp.sqrt(jnp.mean(attn * attn, axis=-1, keepdims=True) + EPSILON)
        normed = attn / root
        cotangent = grad_ref[:, at].astype(jnp.float32)
        scaled = gain_ref[:, at] * cotangent
        shared = jnp.mean(normed * scaled, axis=-1, keepdims=True)
        grad_attn = ((scaled - normed * shared) / root).astype(jnp.bfloat16)
        attn_ref[:, at] = grad_attn
        terms = jnp.sum(normed * cotangent, axis=0, keepdims=True)
        put(delta_ref, head, dot(query, grad_attn, TN))
        for share in range(SHARES):
            delta_ref[head * SHARES + share, OWNED:] = jnp.broadcast_to(terms, (GAIN_ROWS, DH))


def partial_body(query_ref, key_ref, value_ref, attn_ref, state_ref, *refs):
    grad_query_ref, key_part_ref, value_part_ref = refs[-3:]
    keep = causal()
    for head in range(CHAIN_HEADS):
        at = columns(head)
        query, key, value, grad_attn = query_ref[:, at], key_ref[:, at], value_ref[:, at], attn_ref[:, at]
        scores = jnp.where(keep, dot(query, key, NT), 0.0).astype(jnp.bfloat16)
        grad_scores = jnp.where(keep, dot(grad_attn, value, NT), 0.0).astype(jnp.bfloat16)
        carried = dot(grad_attn, state_of(state_ref, head), NT)
        grad_query_ref[:, at] = (dot(grad_scores, key, NN) + carried).astype(jnp.bfloat16)
        key_part_ref[:, at] = dot(grad_scores, query, TN)
        value_part_ref[:, at] = dot(scores, grad_attn, TN)


def final_body(key_ref, value_ref, key_part_ref, value_part_ref, state_ref, *refs):
    grad_key_ref, grad_value_ref = refs[-2:]
    for head in range(CHAIN_HEADS):
        at = columns(head)
        state = state_of(state_ref, head)
        grad_key_ref[:, at] = (key_part_ref[:, at] + dot(value_ref[:, at], state, NT)).astype(jnp.bfloat16)
        grad_value_ref[:, at] = (value_part_ref[:, at] + dot(key_ref[:, at], state, NN)).astype(jnp.bfloat16)


def gain_body(*refs):
    for chain, state_ref in enumerate(refs[:-1]):
        for head in range(CHAIN_HEADS):
            row = chain * CHAIN_HEADS + head
            refs[-1][row : row + 1, :] = state_ref[head * SHARES, OWNED : OWNED + 1, :]


def prefix_body(reverse, carried_ref, total_ref, held_ref, back_ref):
    running = carried_ref[:OWNED]
    for member in reversed(range(GROUP)) if reverse else range(GROUP):
        back_ref[member, :OWNED] = running
        running = running + held_ref[member, :OWNED]
        if back_ref.shape[1] > OWNED:
            back_ref[member, OWNED:] = total_ref[OWNED:]


def whole(*shape):
    return pl.BlockSpec(shape, lambda step: (0,) * len(shape))


def part_of(chain):
    return pl.BlockSpec((BLOCK, WIDE), lambda step: (0, chain))


def call(body, in_specs, out_specs, outs, flops, name, aliases=None):
    return pl.pallas_call(
        body,
        grid=(1,),
        in_specs=in_specs,
        out_specs=out_specs,
        out_shape=outs,
        input_output_aliases=aliases or {},
        compiler_params=pltpu.CompilerParams(vmem_limit_bytes=16 * 1024 * 1024),
        cost_estimate=pl.CostEstimate(flops=flops, bytes_accessed=2 << 20, transcendentals=0),
        name=name,
    )


def swap(array, axis, mask):
    if mask == 0:
        return array
    return lax.ppermute(array, axis, [(s, s ^ mask) for s in range(lax.axis_size(axis))])


def carried_in(parts, axis, reverse):
    count, place = lax.axis_size(axis), lax.axis_index(axis)
    teams = [list(range(first, first + GROUP)) for first in range(0, count, GROUP)]
    held = lax.all_to_all(parts, axis, 0, 0, axis_index_groups=teams)
    total = jnp.sum(held, axis=0)
    carried = jnp.zeros_like(total)
    mask = GROUP
    while mask < count:
        arrived = swap(total, axis, mask)
        later = ((place & mask) != 0) != reverse
        carried = carried + jnp.where(later, arrived, 0.0)
        total = total + arrived
        mask *= 2
    single, stacked = whole(*total.shape), whole(*held.shape)
    back = call(
        functools.partial(prefix_body, reverse),
        [single, single, stacked],
        stacked,
        jax.ShapeDtypeStruct(held.shape, jnp.float32),
        1 << 24,
        "prefix",
    )(carried, total, held)
    return lax.all_to_all(back, axis, 0, 0, axis_index_groups=teams)


def local(queries, keys, values, out_gain, grad_out):
    full = queries.shape
    flat = (full[0] * full[1], full[2])
    assert flat == (BLOCK, HEADS * DH)
    query, key, value, grad = (a.reshape(flat) for a in (queries, keys, values, grad_out))
    gain = out_gain.reshape(1, HEADS * DH)
    assert lax.axis_size("seq") % GROUP == 0
    plain = jax.ShapeDtypeStruct((GROUP, OWNED, DH), jnp.float32)
    taller = jax.ShapeDtypeStruct((GROUP, OWNED + GAIN_ROWS, DH), jnp.float32)
    wide_float = jax.ShapeDtypeStruct((BLOCK, WIDE), jnp.float32)
    wide_low = jax.ShapeDtypeStruct((BLOCK, WIDE), jnp.bfloat16)
    full_low = jax.ShapeDtypeStruct(flat, jnp.bfloat16)
    short, tall, wide = whole(*plain.shape), whole(*taller.shape), whole(BLOCK, WIDE)
    spot = pl.BlockSpec(memory_space=pl.ANY)
    unit = 2 * BLOCK * DH * DH * CHAIN_HEADS

    states, inner = [], []
    for chain in range(CHAINS):
        cols = part_of(chain)
        delta = call(delta_body, [cols, cols], short, plain, 6 * unit, "delta")(key, value)
        states.append(carried_in(delta, "seq", False))
        inner.append(call(inner_body, [cols] * 3, wide, wide_float, 16 * unit, "inner")(query, key, value))

    later, parts, grad_query = [], [], []
    for chain in range(CHAINS):
        cols = part_of(chain)
        attn, delta = call(
            norm_body,
            [cols, cols, wide, pl.BlockSpec((1, WIDE), lambda step, c=chain: (0, c)), short],
            [wide, tall],
            [wide_low, taller],
            16 * unit,
            "norm",
        )(query, grad, inner[chain], gain, states[chain])
        later.append(carried_in(delta, "seq", True))
        *grad_query, key_part, value_part = call(
            partial_body,
            [cols, cols, cols, wide, short] + [spot] * len(grad_query),
            [cols, wide, wide],
            [full_low, wide_float, wide_float],
            48 * unit,
            "partial",
            {5: 0} if grad_query else None,
        )(query, key, value, attn, states[chain], *grad_query)
        parts.append((key_part, value_part))

    gain_terms = call(
        gain_body, [tall] * CHAINS, whole(HEADS, DH), jax.ShapeDtypeStruct((HEADS, DH), jnp.float32), unit, "gain"
    )(*later)
    mask = 1
    while mask < lax.axis_size("dp"):
        gain_terms = gain_terms + swap(gain_terms, "dp", mask)
        mask *= 2
    grads = []
    for chain in range(CHAINS):
        cols = part_of(chain)
        grads = call(
            final_body,
            [cols, cols, wide, wide, tall] + [spot] * len(grads),
            [cols] * 2,
            [full_low] * 2,
            16 * unit,
            "final",
            {5: 0, 6: 1} if grads else None,
        )(key, value, *parts[chain], later[chain], *grads)
    grad_key, grad_value = grads
    positions = lax.axis_size("seq") * lax.axis_size("dp") * BLOCK
    grad_gain = gain_terms.reshape(HEADS * DH) / math.sqrt(positions)
    return (grad_query[0].reshape(full), grad_key.reshape(full), grad_value.reshape(full), grad_gain)


def solution(mesh):
    sharded = P("dp", "seq", None)
    return jax.shard_map(
        local,
        mesh=mesh,
        in_specs=(sharded, sharded, sharded, P(), sharded),
        out_specs=(sharded, sharded, sharded, P()),
        check_vma=False,
    )
```

```python
import functools
import math

import jax
import jax.numpy as jnp
from jax import lax
from jax.experimental import pallas as pl
from jax.experimental.pallas import tpu as pltpu
from jax.sharding import PartitionSpec as P

HEADS = 8
DH = 128
BLOCK = 256
GROUP = 8
GAIN_ROWS = 8
STEPS = 4
STEP_HEADS = HEADS // STEPS
EPSILON = 1e-06

NT = (((1,), (1,)), ((), ()))
TN = (((0,), (0,)), ((), ()))
NN = (((1,), (0,)), ((), ()))


def dot(left, right, dims):
    return lax.dot_general(left, right, dims, preferred_element_type=jnp.float32)


def columns(head):
    return pl.ds(head * DH, DH)


def causal():
    shape = (BLOCK, BLOCK)
    return lax.broadcasted_iota(jnp.int32, shape, 0) >= lax.broadcasted_iota(jnp.int32, shape, 1)


def delta_body(key_ref, value_ref, delta_ref, key_here, value_here, sems):
    copies = []
    for head in range(HEADS):
        at = columns(head)
        copies.append(
            [
                pltpu.make_async_copy(source.at[:, at], here.at[:, at], sems.at[side, head])
                for side, (source, here) in enumerate(((key_ref, key_here), (value_ref, value_here)))
            ]
        )
        for copy in copies[-1]:
            copy.start()
    for head in range(HEADS):
        at = columns(head)
        for copy in copies[head]:
            copy.wait()
        delta_ref[head] = dot(key_here[:, at], value_here[:, at], TN)


def inner_body(query_ref, key_ref, value_ref, inner_ref):
    keep = causal()
    for head in range(HEADS):
        at = columns(head)
        raw = dot(query_ref[:, at], key_ref[:, at], NT)
        scores = jnp.where(keep, raw, 0.0).astype(jnp.bfloat16)
        inner_ref[:, at] = dot(scores, value_ref[:, at], NN)


def norm_body(query_ref, grad_ref, inner_ref, gain_ref, state_ref, attn_ref, delta_ref):
    for head in range(HEADS):
        at = columns(head)
        query = query_ref[:, at]
        attn = inner_ref[:, at] + dot(query, state_ref[head].astype(jnp.bfloat16), NN)
        per_root = lax.rsqrt(jnp.mean(attn * attn, axis=-1, keepdims=True) + EPSILON)
        normed = attn * per_root
        cotangent = grad_ref[:, at].astype(jnp.float32)
        product = normed * cotangent
        gain = gain_ref[:, at]
        shared = jnp.mean(product * gain, axis=-1, keepdims=True)
        grad_attn = ((gain * cotangent - normed * shared) * per_root).astype(jnp.bfloat16)
        attn_ref[:, at] = grad_attn
        terms = jnp.sum(product, axis=0, keepdims=True)
        delta_ref[head, :DH] = dot(query, grad_attn, TN)
        delta_ref[head, DH:] = jnp.broadcast_to(terms, (GAIN_ROWS, DH))


def partial_body(query_ref, key_ref, value_ref, attn_ref, state_ref, grad_query_ref, key_part_ref, value_part_ref):
    keep = causal()
    for head in range(HEADS):
        at = columns(head)
        query, key, value, grad_attn = query_ref[:, at], key_ref[:, at], value_ref[:, at], attn_ref[:, at]
        scores = jnp.where(keep, dot(query, key, NT), 0.0).astype(jnp.bfloat16)
        grad_scores = jnp.where(keep, dot(grad_attn, value, NT), 0.0).astype(jnp.bfloat16)
        carried = dot(grad_attn, state_ref[head].astype(jnp.bfloat16), NT)
        grad_query_ref[:, at] = (dot(grad_scores, key, NN) + carried).astype(jnp.bfloat16)
        key_part_ref[:, at] = dot(grad_scores, query, TN)
        value_part_ref[:, at] = dot(scores, grad_attn, TN)


def final_body(key_ref, value_ref, key_part_ref, value_part_ref, state_ref, grad_key_ref, grad_value_ref):
    step = pl.program_id(0)
    for head in range(STEP_HEADS):
        whole_head = step * STEP_HEADS + head
        wide = pl.ds(pl.multiple_of(whole_head * DH, DH), DH)
        at = columns(head)
        state = state_ref[whole_head, :DH].astype(jnp.bfloat16)
        grad_key_ref[:, at] = (key_part_ref[:, wide] + dot(value_ref[:, wide], state, NT)).astype(jnp.bfloat16)
        grad_value_ref[:, at] = (value_part_ref[:, wide] + dot(key_ref[:, wide], state, NN)).astype(jnp.bfloat16)


def gain_body(state_ref, gain_ref):
    for head in range(HEADS):
        gain_ref[head : head + 1, :] = state_ref[head, DH : DH + 1]


def prefix_body(reverse, carried_ref, total_ref, held_ref, back_ref):
    running = carried_ref[:DH]
    for member in reversed(range(GROUP)) if reverse else range(GROUP):
        back_ref[member, :DH] = running
        running = running + held_ref[member, :DH]
        if back_ref.shape[1] > DH:
            back_ref[member, DH:] = total_ref[DH:]


def whole(*shape):
    return pl.BlockSpec(shape, lambda step: (0,) * len(shape))


def call(body, in_specs, out_specs, outs, flops, name, steps=1, scratch=()):
    return pl.pallas_call(
        body,
        grid=(steps,),
        in_specs=in_specs,
        out_specs=out_specs,
        out_shape=outs,
        scratch_shapes=scratch,
        compiler_params=pltpu.CompilerParams(vmem_limit_bytes=16 * 1024 * 1024),
        cost_estimate=pl.CostEstimate(flops=flops, bytes_accessed=2 << 20, transcendentals=0),
        name=name,
    )


def carried_in(parts, reverse):
    count, place = lax.axis_size("seq"), lax.axis_index("seq")
    teams = [list(range(first, first + GROUP)) for first in range(0, count, GROUP)]
    held = lax.all_to_all(parts, "seq", 0, 0, axis_index_groups=teams)
    total = jnp.sum(held, axis=0)
    carried = jnp.zeros_like(total)
    mask = GROUP
    while mask < count:
        arrived = lax.ppermute(total, "seq", [(s, s ^ mask) for s in range(count)])
        later = ((place & mask) != 0) != reverse
        carried = carried + jnp.where(later, arrived, 0.0)
        total = total + arrived
        mask *= 2
    single, stacked = whole(*total.shape), whole(*held.shape)
    back = call(
        functools.partial(prefix_body, reverse),
        [single, single, stacked],
        stacked,
        jax.ShapeDtypeStruct(held.shape, jnp.float32),
        1 << 24,
        "prefix",
    )(carried, total, held)
    return lax.all_to_all(back, "seq", 0, 0, axis_index_groups=teams)


def local(queries, keys, values, out_gain, grad_out):
    full = queries.shape
    flat = (full[0] * full[1], full[2])
    assert flat == (BLOCK, HEADS * DH) and lax.axis_size("seq") % GROUP == 0 and GROUP == HEADS
    query, key, value, grad = (a.reshape(flat) for a in (queries, keys, values, grad_out))
    gain = out_gain.reshape(1, HEADS * DH)
    plain = jax.ShapeDtypeStruct((GROUP, DH, DH), jnp.float32)
    taller = jax.ShapeDtypeStruct((GROUP, DH + GAIN_ROWS, DH), jnp.float32)
    full_float = jax.ShapeDtypeStruct(flat, jnp.float32)
    full_low = jax.ShapeDtypeStruct(flat, jnp.bfloat16)
    short, tall, wide = whole(*plain.shape), whole(*taller.shape), whole(*flat)
    unit = 2 * BLOCK * DH * DH * HEADS

    delta = call(
        delta_body,
        [pl.BlockSpec(memory_space=pltpu.HBM)] * 2,
        short,
        plain,
        6 * unit,
        "delta",
        scratch=[pltpu.VMEM(flat, jnp.bfloat16)] * 2 + [pltpu.SemaphoreType.DMA((2, HEADS))],
    )(*[pltpu.with_memory_space_constraint(a, pltpu.HBM) for a in (key, value)])
    states = carried_in(delta, False)
    inner = call(inner_body, [wide] * 3, wide, full_float, 16 * unit, "inner")(query, key, value)
    attn, delta = call(
        norm_body, [wide, wide, wide, whole(1, HEADS * DH), short], [wide, tall], [full_low, taller], 16 * unit, "norm"
    )(query, grad, inner, gain, states)
    later = carried_in(delta, True)
    grad_query, key_part, value_part = call(
        partial_body, [wide] * 4 + [short], [wide] * 3, [full_low, full_float, full_float], 48 * unit, "partial"
    )(query, key, value, attn, states)
    gain_terms = call(
        gain_body, [tall], whole(HEADS, DH), jax.ShapeDtypeStruct((HEADS, DH), jnp.float32), unit, "gain"
    )(later)
    docs, mask = lax.axis_size("dp"), 1
    while mask < docs:
        gain_terms = gain_terms + lax.ppermute(gain_terms, "dp", [(d, d ^ mask) for d in range(docs)])
        mask *= 2
    chunk = pl.BlockSpec((BLOCK, STEP_HEADS * DH), lambda step: (0, step))
    grad_key, grad_value = call(
        final_body, [wide] * 4 + [tall], [chunk] * 2, [full_low] * 2, 16 * unit, "final", steps=STEPS
    )(key, value, key_part, value_part, later)
    grad_gain = gain_terms / math.sqrt(lax.axis_size("seq") * docs * BLOCK)
    return (
        grad_query.reshape(full),
        grad_key.reshape(full),
        grad_value.reshape(full),
        grad_gain.reshape(HEADS * DH),
    )


def solution(mesh):
    sharded = P("dp", "seq", None)
    return jax.shard_map(
        local,
        mesh=mesh,
        in_specs=(sharded, sharded, sharded, P(), sharded),
        out_specs=(sharded, sharded, sharded, P()),
        check_vma=False,
    )
```

```python
import functools
import math

import jax
import jax.numpy as jnp
from jax import lax
from jax.experimental import pallas as pl
from jax.experimental.pallas import tpu as pltpu
from jax.sharding import PartitionSpec as P

HEADS = 8
DH = 128
BLOCK = 256
GROUP = 8
GAIN_ROWS = 8
PARTS = 2
PART_ROWS = BLOCK // PARTS
EPSILON = 1e-06

NT = (((1,), (1,)), ((), ()))
TN = (((0,), (0,)), ((), ()))
NN = (((1,), (0,)), ((), ()))


def dot(left, right, dims):
    return lax.dot_general(left, right, dims, preferred_element_type=jnp.float32)


def columns(head):
    return pl.ds(head * DH, DH)


def causal():
    shape = (BLOCK, BLOCK)
    return lax.broadcasted_iota(jnp.int32, shape, 0) >= lax.broadcasted_iota(jnp.int32, shape, 1)


def delta_body(key_ref, value_ref, delta_ref, key_here, value_here, sems):
    copies = []
    for part in range(PARTS):
        rows = pl.ds(part * PART_ROWS, PART_ROWS)
        for side, (source, here) in enumerate(((key_ref, key_here), (value_ref, value_here))):
            copies.append(pltpu.make_async_copy(source.at[rows], here.at[rows], sems.at[part, side]))
            copies[-1].start()
    for part in range(PARTS):
        rows = pl.ds(part * PART_ROWS, PART_ROWS)
        for copy in copies[2 * part : 2 * part + 2]:
            copy.wait()
        for head in range(HEADS):
            at = columns(head)
            delta = dot(key_here[rows, at], value_here[rows, at], TN)
            delta_ref[head] = delta if part == 0 else delta_ref[head] + delta


def inner_body(query_ref, key_ref, value_ref, inner_ref):
    keep = causal()
    for head in range(HEADS):
        at = columns(head)
        raw = dot(query_ref[:, at], key_ref[:, at], NT)
        scores = jnp.where(keep, raw, 0.0).astype(jnp.bfloat16)
        inner_ref[:, at] = dot(scores, value_ref[:, at], NN)


def norm_body(query_ref, grad_ref, inner_ref, gain_ref, state_ref, attn_ref, delta_ref):
    for head in range(HEADS):
        at = columns(head)
        query = query_ref[:, at]
        attn = inner_ref[:, at] + dot(query, state_ref[head].astype(jnp.bfloat16), NN)
        per_root = lax.rsqrt(jnp.mean(attn * attn, axis=-1, keepdims=True) + EPSILON)
        normed = attn * per_root
        cotangent = grad_ref[:, at].astype(jnp.float32)
        product = normed * cotangent
        gain = gain_ref[:, at]
        shared = jnp.mean(product * gain, axis=-1, keepdims=True)
        grad_attn = ((gain * cotangent - normed * shared) * per_root).astype(jnp.bfloat16)
        attn_ref[:, at] = grad_attn
        terms = jnp.sum(product, axis=0, keepdims=True)
        delta_ref[head, :DH] = dot(query, grad_attn, TN)
        delta_ref[head, DH:] = jnp.broadcast_to(terms, (GAIN_ROWS, DH))


def partial_body(query_ref, key_ref, value_ref, attn_ref, state_ref, grad_query_ref, key_part_ref, value_part_ref):
    keep = causal()
    for head in range(HEADS):
        at = columns(head)
        query, key, value, grad_attn = query_ref[:, at], key_ref[:, at], value_ref[:, at], attn_ref[:, at]
        scores = jnp.where(keep, dot(query, key, NT), 0.0).astype(jnp.bfloat16)
        grad_scores = jnp.where(keep, dot(grad_attn, value, NT), 0.0).astype(jnp.bfloat16)
        carried = dot(grad_attn, state_ref[head].astype(jnp.bfloat16), NT)
        grad_query_ref[:, at] = (dot(grad_scores, key, NN) + carried).astype(jnp.bfloat16)
        key_part_ref[:, at] = dot(grad_scores, query, TN)
        value_part_ref[:, at] = dot(scores, grad_attn, TN)


def final_body(key_ref, value_ref, key_part_ref, value_part_ref, state_ref, grad_key_ref, grad_value_ref):
    rows = pl.ds(pl.multiple_of(pl.program_id(0) * PART_ROWS, PART_ROWS), PART_ROWS)
    for head in range(HEADS):
        at = columns(head)
        state = state_ref[head, :DH].astype(jnp.bfloat16)
        grad_key_ref[:, at] = (key_part_ref[rows, at] + dot(value_ref[rows, at], state, NT)).astype(jnp.bfloat16)
        grad_value_ref[:, at] = (value_part_ref[rows, at] + dot(key_ref[rows, at], state, NN)).astype(jnp.bfloat16)


def gain_body(state_ref, gain_ref):
    for head in range(HEADS):
        gain_ref[head : head + 1, :] = state_ref[head, DH : DH + 1]


def prefix_body(reverse, carried_ref, total_ref, held_ref, back_ref):
    running = carried_ref[:DH]
    for member in reversed(range(GROUP)) if reverse else range(GROUP):
        back_ref[member, :DH] = running
        running = running + held_ref[member, :DH]
        if back_ref.shape[1] > DH:
            back_ref[member, DH:] = total_ref[DH:]


def whole(*shape):
    return pl.BlockSpec(shape, lambda step: (0,) * len(shape))


def call(body, in_specs, out_specs, outs, flops, name, steps=1, scratch=()):
    return pl.pallas_call(
        body,
        grid=(steps,),
        in_specs=in_specs,
        out_specs=out_specs,
        out_shape=outs,
        scratch_shapes=scratch,
        compiler_params=pltpu.CompilerParams(vmem_limit_bytes=16 * 1024 * 1024),
        cost_estimate=pl.CostEstimate(flops=flops, bytes_accessed=2 << 20, transcendentals=0),
        name=name,
    )


def carried_in(parts, reverse, beside, operands):
    count, place = lax.axis_size("seq"), lax.axis_index("seq")
    teams = [list(range(first, first + GROUP)) for first in range(0, count, GROUP)]
    held = lax.all_to_all(parts, "seq", 0, 0, axis_index_groups=teams)
    held, *operands = lax.optimization_barrier((held, *operands))
    aside = beside(*operands)
    total = jnp.sum(held, axis=0)
    carried = jnp.zeros_like(total)
    mask = GROUP
    while mask < count:
        arrived = lax.ppermute(total, "seq", [(s, s ^ mask) for s in range(count)])
        later = ((place & mask) != 0) != reverse
        carried = carried + jnp.where(later, arrived, 0.0)
        total = total + arrived
        mask *= 2
    single, stacked = whole(*total.shape), whole(*held.shape)
    back = call(
        functools.partial(prefix_body, reverse),
        [single, single, stacked],
        stacked,
        jax.ShapeDtypeStruct(held.shape, jnp.float32),
        1 << 24,
        "prefix",
    )(carried, total, held)
    back, aside = lax.optimization_barrier((back, aside))
    return lax.all_to_all(back, "seq", 0, 0, axis_index_groups=teams), aside


def local(queries, keys, values, out_gain, grad_out):
    full = queries.shape
    flat = (full[0] * full[1], full[2])
    assert flat == (BLOCK, HEADS * DH) and lax.axis_size("seq") % GROUP == 0 and GROUP == HEADS
    query, key, value, grad = (a.reshape(flat) for a in (queries, keys, values, grad_out))
    gain = out_gain.reshape(1, HEADS * DH)
    plain = jax.ShapeDtypeStruct((GROUP, DH, DH), jnp.float32)
    taller = jax.ShapeDtypeStruct((GROUP, DH + GAIN_ROWS, DH), jnp.float32)
    full_float = jax.ShapeDtypeStruct(flat, jnp.float32)
    full_low = jax.ShapeDtypeStruct(flat, jnp.bfloat16)
    short, tall, wide = whole(*plain.shape), whole(*taller.shape), whole(*flat)
    unit = 2 * BLOCK * DH * DH * HEADS

    delta = call(
        delta_body,
        [pl.BlockSpec(memory_space=pltpu.HBM)] * 2,
        short,
        plain,
        6 * unit,
        "delta",
        scratch=[pltpu.VMEM(flat, jnp.bfloat16)] * 2 + [pltpu.SemaphoreType.DMA((PARTS, 2))],
    )(*[pltpu.with_memory_space_constraint(a, pltpu.HBM) for a in (key, value)])
    inner_call = call(inner_body, [wide] * 3, wide, full_float, 16 * unit, "inner")
    states, inner = carried_in(delta, False, inner_call, (query, key, value))
    attn, delta = call(
        norm_body, [wide, wide, wide, whole(1, HEADS * DH), short], [wide, tall], [full_low, taller], 16 * unit, "norm"
    )(query, grad, inner, gain, states)
    partial_call = call(
        partial_body, [wide] * 4 + [short], [wide] * 3, [full_low, full_float, full_float], 48 * unit, "partial"
    )
    later, parts = carried_in(delta, True, partial_call, (query, key, value, attn, states))
    grad_query, key_part, value_part = parts
    gain_terms = call(
        gain_body, [tall], whole(HEADS, DH), jax.ShapeDtypeStruct((HEADS, DH), jnp.float32), unit, "gain"
    )(later)
    docs, mask = lax.axis_size("dp"), 1
    while mask < docs:
        gain_terms = gain_terms + lax.ppermute(gain_terms, "dp", [(d, d ^ mask) for d in range(docs)])
        mask *= 2
    chunk = pl.BlockSpec((PART_ROWS, HEADS * DH), lambda step: (step, 0))
    grad_key, grad_value = call(
        final_body, [wide] * 4 + [tall], [chunk] * 2, [full_low] * 2, 16 * unit, "final", steps=PARTS
    )(key, value, key_part, value_part, later)
    grad_gain = gain_terms / math.sqrt(lax.axis_size("seq") * docs * BLOCK)
    return (
        grad_query.reshape(full),
        grad_key.reshape(full),
        grad_value.reshape(full),
        grad_gain.reshape(HEADS * DH),
    )


def solution(mesh):
    sharded = P("dp", "seq", None)
    return jax.shard_map(
        local,
        mesh=mesh,
        in_specs=(sharded, sharded, sharded, P(), sharded),
        out_specs=(sharded, sharded, sharded, P()),
        check_vma=False,
    )
```

```python
import functools
import math

import jax
import jax.numpy as jnp
from jax import lax
from jax.experimental import pallas as pl
from jax.experimental.pallas import tpu as pltpu
from jax.sharding import PartitionSpec as P

HEADS = 8
DH = 128
BLOCK = 256
GROUP = 8
GAIN_ROWS = 8
PARTS = 2
PART_ROWS = BLOCK // PARTS
EPSILON = 1e-06

NT = (((1,), (1,)), ((), ()))
TN = (((0,), (0,)), ((), ()))
NN = (((1,), (0,)), ((), ()))


def dot(left, right, dims):
    return lax.dot_general(left, right, dims, preferred_element_type=jnp.float32)


def columns(head):
    return pl.ds(head * DH, DH)


def causal(turned=False):
    shape, first = (BLOCK, BLOCK), int(turned)
    return lax.broadcasted_iota(jnp.int32, shape, first) >= lax.broadcasted_iota(jnp.int32, shape, 1 - first)


def delta_body(flags_ref, key_ref, value_ref, delta_ref, key_here, value_here, sems):
    copies = []
    for part in range(PARTS):
        rows = pl.ds(part * PART_ROWS, PART_ROWS)
        for side, (source, here) in enumerate(((key_ref, key_here), (value_ref, value_here))):
            copies.append(pltpu.make_async_copy(source.at[rows], here.at[rows], sems.at[part, side]))
            copies[-1].start()
    for part in range(PARTS):
        rows = pl.ds(part * PART_ROWS, PART_ROWS)
        for copy in copies[2 * part : 2 * part + 2]:
            copy.wait()
        for head in range(HEADS):
            at = columns(head)
            delta = dot(key_here[rows, at], value_here[rows, at], TN)
            delta_ref[head] = delta if part == 0 else delta_ref[head] + delta


def inner_body(query_ref, key_ref, value_ref, inner_ref, turned_ref):
    keep, kept = causal(), causal(True)
    for head in range(HEADS):
        at = columns(head)
        query, key = query_ref[:, at], key_ref[:, at]
        scores = jnp.where(keep, dot(query, key, NT), 0.0).astype(jnp.bfloat16)
        inner_ref[:, at] = dot(scores, value_ref[:, at], NN)
        turned_ref[head] = jnp.where(kept, dot(key, query, NT), 0.0).astype(jnp.bfloat16)


def norm_body(query_ref, grad_ref, inner_ref, gain_ref, state_ref, attn_ref, delta_ref):
    for head in range(HEADS):
        at = columns(head)
        query = query_ref[:, at]
        attn = inner_ref[:, at] + dot(query, state_ref[head].astype(jnp.bfloat16), NN)
        per_root = lax.rsqrt(jnp.mean(attn * attn, axis=-1, keepdims=True) + EPSILON)
        normed = attn * per_root
        cotangent = grad_ref[:, at].astype(jnp.float32)
        product = normed * cotangent
        gain = gain_ref[:, at]
        shared = jnp.mean(product * gain, axis=-1, keepdims=True)
        grad_attn = ((gain * cotangent - normed * shared) * per_root).astype(jnp.bfloat16)
        attn_ref[:, at] = grad_attn
        terms = jnp.sum(product, axis=0, keepdims=True)
        delta_ref[head, :DH] = dot(query, grad_attn, TN)
        delta_ref[head, DH:] = jnp.broadcast_to(terms, (GAIN_ROWS, DH))


def partial_body(
    query_ref, key_ref, value_ref, turned_ref, attn_ref, state_ref, grad_query_ref, key_part_ref, value_part_ref
):
    keep, kept = causal(), causal(True)
    for head in range(HEADS):
        at = columns(head)
        key, value, grad_attn = key_ref[:, at], value_ref[:, at], attn_ref[:, at]
        grad_scores = jnp.where(keep, dot(grad_attn, value, NT), 0.0).astype(jnp.bfloat16)
        turned_grad = jnp.where(kept, dot(value, grad_attn, NT), 0.0).astype(jnp.bfloat16)
        carried = dot(grad_attn, state_ref[head].astype(jnp.bfloat16), NT)
        grad_query_ref[:, at] = (dot(grad_scores, key, NN) + carried).astype(jnp.bfloat16)
        key_part_ref[:, at] = dot(turned_grad, query_ref[:, at], NN)
        value_part_ref[:, at] = dot(turned_ref[head], grad_attn, NN)


def final_body(key_ref, value_ref, key_part_ref, value_part_ref, state_ref, grad_key_ref, grad_value_ref):
    rows = pl.ds(pl.multiple_of(pl.program_id(0) * PART_ROWS, PART_ROWS), PART_ROWS)
    for head in range(HEADS):
        at = columns(head)
        state = state_ref[head, :DH].astype(jnp.bfloat16)
        grad_key_ref[:, at] = (key_part_ref[rows, at] + dot(value_ref[rows, at], state, NT)).astype(jnp.bfloat16)
        grad_value_ref[:, at] = (value_part_ref[rows, at] + dot(key_ref[rows, at], state, NN)).astype(jnp.bfloat16)


def gain_body(state_ref, gain_ref):
    for head in range(HEADS):
        gain_ref[head : head + 1, :] = state_ref[head, DH : DH + 1]


def prefix_body(reverse, flags_ref, *refs):
    *arrived_refs, total_ref, held_ref, back_ref = refs
    running = jnp.zeros((DH, DH), jnp.float32)
    for step, arrived_ref in enumerate(arrived_refs):
        later = (flags_ref[step] != 0) != reverse
        running = running + jnp.where(later, arrived_ref[:DH], 0.0)
    for member in reversed(range(GROUP)) if reverse else range(GROUP):
        back_ref[member, :DH] = running
        running = running + held_ref[member, :DH]
        if back_ref.shape[1] > DH:
            back_ref[member, DH:] = total_ref[DH:]


def whole(*shape):
    return pl.BlockSpec(shape, lambda step: (0,) * len(shape))


FLAGS = pl.BlockSpec(memory_space=pltpu.SMEM)


def call(body, in_specs, out_specs, outs, flops, name, steps=1, scratch=()):
    return pl.pallas_call(
        body,
        grid=(steps,),
        in_specs=in_specs,
        out_specs=out_specs,
        out_shape=outs,
        scratch_shapes=scratch,
        compiler_params=pltpu.CompilerParams(vmem_limit_bytes=16 * 1024 * 1024),
        cost_estimate=pl.CostEstimate(flops=flops, bytes_accessed=2 << 20, transcendentals=0),
        name=name,
    )


def exchange_masks():
    masks = [GROUP]
    while masks[-1] * 2 < lax.axis_size("seq"):
        masks.append(masks[-1] * 2)
    return masks if lax.axis_size("seq") > GROUP else []


def carried_in(parts, reverse, flags, beside, operands):
    count = lax.axis_size("seq")
    teams = [list(range(first, first + GROUP)) for first in range(0, count, GROUP)]
    held = lax.all_to_all(parts, "seq", 0, 0, axis_index_groups=teams)
    held, *operands = lax.optimization_barrier((held, *operands))
    aside = beside(*operands)
    total = jnp.sum(held, axis=0)
    arrived = []
    for mask in exchange_masks():
        arrived.append(lax.ppermute(total, "seq", [(s, s ^ mask) for s in range(count)]))
        total = total + arrived[-1]
    single, stacked = whole(*total.shape), whole(*held.shape)
    back = call(
        functools.partial(prefix_body, reverse),
        [FLAGS] + [single] * (len(arrived) + 1) + [stacked],
        stacked,
        jax.ShapeDtypeStruct(held.shape, jnp.float32),
        1 << 24,
        "prefix",
    )(flags, *arrived, total, held)
    back, aside = lax.optimization_barrier((back, aside))
    return lax.all_to_all(back, "seq", 0, 0, axis_index_groups=teams), aside


def local(queries, keys, values, out_gain, grad_out):
    full = queries.shape
    flat = (full[0] * full[1], full[2])
    assert flat == (BLOCK, HEADS * DH) and lax.axis_size("seq") % GROUP == 0 and GROUP == HEADS
    query, key, value, grad = (a.reshape(flat) for a in (queries, keys, values, grad_out))
    gain = out_gain.reshape(1, HEADS * DH)
    plain = jax.ShapeDtypeStruct((GROUP, DH, DH), jnp.float32)
    taller = jax.ShapeDtypeStruct((GROUP, DH + GAIN_ROWS, DH), jnp.float32)
    full_float = jax.ShapeDtypeStruct(flat, jnp.float32)
    full_low = jax.ShapeDtypeStruct(flat, jnp.bfloat16)
    short, tall, wide = whole(*plain.shape), whole(*taller.shape), whole(*flat)
    unit = 2 * BLOCK * DH * DH * HEADS

    place = lax.axis_index("seq")
    flags = jnp.stack([place & mask for mask in exchange_masks()] or [place]).astype(jnp.int32)
    delta = call(
        delta_body,
        [FLAGS] + [pl.BlockSpec(memory_space=pltpu.HBM)] * 2,
        short,
        plain,
        6 * unit,
        "delta",
        scratch=[pltpu.VMEM(flat, jnp.bfloat16)] * 2 + [pltpu.SemaphoreType.DMA((PARTS, 2))],
    )(flags, *[pltpu.with_memory_space_constraint(a, pltpu.HBM) for a in (key, value)])
    square = jax.ShapeDtypeStruct((HEADS, BLOCK, BLOCK), jnp.bfloat16)
    inner_call = call(inner_body, [wide] * 3, [wide, whole(*square.shape)], [full_float, square], 16 * unit, "inner")
    states, (inner, turned) = carried_in(delta, False, flags, inner_call, (query, key, value))
    attn, delta = call(
        norm_body, [wide, wide, wide, whole(1, HEADS * DH), short], [wide, tall], [full_low, taller], 16 * unit, "norm"
    )(query, grad, inner, gain, states)
    partial_call = call(
        partial_body, [wide] * 3 + [whole(*square.shape), wide, short], [wide] * 3, [full_low, full_float, full_float], 48 * unit, "partial"
    )
    later, parts = carried_in(delta, True, flags, partial_call, (query, key, value, turned, attn, states))
    grad_query, key_part, value_part = parts
    gain_terms = call(
        gain_body, [tall], whole(HEADS, DH), jax.ShapeDtypeStruct((HEADS, DH), jnp.float32), unit, "gain"
    )(later)
    docs, mask = lax.axis_size("dp"), 1
    while mask < docs:
        gain_terms = gain_terms + lax.ppermute(gain_terms, "dp", [(d, d ^ mask) for d in range(docs)])
        mask *= 2
    chunk = pl.BlockSpec((PART_ROWS, HEADS * DH), lambda step: (step, 0))
    grad_key, grad_value = call(
        final_body, [wide] * 4 + [tall], [chunk] * 2, [full_low] * 2, 16 * unit, "final", steps=PARTS
    )(key, value, key_part, value_part, later)
    grad_gain = gain_terms / math.sqrt(lax.axis_size("seq") * docs * BLOCK)
    return (
        grad_query.reshape(full),
        grad_key.reshape(full),
        grad_value.reshape(full),
        grad_gain.reshape(HEADS * DH),
    )


def solution(mesh):
    sharded = P("dp", "seq", None)
    return jax.shard_map(
        local,
        mesh=mesh,
        in_specs=(sharded, sharded, sharded, P(), sharded),
        out_specs=(sharded, sharded, sharded, P()),
        check_vma=False,
    )
```

```python
import functools
import math

import jax
import jax.numpy as jnp
from jax import lax
from jax.experimental import pallas as pl
from jax.experimental.pallas import tpu as pltpu
from jax.sharding import PartitionSpec as P

HEADS = 8
DH = 128
BLOCK = 256
GROUP = 4
CHAINS = HEADS // GROUP
WIDE = GROUP * DH
GAIN_ROWS = 8
PARTS = 2
PART_ROWS = BLOCK // PARTS
EPSILON = 1e-06

NT = (((1,), (1,)), ((), ()))
TN = (((0,), (0,)), ((), ()))
NN = (((1,), (0,)), ((), ()))


def dot(left, right, dims):
    return lax.dot_general(left, right, dims, preferred_element_type=jnp.float32)


def columns(head):
    return pl.ds(head * DH, DH)


def own_columns(place_ref, mask, chain=0):
    return pl.ds(pl.multiple_of(chain * WIDE + (place_ref[0] ^ mask) * DH, DH), DH)


def causal(turned=False):
    shape, first = (BLOCK, BLOCK), int(turned)
    return lax.broadcasted_iota(jnp.int32, shape, first) >= lax.broadcasted_iota(jnp.int32, shape, 1 - first)


def delta_body(place_ref, key_ref, value_ref, *refs):
    delta_refs, (key_here, value_here, sems) = refs[:HEADS], refs[HEADS:]
    copies = []
    for part in range(PARTS):
        rows = pl.ds(part * PART_ROWS, PART_ROWS)
        for side, (source, here) in enumerate(((key_ref, key_here), (value_ref, value_here))):
            copies.append(pltpu.make_async_copy(source.at[rows], here.at[rows], sems.at[part, side]))
            copies[-1].start()
    for part in range(PARTS):
        rows = pl.ds(part * PART_ROWS, PART_ROWS)
        for copy in copies[2 * part : 2 * part + 2]:
            copy.wait()
        for at_head, delta_ref in enumerate(delta_refs):
            at = own_columns(place_ref, at_head % GROUP, at_head // GROUP)
            delta = dot(key_here[rows, at], value_here[rows, at], TN)
            delta_ref[...] = delta if part == 0 else delta_ref[...] + delta


def inner_body(query_ref, key_ref, value_ref, inner_ref):
    keep = causal()
    for head in range(HEADS):
        at = columns(head)
        scores = jnp.where(keep, dot(query_ref[:, at], key_ref[:, at], NT), 0.0).astype(jnp.bfloat16)
        inner_ref[:, at] = dot(scores, value_ref[:, at], NN)


def norm_body(chain, place_ref, query_ref, grad_ref, inner_ref, gain_ref, *refs):
    state_refs, (attn_ref, *delta_refs) = refs[:GROUP], refs[GROUP:]
    for mask, (state_ref, delta_ref) in enumerate(zip(state_refs, delta_refs)):
        at = own_columns(place_ref, mask, chain)
        query = query_ref[:, at]
        attn = inner_ref[:, at] + dot(query, state_ref[...].astype(jnp.bfloat16), NN)
        per_root = lax.rsqrt(jnp.mean(attn * attn, axis=-1, keepdims=True) + EPSILON)
        normed = attn * per_root
        cotangent = grad_ref[:, at].astype(jnp.float32)
        product = normed * cotangent
        gain = gain_ref[:, at]
        shared = jnp.mean(product * gain, axis=-1, keepdims=True)
        grad_attn = ((gain * cotangent - normed * shared) * per_root).astype(jnp.bfloat16)
        attn_ref[:, own_columns(place_ref, mask)] = grad_attn
        delta_ref[:DH] = dot(query, grad_attn, TN)
        delta_ref[DH:] = jnp.broadcast_to(jnp.sum(product, axis=0, keepdims=True), (GAIN_ROWS, DH))


def partial_body(place_ref, query_ref, key_ref, value_ref, *refs):
    attn_refs, state_refs = refs[:CHAINS], refs[CHAINS : CHAINS + HEADS]
    grad_query_ref, key_part_ref, value_part_ref = refs[-3:]
    keep, kept = causal(), causal(True)
    for at_head, state_ref in enumerate(state_refs):
        chain, mask = at_head // GROUP, at_head % GROUP
        at = own_columns(place_ref, mask, chain)
        query, key, value = query_ref[:, at], key_ref[:, at], value_ref[:, at]
        grad_attn = attn_refs[chain][:, own_columns(place_ref, mask)]
        turned = jnp.where(kept, dot(key, query, NT), 0.0).astype(jnp.bfloat16)
        grad_scores = jnp.where(keep, dot(grad_attn, value, NT), 0.0).astype(jnp.bfloat16)
        turned_grad = jnp.where(kept, dot(value, grad_attn, NT), 0.0).astype(jnp.bfloat16)
        carried = dot(grad_attn, state_ref[...].astype(jnp.bfloat16), NT)
        grad_query_ref[:, at] = (dot(grad_scores, key, NN) + carried).astype(jnp.bfloat16)
        key_part_ref[:, at] = dot(turned_grad, query, NN)
        value_part_ref[:, at] = dot(turned, grad_attn, NN)


def final_body(place_ref, key_ref, value_ref, key_part_ref, value_part_ref, *refs):
    state_refs, (grad_key_ref, grad_value_ref) = refs[:HEADS], refs[HEADS:]
    rows = pl.ds(pl.multiple_of(pl.program_id(0) * PART_ROWS, PART_ROWS), PART_ROWS)
    for at_head, state_ref in enumerate(state_refs):
        at = own_columns(place_ref, at_head % GROUP, at_head // GROUP)
        state = state_ref[:DH].astype(jnp.bfloat16)
        grad_key_ref[:, at] = (key_part_ref[rows, at] + dot(value_ref[rows, at], state, NT)).astype(jnp.bfloat16)
        grad_value_ref[:, at] = (value_part_ref[rows, at] + dot(key_ref[rows, at], state, NN)).astype(jnp.bfloat16)


def gain_body(place_ref, *refs):
    for at_head, state_ref in enumerate(refs[:-1]):
        row = (at_head // GROUP) * GROUP + (place_ref[0] ^ (at_head % GROUP))
        refs[-1][pl.ds(row, 1), :] = state_ref[DH : DH + 1]


def prefix_body(reverse, place_ref, *refs):
    (total_ref, *arrived_refs), (*back_refs, ahead) = refs[: -2 * GROUP - 1], refs[-GROUP - 1 :]
    held_refs = refs[-2 * GROUP - 1 : -GROUP - 1]
    for mask, held_ref in enumerate(held_refs):
        ahead[pl.ds(place_ref[0] ^ mask, 1)] = held_ref[:DH][None]
    running = jnp.zeros((DH, DH), jnp.float32)
    for step, arrived_ref in enumerate(arrived_refs):
        later = (place_ref[step + 1] != 0) != reverse
        running = running + jnp.where(later, arrived_ref[:DH], 0.0)
    for member in reversed(range(GROUP)) if reverse else range(GROUP):
        own = ahead[member]
        ahead[member] = running
        running = running + own
    for mask, back_ref in enumerate(back_refs):
        back_ref[:DH] = ahead[pl.ds(place_ref[0] ^ mask, 1)][0]
        if back_ref.shape[0] > DH:
            back_ref[DH:] = total_ref[DH:]


def whole(*shape):
    return pl.BlockSpec(shape, lambda step: (0,) * len(shape))


PLACE = pl.BlockSpec(memory_space=pltpu.SMEM)


def call(body, in_specs, out_specs, outs, flops, name, steps=1, scratch=()):
    return pl.pallas_call(
        body,
        grid=(steps,),
        in_specs=[PLACE] + in_specs,
        out_specs=out_specs,
        out_shape=outs,
        scratch_shapes=scratch,
        compiler_params=pltpu.CompilerParams(vmem_limit_bytes=16 * 1024 * 1024),
        cost_estimate=pl.CostEstimate(flops=flops, bytes_accessed=2 << 20, transcendentals=0),
        name=name,
    )


def exchange_masks():
    masks = [GROUP]
    while masks[-1] * 2 < lax.axis_size("seq"):
        masks.append(masks[-1] * 2)
    return masks if lax.axis_size("seq") > GROUP else []


def swap(array, mask):
    if mask == 0:
        return array
    return lax.ppermute(array, "seq", [(s, s ^ mask) for s in range(lax.axis_size("seq"))])


def carried_in(pieces, reverse, place):
    held = [swap(piece, mask) for mask, piece in enumerate(pieces)]
    total = sum(held[1:], held[0])
    arrived = []
    for mask in exchange_masks():
        arrived.append(swap(total, mask))
        total = total + arrived[-1]
    single = whole(*total.shape)
    back = call(
        functools.partial(prefix_body, reverse),
        [single] * (1 + len(arrived) + GROUP),
        [single] * GROUP,
        [jax.ShapeDtypeStruct(total.shape, jnp.float32)] * GROUP,
        1 << 24,
        "prefix",
        scratch=[pltpu.VMEM((GROUP, DH, DH), jnp.float32)],
    )(place, total, *arrived, *held)
    return [swap(piece, mask) for mask, piece in enumerate(back)]


def local(queries, keys, values, out_gain, grad_out):
    full = queries.shape
    flat = (full[0] * full[1], full[2])
    assert flat == (BLOCK, HEADS * DH) and lax.axis_size("seq") % GROUP == 0
    query, key, value, grad = (a.reshape(flat) for a in (queries, keys, values, grad_out))
    gain = out_gain.reshape(1, HEADS * DH)
    square = jax.ShapeDtypeStruct((DH, DH), jnp.float32)
    taller = jax.ShapeDtypeStruct((DH + GAIN_ROWS, DH), jnp.float32)
    full_float = jax.ShapeDtypeStruct(flat, jnp.float32)
    full_low = jax.ShapeDtypeStruct(flat, jnp.bfloat16)
    half_low = jax.ShapeDtypeStruct((BLOCK, WIDE), jnp.bfloat16)
    short, tall, wide, half = whole(*square.shape), whole(*taller.shape), whole(*flat), whole(BLOCK, WIDE)
    unit = 2 * BLOCK * DH * DH * HEADS

    at = lax.axis_index("seq")
    place = jnp.stack([lax.rem(at, GROUP)] + [at & mask for mask in exchange_masks()]).astype(jnp.int32)
    deltas = call(
        delta_body,
        [pl.BlockSpec(memory_space=pltpu.HBM)] * 2,
        [short] * HEADS,
        [square] * HEADS,
        6 * unit,
        "delta",
        scratch=[pltpu.VMEM(flat, jnp.bfloat16)] * 2 + [pltpu.SemaphoreType.DMA((PARTS, 2))],
    )(place, *[pltpu.with_memory_space_constraint(a, pltpu.HBM) for a in (key, value)])
    chains = [slice(chain * GROUP, (chain + 1) * GROUP) for chain in range(CHAINS)]
    states = [carried_in(deltas[chain], False, place) for chain in chains]
    inner = call(
        lambda place_ref, *refs: inner_body(*refs), [wide] * 3, wide, full_float, 16 * unit, "inner"
    )(place, query, key, value)
    attns, later = [], []
    for chain in range(CHAINS):
        attn, *deltas = call(
            functools.partial(norm_body, chain),
            [wide, wide, wide, whole(1, HEADS * DH)] + [short] * GROUP,
            [half] + [tall] * GROUP,
            [half_low] + [taller] * GROUP,
            8 * unit,
            "norm",
        )(place, query, grad, inner, gain, *states[chain])
        attns.append(attn)
        later += carried_in(deltas, True, place)
    grad_query, key_part, value_part = call(
        partial_body,
        [wide] * 3 + [half] * CHAINS + [short] * HEADS,
        [wide] * 3,
        [full_low, full_float, full_float],
        48 * unit,
        "partial",
    )(place, query, key, value, *attns, *[state for chain in states for state in chain])
    gain_terms = call(
        gain_body, [tall] * HEADS, whole(HEADS, DH), jax.ShapeDtypeStruct((HEADS, DH), jnp.float32), unit, "gain"
    )(place, *later)
    docs, mask = lax.axis_size("dp"), 1
    while mask < docs:
        gain_terms = gain_terms + lax.ppermute(gain_terms, "dp", [(d, d ^ mask) for d in range(docs)])
        mask *= 2
    chunk = pl.BlockSpec((PART_ROWS, HEADS * DH), lambda step: (step, 0))
    grad_key, grad_value = call(
        final_body, [wide] * 4 + [tall] * HEADS, [chunk] * 2, [full_low] * 2, 16 * unit, "final", steps=PARTS
    )(place, key, value, key_part, value_part, *later)
    grad_gain = gain_terms / math.sqrt(lax.axis_size("seq") * docs * BLOCK)
    return (
        grad_query.reshape(full),
        grad_key.reshape(full),
        grad_value.reshape(full),
        grad_gain.reshape(HEADS * DH),
    )


def solution(mesh):
    sharded = P("dp", "seq", None)
    return jax.shard_map(
        local,
        mesh=mesh,
        in_specs=(sharded, sharded, sharded, P(), sharded),
        out_specs=(sharded, sharded, sharded, P()),
        check_vma=False,
    )
```

```python
import functools
import math

import jax
import jax.numpy as jnp
from jax import lax
from jax.experimental import pallas as pl
from jax.experimental.pallas import tpu as pltpu
from jax.sharding import PartitionSpec as P

HEADS = 8
DH = 128
BLOCK = 256
GROUP = 4
CHAINS = HEADS // GROUP
WIDE = GROUP * DH
GAIN_ROWS = 8
PARTS = 2
PART_ROWS = BLOCK // PARTS
EPSILON = 1e-06

NT = (((1,), (1,)), ((), ()))
TN = (((0,), (0,)), ((), ()))
NN = (((1,), (0,)), ((), ()))


def dot(left, right, dims):
    return lax.dot_general(left, right, dims, preferred_element_type=jnp.float32)


def columns(head):
    return pl.ds(head * DH, DH)


def own_columns(place_ref, mask, chain=0):
    return pl.ds(pl.multiple_of(chain * WIDE + (place_ref[0] & (GROUP - 1) ^ mask) * DH, DH), DH)


def causal(turned=False):
    shape, first = (BLOCK, BLOCK), int(turned)
    return lax.broadcasted_iota(jnp.int32, shape, first) >= lax.broadcasted_iota(jnp.int32, shape, 1 - first)


def delta_body(place_ref, key_ref, value_ref, *refs):
    delta_refs, (key_here, value_here, sems) = refs[:HEADS], refs[HEADS:]
    copies = []
    for part in range(PARTS):
        rows = pl.ds(part * PART_ROWS, PART_ROWS)
        for side, (source, here) in enumerate(((key_ref, key_here), (value_ref, value_here))):
            copies.append(pltpu.make_async_copy(source.at[rows], here.at[rows], sems.at[part, side]))
            copies[-1].start()
    for part in range(PARTS):
        rows = pl.ds(part * PART_ROWS, PART_ROWS)
        for copy in copies[2 * part : 2 * part + 2]:
            copy.wait()
        for at_head, delta_ref in enumerate(delta_refs):
            at = own_columns(place_ref, at_head % GROUP, at_head // GROUP)
            delta = dot(key_here[rows, at], value_here[rows, at], TN)
            delta_ref[...] = delta if part == 0 else delta_ref[...] + delta


def inner_body(query_ref, key_ref, value_ref, inner_ref):
    keep = causal()
    for head in range(HEADS):
        at = columns(head)
        scores = jnp.where(keep, dot(query_ref[:, at], key_ref[:, at], NT), 0.0).astype(jnp.bfloat16)
        inner_ref[:, at] = dot(scores, value_ref[:, at], NN)


def norm_body(chain, place_ref, query_ref, grad_ref, inner_ref, gain_ref, *refs):
    state_refs, (attn_ref, *delta_refs) = refs[:GROUP], refs[GROUP:]
    for mask, (state_ref, delta_ref) in enumerate(zip(state_refs, delta_refs)):
        at = own_columns(place_ref, mask, chain)
        query = query_ref[:, at]
        attn = inner_ref[:, at] + dot(query, state_ref[...].astype(jnp.bfloat16), NN)
        per_root = lax.rsqrt(jnp.mean(attn * attn, axis=-1, keepdims=True) + EPSILON)
        normed = attn * per_root
        cotangent = grad_ref[:, at].astype(jnp.float32)
        product = normed * cotangent
        gain = gain_ref[:, at]
        shared = jnp.mean(product * gain, axis=-1, keepdims=True)
        grad_attn = ((gain * cotangent - normed * shared) * per_root).astype(jnp.bfloat16)
        attn_ref[:, own_columns(place_ref, mask)] = grad_attn
        delta_ref[:DH] = dot(query, grad_attn, TN)
        delta_ref[DH:] = jnp.broadcast_to(jnp.sum(product, axis=0, keepdims=True), (GAIN_ROWS, DH))


def partial_body(place_ref, query_ref, key_ref, value_ref, *refs):
    attn_refs, state_refs = refs[:CHAINS], refs[CHAINS : CHAINS + HEADS]
    grad_query_ref, key_part_ref, value_part_ref = refs[-3:]
    keep, kept = causal(), causal(True)
    for at_head, state_ref in enumerate(state_refs):
        chain, mask = at_head // GROUP, at_head % GROUP
        at = own_columns(place_ref, mask, chain)
        query, key, value = query_ref[:, at], key_ref[:, at], value_ref[:, at]
        grad_attn = attn_refs[chain][:, own_columns(place_ref, mask)]
        turned = jnp.where(kept, dot(key, query, NT), 0.0).astype(jnp.bfloat16)
        grad_scores = jnp.where(keep, dot(grad_attn, value, NT), 0.0).astype(jnp.bfloat16)
        turned_grad = jnp.where(kept, dot(value, grad_attn, NT), 0.0).astype(jnp.bfloat16)
        carried = dot(grad_attn, state_ref[...].astype(jnp.bfloat16), NT)
        grad_query_ref[:, at] = (dot(grad_scores, key, NN) + carried).astype(jnp.bfloat16)
        key_part_ref[:, at] = dot(turned_grad, query, NN)
        value_part_ref[:, at] = dot(turned, grad_attn, NN)


def final_body(place_ref, key_ref, value_ref, key_part_ref, value_part_ref, *refs):
    state_refs, (grad_key_ref, grad_value_ref) = refs[:HEADS], refs[HEADS:]
    rows = pl.ds(pl.multiple_of(pl.program_id(0) * PART_ROWS, PART_ROWS), PART_ROWS)
    for at_head, state_ref in enumerate(state_refs):
        at = own_columns(place_ref, at_head % GROUP, at_head // GROUP)
        state = state_ref[:DH].astype(jnp.bfloat16)
        grad_key_ref[:, at] = (key_part_ref[rows, at] + dot(value_ref[rows, at], state, NT)).astype(jnp.bfloat16)
        grad_value_ref[:, at] = (value_part_ref[rows, at] + dot(key_ref[rows, at], state, NN)).astype(jnp.bfloat16)


def gain_body(place_ref, *refs):
    for at_head, state_ref in enumerate(refs[:-1]):
        row = (at_head // GROUP) * GROUP + (place_ref[0] & (GROUP - 1) ^ (at_head % GROUP))
        refs[-1][pl.ds(row, 1), :] = state_ref[DH : DH + 1]


def prefix_body(reverse, masks, place_ref, *refs):
    (total_ref, *arrived_refs), (*back_refs, ahead) = refs[: -2 * GROUP - 1], refs[-GROUP - 1 :]
    held_refs = refs[-2 * GROUP - 1 : -GROUP - 1]
    for mask, held_ref in enumerate(held_refs):
        ahead[pl.ds(place_ref[0] & (GROUP - 1) ^ mask, 1)] = held_ref[:DH][None]
    running = jnp.zeros((DH, DH), jnp.float32)
    for mask, arrived_ref in zip(masks, arrived_refs):
        later = (place_ref[0] & mask == 0) == reverse
        running = running + jnp.where(later, arrived_ref[:DH], 0.0)
    for member in reversed(range(GROUP)) if reverse else range(GROUP):
        own = ahead[member]
        ahead[member] = running
        running = running + own
    for mask, back_ref in enumerate(back_refs):
        back_ref[:DH] = ahead[pl.ds(place_ref[0] & (GROUP - 1) ^ mask, 1)][0]
        if back_ref.shape[0] > DH:
            back_ref[DH:] = total_ref[DH:]


def whole(*shape):
    return pl.BlockSpec(shape, lambda step: (0,) * len(shape))


PLACE = pl.BlockSpec(memory_space=pltpu.SMEM)


def call(body, in_specs, out_specs, outs, flops, name, steps=1, scratch=()):
    return pl.pallas_call(
        body,
        grid=(steps,),
        in_specs=[PLACE] + in_specs,
        out_specs=out_specs,
        out_shape=outs,
        scratch_shapes=scratch,
        compiler_params=pltpu.CompilerParams(vmem_limit_bytes=16 * 1024 * 1024),
        cost_estimate=pl.CostEstimate(flops=flops, bytes_accessed=2 << 20, transcendentals=0),
        name=name,
    )


def exchange_masks():
    masks = [GROUP]
    while masks[-1] * 2 < lax.axis_size("seq"):
        masks.append(masks[-1] * 2)
    return masks if lax.axis_size("seq") > GROUP else []


def swap(array, mask):
    if mask == 0:
        return array
    return lax.ppermute(array, "seq", [(s, s ^ mask) for s in range(lax.axis_size("seq"))])


def carried_in(pieces, reverse, place):
    held = [swap(piece, mask) for mask, piece in enumerate(pieces)]
    total = sum(held[1:], held[0])
    arrived = []
    for mask in exchange_masks():
        arrived.append(swap(total, mask))
        total = total + arrived[-1]
    single = whole(*total.shape)
    back = call(
        functools.partial(prefix_body, reverse, exchange_masks()),
        [single] * (1 + len(arrived) + GROUP),
        [single] * GROUP,
        [jax.ShapeDtypeStruct(total.shape, jnp.float32)] * GROUP,
        1 << 24,
        "prefix",
        scratch=[pltpu.VMEM((GROUP, DH, DH), jnp.float32)],
    )(place, total, *arrived, *held)
    return [swap(piece, mask) for mask, piece in enumerate(back)]


def local(queries, keys, values, out_gain, grad_out):
    full = queries.shape
    flat = (full[0] * full[1], full[2])
    assert flat == (BLOCK, HEADS * DH) and lax.axis_size("seq") % GROUP == 0
    query, key, value, grad = (a.reshape(flat) for a in (queries, keys, values, grad_out))
    gain = out_gain.reshape(1, HEADS * DH)
    square = jax.ShapeDtypeStruct((DH, DH), jnp.float32)
    taller = jax.ShapeDtypeStruct((DH + GAIN_ROWS, DH), jnp.float32)
    full_float = jax.ShapeDtypeStruct(flat, jnp.float32)
    full_low = jax.ShapeDtypeStruct(flat, jnp.bfloat16)
    half_low = jax.ShapeDtypeStruct((BLOCK, WIDE), jnp.bfloat16)
    short, tall, wide, half = whole(*square.shape), whole(*taller.shape), whole(*flat), whole(BLOCK, WIDE)
    unit = 2 * BLOCK * DH * DH * HEADS

    place = lax.axis_index("seq").astype(jnp.int32).reshape(1)
    deltas = call(
        delta_body,
        [pl.BlockSpec(memory_space=pltpu.HBM)] * 2,
        [short] * HEADS,
        [square] * HEADS,
        6 * unit,
        "delta",
        scratch=[pltpu.VMEM(flat, jnp.bfloat16)] * 2 + [pltpu.SemaphoreType.DMA((PARTS, 2))],
    )(place, *[pltpu.with_memory_space_constraint(a, pltpu.HBM) for a in (key, value)])
    chains = [slice(chain * GROUP, (chain + 1) * GROUP) for chain in range(CHAINS)]
    states = [carried_in(deltas[chain], False, place) for chain in chains]
    inner = call(
        lambda place_ref, *refs: inner_body(*refs), [wide] * 3, wide, full_float, 16 * unit, "inner"
    )(place, query, key, value)
    attns, later = [], []
    for chain in range(CHAINS):
        attn, *deltas = call(
            functools.partial(norm_body, chain),
            [wide, wide, wide, whole(1, HEADS * DH)] + [short] * GROUP,
            [half] + [tall] * GROUP,
            [half_low] + [taller] * GROUP,
            8 * unit,
            "norm",
        )(place, query, grad, inner, gain, *states[chain])
        attns.append(attn)
        later += carried_in(deltas, True, place)
    grad_query, key_part, value_part = call(
        partial_body,
        [wide] * 3 + [half] * CHAINS + [short] * HEADS,
        [wide] * 3,
        [full_low, full_float, full_float],
        48 * unit,
        "partial",
    )(place, query, key, value, *attns, *[state for chain in states for state in chain])
    gain_terms = call(
        gain_body, [tall] * HEADS, whole(HEADS, DH), jax.ShapeDtypeStruct((HEADS, DH), jnp.float32), unit, "gain"
    )(place, *later)
    docs, mask = lax.axis_size("dp"), 1
    while mask < docs:
        gain_terms = gain_terms + lax.ppermute(gain_terms, "dp", [(d, d ^ mask) for d in range(docs)])
        mask *= 2
    chunk = pl.BlockSpec((PART_ROWS, HEADS * DH), lambda step: (step, 0))
    grad_key, grad_value = call(
        final_body, [wide] * 4 + [tall] * HEADS, [chunk] * 2, [full_low] * 2, 16 * unit, "final", steps=PARTS
    )(place, key, value, key_part, value_part, *later)
    grad_gain = gain_terms / math.sqrt(lax.axis_size("seq") * docs * BLOCK)
    return (
        grad_query.reshape(full),
        grad_key.reshape(full),
        grad_value.reshape(full),
        grad_gain.reshape(HEADS * DH),
    )


def solution(mesh):
    sharded = P("dp", "seq", None)
    return jax.shard_map(
        local,
        mesh=mesh,
        in_specs=(sharded, sharded, sharded, P(), sharded),
        out_specs=(sharded, sharded, sharded, P()),
        check_vma=False,
    )
```

```python
import functools
import math

import jax
import jax.numpy as jnp
from jax import lax
from jax.experimental import pallas as pl
from jax.experimental.pallas import tpu as pltpu
from jax.sharding import PartitionSpec as P

HEADS = 8
DH = 128
BLOCK = 256
GROUP = 4
CHAINS = HEADS // GROUP
WIDE = GROUP * DH
GAIN_ROWS = 8
PARTS = 2
PART_ROWS = BLOCK // PARTS
EPSILON = 1e-06

NT = (((1,), (1,)), ((), ()))
TN = (((0,), (0,)), ((), ()))
NN = (((1,), (0,)), ((), ()))


def dot(left, right, dims):
    return lax.dot_general(left, right, dims, preferred_element_type=jnp.float32)


def columns(head):
    return pl.ds(head * DH, DH)


def own_columns(place_ref, mask, chain=0):
    return pl.ds(pl.multiple_of(chain * WIDE + (place_ref[0] & (GROUP - 1) ^ mask) * DH, DH), DH)


def causal(turned=False):
    shape, first = (BLOCK, BLOCK), int(turned)
    return lax.broadcasted_iota(jnp.int32, shape, first) >= lax.broadcasted_iota(jnp.int32, shape, 1 - first)


def delta_body(place_ref, key_ref, value_ref, *refs):
    delta_refs, (key_here, value_here, sems) = refs[:HEADS], refs[HEADS:]
    copies = []
    for part in range(PARTS):
        rows = pl.ds(part * PART_ROWS, PART_ROWS)
        for side, (source, here) in enumerate(((key_ref, key_here), (value_ref, value_here))):
            copies.append(pltpu.make_async_copy(source.at[rows], here.at[rows], sems.at[part, side]))
            copies[-1].start()
    for part in range(PARTS):
        rows = pl.ds(part * PART_ROWS, PART_ROWS)
        for copy in copies[2 * part : 2 * part + 2]:
            copy.wait()
        for at_head, delta_ref in enumerate(delta_refs):
            at = own_columns(place_ref, at_head % GROUP, at_head // GROUP)
            delta = dot(key_here[rows, at], value_here[rows, at], TN)
            delta_ref[...] = delta if part == 0 else delta_ref[...] + delta


def inner_body(query_ref, key_ref, value_ref, inner_ref):
    keep = causal()
    for head in range(HEADS):
        at = columns(head)
        scores = jnp.where(keep, dot(query_ref[:, at], key_ref[:, at], NT), 0.0).astype(jnp.bfloat16)
        inner_ref[:, at] = dot(scores, value_ref[:, at], NN)


def norm_body(chain, place_ref, query_ref, grad_ref, inner_ref, gain_ref, *refs):
    state_refs, (attn_ref, *delta_refs) = refs[:GROUP], refs[GROUP:]
    for mask, (state_ref, delta_ref) in enumerate(zip(state_refs, delta_refs)):
        at = own_columns(place_ref, mask, chain)
        query = query_ref[:, at]
        attn = inner_ref[:, at] + dot(query, state_ref[...].astype(jnp.bfloat16), NN)
        per_root = lax.rsqrt(jnp.mean(attn * attn, axis=-1, keepdims=True) + EPSILON)
        normed = attn * per_root
        cotangent = grad_ref[:, at].astype(jnp.float32)
        product = normed * cotangent
        gain = gain_ref[:, at]
        shared = jnp.mean(product * gain, axis=-1, keepdims=True)
        grad_attn = ((gain * cotangent - normed * shared) * per_root).astype(jnp.bfloat16)
        attn_ref[:, own_columns(place_ref, mask)] = grad_attn
        delta_ref[:DH] = dot(query, grad_attn, TN)
        delta_ref[DH:] = jnp.broadcast_to(jnp.sum(product, axis=0, keepdims=True), (GAIN_ROWS, DH))


def partial_body(chain, place_ref, query_ref, key_ref, value_ref, attn_ref, *refs):
    state_refs, (grad_query_ref, key_part_ref, value_part_ref) = refs[:GROUP], refs[-3:]
    keep, kept = causal(), causal(True)
    for mask, state_ref in enumerate(state_refs):
        at, here = own_columns(place_ref, mask, chain), own_columns(place_ref, mask)
        query, key, value, grad_attn = query_ref[:, at], key_ref[:, at], value_ref[:, at], attn_ref[:, here]
        turned = jnp.where(kept, dot(key, query, NT), 0.0).astype(jnp.bfloat16)
        grad_scores = jnp.where(keep, dot(grad_attn, value, NT), 0.0).astype(jnp.bfloat16)
        turned_grad = jnp.where(kept, dot(value, grad_attn, NT), 0.0).astype(jnp.bfloat16)
        carried = dot(grad_attn, state_ref[...].astype(jnp.bfloat16), NT)
        grad_query_ref[:, here] = (dot(grad_scores, key, NN) + carried).astype(jnp.bfloat16)
        key_part_ref[:, here] = dot(turned_grad, query, NN)
        value_part_ref[:, here] = dot(turned, grad_attn, NN)


def final_body(place_ref, key_ref, value_ref, *refs):
    part_refs, state_refs, (grad_key_ref, grad_value_ref) = refs[: 2 * CHAINS], refs[2 * CHAINS : -2], refs[-2:]
    rows = pl.ds(pl.multiple_of(pl.program_id(0) * PART_ROWS, PART_ROWS), PART_ROWS)
    for at_head, state_ref in enumerate(state_refs):
        chain, mask = at_head // GROUP, at_head % GROUP
        at, here = own_columns(place_ref, mask, chain), own_columns(place_ref, mask)
        state = state_ref[:DH].astype(jnp.bfloat16)
        key_part, value_part = part_refs[2 * chain][rows, here], part_refs[2 * chain + 1][rows, here]
        grad_key_ref[:, at] = (key_part + dot(value_ref[rows, at], state, NT)).astype(jnp.bfloat16)
        grad_value_ref[:, at] = (value_part + dot(key_ref[rows, at], state, NN)).astype(jnp.bfloat16)


def gain_body(place_ref, *refs):
    for at_head, state_ref in enumerate(refs[:-1]):
        row = (at_head // GROUP) * GROUP + (place_ref[0] & (GROUP - 1) ^ (at_head % GROUP))
        refs[-1][pl.ds(row, 1), :] = state_ref[DH : DH + 1]


def prefix_body(reverse, masks, place_ref, *refs):
    (total_ref, *arrived_refs), (*back_refs, ahead) = refs[: -2 * GROUP - 1], refs[-GROUP - 1 :]
    held_refs = refs[-2 * GROUP - 1 : -GROUP - 1]
    for mask, held_ref in enumerate(held_refs):
        ahead[pl.ds(place_ref[0] & (GROUP - 1) ^ mask, 1)] = held_ref[:DH][None]
    running = jnp.zeros((DH, DH), jnp.float32)
    for mask, arrived_ref in zip(masks, arrived_refs):
        later = (place_ref[0] & mask == 0) == reverse
        running = running + jnp.where(later, arrived_ref[:DH], 0.0)
    for member in reversed(range(GROUP)) if reverse else range(GROUP):
        own = ahead[member]
        ahead[member] = running
        running = running + own
    for mask, back_ref in enumerate(back_refs):
        back_ref[:DH] = ahead[pl.ds(place_ref[0] & (GROUP - 1) ^ mask, 1)][0]
        if back_ref.shape[0] > DH:
            back_ref[DH:] = total_ref[DH:]


def whole(*shape):
    return pl.BlockSpec(shape, lambda step: (0,) * len(shape))


PLACE = pl.BlockSpec(memory_space=pltpu.SMEM)


def call(body, in_specs, out_specs, outs, flops, name, steps=1, scratch=(), aliases=None):
    return pl.pallas_call(
        body,
        grid=(steps,),
        in_specs=[PLACE] + in_specs,
        out_specs=out_specs,
        out_shape=outs,
        scratch_shapes=scratch,
        input_output_aliases=aliases or {},
        compiler_params=pltpu.CompilerParams(vmem_limit_bytes=16 * 1024 * 1024),
        cost_estimate=pl.CostEstimate(flops=flops, bytes_accessed=2 << 20, transcendentals=0),
        name=name,
    )


def exchange_masks():
    masks = [GROUP]
    while masks[-1] * 2 < lax.axis_size("seq"):
        masks.append(masks[-1] * 2)
    return masks if lax.axis_size("seq") > GROUP else []


def swap(array, mask):
    if mask == 0:
        return array
    return lax.ppermute(array, "seq", [(s, s ^ mask) for s in range(lax.axis_size("seq"))])


def carried_in(pieces, reverse, place, beside=None, operands=()):
    held = [swap(piece, mask) for mask, piece in enumerate(pieces)]
    total, aside = sum(held[1:], held[0]), None
    if beside:
        total, operands = lax.optimization_barrier((total, operands))
        aside = beside(*operands)
    arrived = []
    for mask in exchange_masks():
        arrived.append(swap(total, mask))
        total = total + arrived[-1]
        if beside and len(arrived) == 1:
            total, aside = lax.optimization_barrier((total, aside))
    single = whole(*total.shape)
    back = call(
        functools.partial(prefix_body, reverse, exchange_masks()),
        [single] * (1 + len(arrived) + GROUP),
        [single] * GROUP,
        [jax.ShapeDtypeStruct(total.shape, jnp.float32)] * GROUP,
        1 << 24,
        "prefix",
        scratch=[pltpu.VMEM((GROUP, DH, DH), jnp.float32)],
    )(place, total, *arrived, *held)
    return [swap(piece, mask) for mask, piece in enumerate(back)], aside


def local(queries, keys, values, out_gain, grad_out):
    full = queries.shape
    flat = (full[0] * full[1], full[2])
    assert flat == (BLOCK, HEADS * DH) and lax.axis_size("seq") % GROUP == 0
    query, key, value, grad = (a.reshape(flat) for a in (queries, keys, values, grad_out))
    gain = out_gain.reshape(1, HEADS * DH)
    square = jax.ShapeDtypeStruct((DH, DH), jnp.float32)
    taller = jax.ShapeDtypeStruct((DH + GAIN_ROWS, DH), jnp.float32)
    full_float = jax.ShapeDtypeStruct(flat, jnp.float32)
    full_low = jax.ShapeDtypeStruct(flat, jnp.bfloat16)
    half_float = jax.ShapeDtypeStruct((BLOCK, WIDE), jnp.float32)
    half_low = jax.ShapeDtypeStruct((BLOCK, WIDE), jnp.bfloat16)
    short, tall, wide, half = whole(*square.shape), whole(*taller.shape), whole(*flat), whole(BLOCK, WIDE)
    unit = 2 * BLOCK * DH * DH * HEADS

    place = lax.axis_index("seq").astype(jnp.int32).reshape(1)
    deltas = call(
        delta_body,
        [pl.BlockSpec(memory_space=pltpu.HBM)] * 2,
        [short] * HEADS,
        [square] * HEADS,
        6 * unit,
        "delta",
        scratch=[pltpu.VMEM(flat, jnp.bfloat16)] * 2 + [pltpu.SemaphoreType.DMA((PARTS, 2))],
    )(place, *[pltpu.with_memory_space_constraint(a, pltpu.HBM) for a in (key, value)])
    chains = [slice(chain * GROUP, (chain + 1) * GROUP) for chain in range(CHAINS)]
    inner_call = call(
        lambda place_ref, *refs: inner_body(*refs), [wide] * 3, wide, full_float, 16 * unit, "inner"
    )
    first, inner = carried_in(deltas[chains[0]], False, place, inner_call, (place, query, key, value))
    states = [first] + [carried_in(deltas[chain], False, place)[0] for chain in chains[1:]]
    later, parts, grad_query = [], [], []
    for chain in range(CHAINS):
        attn, *deltas = call(
            functools.partial(norm_body, chain),
            [wide, wide, wide, whole(1, HEADS * DH)] + [short] * GROUP,
            [half] + [tall] * GROUP,
            [half_low] + [taller] * GROUP,
            8 * unit,
            "norm",
        )(place, query, grad, inner, gain, *states[chain])
        partial_call = call(
            functools.partial(partial_body, chain),
            [wide] * 3 + [half] + [short] * GROUP + [pl.BlockSpec(memory_space=pl.ANY)] * len(grad_query),
            [pl.BlockSpec((BLOCK, WIDE), lambda step, chain=chain: (0, chain)), half, half],
            [full_low, half_float, half_float],
            24 * unit,
            "partial",
            aliases={5 + GROUP: 0} if grad_query else None,
        )
        operands = (place, query, key, value, attn, *states[chain], *grad_query)
        if chain == 0:
            pieces, aside = carried_in(deltas, True, place, partial_call, operands)
        else:
            pieces, aside = carried_in(deltas, True, place)[0], partial_call(*operands)
        *grad_query, key_part, value_part = aside
        later += pieces
        parts += [key_part, value_part]
    (grad_query,) = grad_query
    gain_terms = call(
        gain_body, [tall] * HEADS, whole(HEADS, DH), jax.ShapeDtypeStruct((HEADS, DH), jnp.float32), unit, "gain"
    )(place, *later)
    docs, mask = lax.axis_size("dp"), 1
    while mask < docs:
        gain_terms = gain_terms + lax.ppermute(gain_terms, "dp", [(d, d ^ mask) for d in range(docs)])
        mask *= 2
    chunk = pl.BlockSpec((PART_ROWS, HEADS * DH), lambda step: (step, 0))
    grad_key, grad_value = call(
        final_body, [wide] * 2 + [half] * (2 * CHAINS) + [tall] * HEADS, [chunk] * 2, [full_low] * 2, 16 * unit, "final", steps=PARTS
    )(place, key, value, *parts, *later)
    grad_gain = gain_terms / math.sqrt(lax.axis_size("seq") * docs * BLOCK)
    return (
        grad_query.reshape(full),
        grad_key.reshape(full),
        grad_value.reshape(full),
        grad_gain.reshape(HEADS * DH),
    )


def solution(mesh):
    sharded = P("dp", "seq", None)
    return jax.shard_map(
        local,
        mesh=mesh,
        in_specs=(sharded, sharded, sharded, P(), sharded),
        out_specs=(sharded, sharded, sharded, P()),
        check_vma=False,
    )
```

```python
import functools
import math

import jax
import jax.numpy as jnp
from jax import lax
from jax.experimental import pallas as pl
from jax.experimental.pallas import tpu as pltpu
from jax.sharding import PartitionSpec as P

HEADS = 8
DH = 128
BLOCK = 256
GROUP = 4
CHAINS = HEADS // GROUP
WIDE = GROUP * DH
GAIN_ROWS = 8
PARTS = 2
PART_ROWS = BLOCK // PARTS
EPSILON = 1e-06

NT = (((1,), (1,)), ((), ()))
TN = (((0,), (0,)), ((), ()))
NN = (((1,), (0,)), ((), ()))


def dot(left, right, dims):
    return lax.dot_general(left, right, dims, preferred_element_type=jnp.float32)


def columns(head):
    return pl.ds(head * DH, DH)


def own_columns(place_ref, mask, chain=0):
    return pl.ds(pl.multiple_of(chain * WIDE + (place_ref[0] & (GROUP - 1) ^ mask) * DH, DH), DH)


def causal(turned=False):
    shape, first = (BLOCK, BLOCK), int(turned)
    return lax.broadcasted_iota(jnp.int32, shape, first) >= lax.broadcasted_iota(jnp.int32, shape, 1 - first)


def delta_body(place_ref, key_ref, value_ref, *refs):
    delta_refs, (key_here, value_here, sems) = refs[:HEADS], refs[HEADS:]
    copies = []
    for part in range(PARTS):
        rows = pl.ds(part * PART_ROWS, PART_ROWS)
        for side, (source, here) in enumerate(((key_ref, key_here), (value_ref, value_here))):
            copies.append(pltpu.make_async_copy(source.at[rows], here.at[rows], sems.at[part, side]))
            copies[-1].start()
    for part in range(PARTS):
        rows = pl.ds(part * PART_ROWS, PART_ROWS)
        for copy in copies[2 * part : 2 * part + 2]:
            copy.wait()
        for at_head, delta_ref in enumerate(delta_refs):
            at = own_columns(place_ref, at_head % GROUP, at_head // GROUP)
            delta = dot(key_here[rows, at], value_here[rows, at], TN)
            delta_ref[...] = delta if part == 0 else delta_ref[...] + delta


def inner_body(query_ref, key_ref, value_ref, inner_ref):
    keep = causal()
    for head in range(HEADS):
        at = columns(head)
        scores = jnp.where(keep, dot(query_ref[:, at], key_ref[:, at], NT), 0.0).astype(jnp.bfloat16)
        inner_ref[:, at] = dot(scores, value_ref[:, at], NN)


def norm_body(chain, place_ref, query_ref, grad_ref, inner_ref, gain_ref, *refs):
    state_refs, (attn_ref, *delta_refs) = refs[:GROUP], refs[GROUP:]
    for mask, (state_ref, delta_ref) in enumerate(zip(state_refs, delta_refs)):
        at = own_columns(place_ref, mask, chain)
        query = query_ref[:, at]
        attn = inner_ref[:, at] + dot(query, state_ref[...].astype(jnp.bfloat16), NN)
        per_root = lax.rsqrt(jnp.mean(attn * attn, axis=-1, keepdims=True) + EPSILON)
        normed = attn * per_root
        cotangent = grad_ref[:, at].astype(jnp.float32)
        product = normed * cotangent
        gain = gain_ref[:, at]
        shared = jnp.mean(product * gain, axis=-1, keepdims=True)
        grad_attn = ((gain * cotangent - normed * shared) * per_root).astype(jnp.bfloat16)
        attn_ref[:, own_columns(place_ref, mask)] = grad_attn
        delta_ref[:DH] = dot(query, grad_attn, TN)
        delta_ref[DH:] = jnp.broadcast_to(jnp.sum(product, axis=0, keepdims=True), (GAIN_ROWS, DH))


def partial_body(chain, place_ref, query_ref, key_ref, value_ref, attn_ref, *refs):
    state_refs, (grad_query_ref, key_part_ref, value_part_ref) = refs[:GROUP], refs[-3:]
    keep, kept = causal(), causal(True)
    for mask, state_ref in enumerate(state_refs):
        at, here = own_columns(place_ref, mask, chain), own_columns(place_ref, mask)
        query, key, value, grad_attn = query_ref[:, at], key_ref[:, at], value_ref[:, at], attn_ref[:, here]
        turned = jnp.where(kept, dot(key, query, NT), 0.0).astype(jnp.bfloat16)
        grad_scores = jnp.where(keep, dot(grad_attn, value, NT), 0.0).astype(jnp.bfloat16)
        turned_grad = jnp.where(kept, dot(value, grad_attn, NT), 0.0).astype(jnp.bfloat16)
        carried = dot(grad_attn, state_ref[...].astype(jnp.bfloat16), NT)
        grad_query_ref[:, here] = (dot(grad_scores, key, NN) + carried).astype(jnp.bfloat16)
        key_part_ref[:, here] = dot(turned_grad, query, NN)
        value_part_ref[:, here] = dot(turned, grad_attn, NN)


def final_body(place_ref, key_ref, value_ref, *refs):
    part_refs, state_refs, (grad_key_ref, grad_value_ref) = refs[: 2 * CHAINS], refs[2 * CHAINS : -2], refs[-2:]
    rows = pl.ds(pl.multiple_of(pl.program_id(0) * PART_ROWS, PART_ROWS), PART_ROWS)
    for at_head, state_ref in enumerate(state_refs):
        chain, mask = at_head // GROUP, at_head % GROUP
        at, here = own_columns(place_ref, mask, chain), own_columns(place_ref, mask)
        state = state_ref[:DH].astype(jnp.bfloat16)
        key_part, value_part = part_refs[2 * chain][rows, here], part_refs[2 * chain + 1][rows, here]
        grad_key_ref[:, at] = (key_part + dot(value_ref[rows, at], state, NT)).astype(jnp.bfloat16)
        grad_value_ref[:, at] = (value_part + dot(key_ref[rows, at], state, NN)).astype(jnp.bfloat16)


def gain_body(place_ref, *refs):
    for at_head, state_ref in enumerate(refs[:-1]):
        row = (at_head // GROUP) * GROUP + (place_ref[0] & (GROUP - 1) ^ (at_head % GROUP))
        refs[-1][pl.ds(row, 1), :] = state_ref[DH : DH + 1]


def prefix_body(reverse, masks, place_ref, *refs):
    (total_ref, *arrived_refs), (*back_refs, ahead) = refs[: -2 * GROUP - 1], refs[-GROUP - 1 :]
    held_refs = refs[-2 * GROUP - 1 : -GROUP - 1]
    for mask, held_ref in enumerate(held_refs):
        ahead[pl.ds(place_ref[0] & (GROUP - 1) ^ mask, 1)] = held_ref[:DH][None]
    running = jnp.zeros((DH, DH), jnp.float32)
    for mask, arrived_ref in zip(masks, arrived_refs):
        later = (place_ref[0] & mask == 0) == reverse
        running = running + jnp.where(later, arrived_ref[:DH], 0.0)
    for member in reversed(range(GROUP)) if reverse else range(GROUP):
        own = ahead[member]
        ahead[member] = running
        running = running + own
    for mask, back_ref in enumerate(back_refs):
        back_ref[:DH] = ahead[pl.ds(place_ref[0] & (GROUP - 1) ^ mask, 1)][0]
        if back_ref.shape[0] > DH:
            back_ref[DH:] = total_ref[DH:]


def whole(*shape):
    return pl.BlockSpec(shape, lambda step: (0,) * len(shape))


PLACE = pl.BlockSpec(memory_space=pltpu.SMEM)


def call(body, in_specs, out_specs, outs, flops, name, steps=1, scratch=(), aliases=None):
    return pl.pallas_call(
        body,
        grid=(steps,),
        in_specs=[PLACE] + in_specs,
        out_specs=out_specs,
        out_shape=outs,
        scratch_shapes=scratch,
        input_output_aliases=aliases or {},
        compiler_params=pltpu.CompilerParams(vmem_limit_bytes=16 * 1024 * 1024),
        cost_estimate=pl.CostEstimate(flops=flops, bytes_accessed=2 << 20, transcendentals=0),
        name=name,
    )


def exchange_masks():
    masks = [GROUP]
    while masks[-1] * 2 < lax.axis_size("seq"):
        masks.append(masks[-1] * 2)
    return masks if lax.axis_size("seq") > GROUP else []


def swap(array, mask):
    if mask == 0:
        return array
    return lax.ppermute(array, "seq", [(s, s ^ mask) for s in range(lax.axis_size("seq"))])


def plane_swap(pieces):
    return [swap(piece, mask) for mask, piece in enumerate(pieces)]


def beside(function, operands, first, second):
    total = sum(first[1:], first[0])
    total, operands = lax.optimization_barrier((total, operands))
    result = function(*operands)
    second, result = lax.optimization_barrier((second, result))
    return [(first, total), (second, sum(second[1:], second[0]))], result


def carried_in(held, total, reverse, place):
    arrived = []
    for mask in exchange_masks():
        arrived.append(swap(total, mask))
        total = total + arrived[-1]
    single = whole(*total.shape)
    back = call(
        functools.partial(prefix_body, reverse, exchange_masks()),
        [single] * (1 + len(arrived) + GROUP),
        [single] * GROUP,
        [jax.ShapeDtypeStruct(total.shape, jnp.float32)] * GROUP,
        1 << 24,
        "prefix",
        scratch=[pltpu.VMEM((GROUP, DH, DH), jnp.float32)],
    )(place, total, *arrived, *held)
    return [swap(piece, mask) for mask, piece in enumerate(back)]


def local(queries, keys, values, out_gain, grad_out):
    full = queries.shape
    flat = (full[0] * full[1], full[2])
    assert flat == (BLOCK, HEADS * DH) and lax.axis_size("seq") % GROUP == 0
    query, key, value, grad = (a.reshape(flat) for a in (queries, keys, values, grad_out))
    gain = out_gain.reshape(1, HEADS * DH)
    square = jax.ShapeDtypeStruct((DH, DH), jnp.float32)
    taller = jax.ShapeDtypeStruct((DH + GAIN_ROWS, DH), jnp.float32)
    full_float = jax.ShapeDtypeStruct(flat, jnp.float32)
    full_low = jax.ShapeDtypeStruct(flat, jnp.bfloat16)
    half_float = jax.ShapeDtypeStruct((BLOCK, WIDE), jnp.float32)
    half_low = jax.ShapeDtypeStruct((BLOCK, WIDE), jnp.bfloat16)
    short, tall, wide, half = whole(*square.shape), whole(*taller.shape), whole(*flat), whole(BLOCK, WIDE)
    unit = 2 * BLOCK * DH * DH * HEADS

    place = lax.axis_index("seq").astype(jnp.int32).reshape(1)
    deltas = call(
        delta_body,
        [pl.BlockSpec(memory_space=pltpu.HBM)] * 2,
        [short] * HEADS,
        [square] * HEADS,
        6 * unit,
        "delta",
        scratch=[pltpu.VMEM(flat, jnp.bfloat16)] * 2 + [pltpu.SemaphoreType.DMA((PARTS, 2))],
    )(place, *[pltpu.with_memory_space_constraint(a, pltpu.HBM) for a in (key, value)])
    chains = [slice(chain * GROUP, (chain + 1) * GROUP) for chain in range(CHAINS)]
    inner_call = call(
        lambda place_ref, *refs: inner_body(*refs), [wide] * 3, wide, full_float, 16 * unit, "inner"
    )
    sums, inner = beside(inner_call, (place, query, key, value), *[plane_swap(deltas[chain]) for chain in chains])
    states = [carried_in(held, total, False, place) for held, total in sums]
    attns, helds = [], []
    for chain in range(CHAINS):
        attn, *deltas = call(
            functools.partial(norm_body, chain),
            [wide, wide, wide, whole(1, HEADS * DH)] + [short] * GROUP,
            [half] + [tall] * GROUP,
            [half_low] + [taller] * GROUP,
            8 * unit,
            "norm",
        )(place, query, grad, inner, gain, *states[chain])
        attns.append(attn)
        helds.append(plane_swap(deltas))

    def partial_call(chain, *operands):
        return call(
            functools.partial(partial_body, chain),
            [wide] * 3 + [half] + [short] * GROUP + [pl.BlockSpec(memory_space=pl.ANY)] * chain,
            [pl.BlockSpec((BLOCK, WIDE), lambda step: (0, chain)), half, half],
            [full_low, half_float, half_float],
            24 * unit,
            "partial",
            aliases={5 + GROUP: 0} if chain else None,
        )(*operands)

    operands = [(place, query, key, value, attns[chain], *states[chain]) for chain in range(CHAINS)]
    sums, (grad_query, *parts) = beside(functools.partial(partial_call, 0), operands[0], *helds)
    later = [piece for held, total in sums for piece in carried_in(held, total, True, place)]
    grad_query, *rest = partial_call(1, *operands[1], grad_query)
    parts += rest
    gain_terms = call(
        gain_body, [tall] * HEADS, whole(HEADS, DH), jax.ShapeDtypeStruct((HEADS, DH), jnp.float32), unit, "gain"
    )(place, *later)
    docs, mask = lax.axis_size("dp"), 1
    while mask < docs:
        gain_terms = gain_terms + lax.ppermute(gain_terms, "dp", [(d, d ^ mask) for d in range(docs)])
        mask *= 2
    chunk = pl.BlockSpec((PART_ROWS, HEADS * DH), lambda step: (step, 0))
    grad_key, grad_value = call(
        final_body, [wide] * 2 + [half] * (2 * CHAINS) + [tall] * HEADS, [chunk] * 2, [full_low] * 2, 16 * unit, "final", steps=PARTS
    )(place, key, value, *parts, *later)
    grad_gain = gain_terms / math.sqrt(lax.axis_size("seq") * docs * BLOCK)
    return (
        grad_query.reshape(full),
        grad_key.reshape(full),
        grad_value.reshape(full),
        grad_gain.reshape(HEADS * DH),
    )


def solution(mesh):
    sharded = P("dp", "seq", None)
    return jax.shard_map(
        local,
        mesh=mesh,
        in_specs=(sharded, sharded, sharded, P(), sharded),
        out_specs=(sharded, sharded, sharded, P()),
        check_vma=False,
    )
```

```python
import functools
import math

import jax
import jax.numpy as jnp
from jax import lax
from jax.experimental import pallas as pl
from jax.experimental.pallas import tpu as pltpu
from jax.sharding import PartitionSpec as P

HEADS = 8
DH = 128
BLOCK = 256
GROUP = 4
CHAINS = HEADS // GROUP
WIDE = GROUP * DH
GAIN_ROWS = 8
ORDER = (0, 3, 2, 1)
PARTS = 2
PART_ROWS = BLOCK // PARTS
EPSILON = 1e-06

NT = (((1,), (1,)), ((), ()))
TN = (((0,), (0,)), ((), ()))
NN = (((1,), (0,)), ((), ()))


def dot(left, right, dims):
    return lax.dot_general(left, right, dims, preferred_element_type=jnp.float32)


def columns(head):
    return pl.ds(head * DH, DH)


def own_columns(place_ref, mask, chain=0):
    return pl.ds(pl.multiple_of(chain * WIDE + (place_ref[0] & (GROUP - 1) ^ mask) * DH, DH), DH)


def causal(turned=False):
    shape, first = (BLOCK, BLOCK), int(turned)
    return lax.broadcasted_iota(jnp.int32, shape, first) >= lax.broadcasted_iota(jnp.int32, shape, 1 - first)


def delta_body(place_ref, key_ref, value_ref, *refs):
    delta_refs, (key_here, value_here, sems) = refs[:HEADS], refs[HEADS:]
    copies = []
    for part in range(PARTS):
        rows = pl.ds(part * PART_ROWS, PART_ROWS)
        for side, (source, here) in enumerate(((key_ref, key_here), (value_ref, value_here))):
            copies.append(pltpu.make_async_copy(source.at[rows], here.at[rows], sems.at[part, side]))
            copies[-1].start()
    for part in range(PARTS):
        rows = pl.ds(part * PART_ROWS, PART_ROWS)
        for copy in copies[2 * part : 2 * part + 2]:
            copy.wait()
        for at_head, delta_ref in enumerate(delta_refs):
            at = own_columns(place_ref, ORDER[at_head % GROUP], at_head // GROUP)
            delta = dot(key_here[rows, at], value_here[rows, at], TN)
            delta_ref[...] = delta if part == 0 else delta_ref[...] + delta


def inner_body(query_ref, key_ref, value_ref, inner_ref):
    keep = causal()
    for head in range(HEADS):
        at = columns(head)
        scores = jnp.where(keep, dot(query_ref[:, at], key_ref[:, at], NT), 0.0).astype(jnp.bfloat16)
        inner_ref[:, at] = dot(scores, value_ref[:, at], NN)


def norm_body(chain, place_ref, query_ref, grad_ref, inner_ref, gain_ref, *refs):
    state_refs, (attn_ref, *delta_refs) = refs[:GROUP], refs[GROUP:]
    for mask, state_ref, delta_ref in zip(ORDER, state_refs, delta_refs):
        at = own_columns(place_ref, mask, chain)
        query = query_ref[:, at]
        attn = inner_ref[:, at] + dot(query, state_ref[...].astype(jnp.bfloat16), NN)
        per_root = lax.rsqrt(jnp.mean(attn * attn, axis=-1, keepdims=True) + EPSILON)
        normed = attn * per_root
        cotangent = grad_ref[:, at].astype(jnp.float32)
        product = normed * cotangent
        gain = gain_ref[:, at]
        shared = jnp.mean(product * gain, axis=-1, keepdims=True)
        grad_attn = ((gain * cotangent - normed * shared) * per_root).astype(jnp.bfloat16)
        attn_ref[:, own_columns(place_ref, mask)] = grad_attn
        delta_ref[:DH] = dot(query, grad_attn, TN)
        delta_ref[DH:] = jnp.broadcast_to(jnp.sum(product, axis=0, keepdims=True), (GAIN_ROWS, DH))


def partial_body(chain, place_ref, query_ref, key_ref, value_ref, attn_ref, *refs):
    state_refs, (grad_query_ref, key_part_ref, value_part_ref) = refs[:GROUP], refs[-3:]
    keep, kept = causal(), causal(True)
    for mask, state_ref in zip(ORDER, state_refs):
        at, here = own_columns(place_ref, mask, chain), own_columns(place_ref, mask)
        query, key, value, grad_attn = query_ref[:, at], key_ref[:, at], value_ref[:, at], attn_ref[:, here]
        turned = jnp.where(kept, dot(key, query, NT), 0.0).astype(jnp.bfloat16)
        grad_scores = jnp.where(keep, dot(grad_attn, value, NT), 0.0).astype(jnp.bfloat16)
        turned_grad = jnp.where(kept, dot(value, grad_attn, NT), 0.0).astype(jnp.bfloat16)
        carried = dot(grad_attn, state_ref[...].astype(jnp.bfloat16), NT)
        grad_query_ref[:, here] = (dot(grad_scores, key, NN) + carried).astype(jnp.bfloat16)
        key_part_ref[:, here] = dot(turned_grad, query, NN)
        value_part_ref[:, here] = dot(turned, grad_attn, NN)


def final_body(place_ref, key_ref, value_ref, *refs):
    part_refs, state_refs, (grad_key_ref, grad_value_ref) = refs[: 2 * CHAINS], refs[2 * CHAINS : -2], refs[-2:]
    rows = pl.ds(pl.multiple_of(pl.program_id(0) * PART_ROWS, PART_ROWS), PART_ROWS)
    for at_head, state_ref in enumerate(state_refs):
        chain, mask = at_head // GROUP, ORDER[at_head % GROUP]
        at, here = own_columns(place_ref, mask, chain), own_columns(place_ref, mask)
        state = state_ref[:DH].astype(jnp.bfloat16)
        key_part, value_part = part_refs[2 * chain][rows, here], part_refs[2 * chain + 1][rows, here]
        grad_key_ref[:, at] = (key_part + dot(value_ref[rows, at], state, NT)).astype(jnp.bfloat16)
        grad_value_ref[:, at] = (value_part + dot(key_ref[rows, at], state, NN)).astype(jnp.bfloat16)


def gain_body(place_ref, *refs):
    for at_head, state_ref in enumerate(refs[:-1]):
        row = (at_head // GROUP) * GROUP + (place_ref[0] & (GROUP - 1) ^ ORDER[at_head % GROUP])
        refs[-1][pl.ds(row, 1), :] = state_ref[DH : DH + 1]


def prefix_body(reverse, masks, place_ref, *refs):
    (total_ref, *arrived_refs), (*back_refs, ahead) = refs[: -2 * GROUP - 1], refs[-GROUP - 1 :]
    held_refs = refs[-2 * GROUP - 1 : -GROUP - 1]
    for mask, held_ref in zip(ORDER, held_refs):
        ahead[pl.ds(place_ref[0] & (GROUP - 1) ^ mask, 1)] = held_ref[:DH][None]
    running = jnp.zeros((DH, DH), jnp.float32)
    for mask, arrived_ref in zip(masks, arrived_refs):
        later = (place_ref[0] & mask == 0) == reverse
        running = running + jnp.where(later, arrived_ref[:DH], 0.0)
    for member in reversed(range(GROUP)) if reverse else range(GROUP):
        own = ahead[member]
        ahead[member] = running
        running = running + own
    for mask, back_ref in zip(ORDER, back_refs):
        back_ref[:DH] = ahead[pl.ds(place_ref[0] & (GROUP - 1) ^ mask, 1)][0]
        if back_ref.shape[0] > DH:
            back_ref[DH:] = total_ref[DH:]


def whole(*shape):
    return pl.BlockSpec(shape, lambda step: (0,) * len(shape))


PLACE = pl.BlockSpec(memory_space=pltpu.SMEM)


def call(body, in_specs, out_specs, outs, flops, name, steps=1, scratch=(), aliases=None):
    return pl.pallas_call(
        body,
        grid=(steps,),
        in_specs=[PLACE] + in_specs,
        out_specs=out_specs,
        out_shape=outs,
        scratch_shapes=scratch,
        input_output_aliases=aliases or {},
        compiler_params=pltpu.CompilerParams(vmem_limit_bytes=16 * 1024 * 1024),
        cost_estimate=pl.CostEstimate(flops=flops, bytes_accessed=2 << 20, transcendentals=0),
        name=name,
    )


def exchange_masks():
    masks = [GROUP]
    while masks[-1] * 2 < lax.axis_size("seq"):
        masks.append(masks[-1] * 2)
    return masks if lax.axis_size("seq") > GROUP else []


def swap(array, mask):
    if mask == 0:
        return array
    return lax.ppermute(array, "seq", [(s, s ^ mask) for s in range(lax.axis_size("seq"))])


def plane_swap(pieces):
    return [swap(piece, mask) for mask, piece in zip(ORDER, pieces)]


def beside(function, operands, first, second):
    total = sum(first[1:], first[0])
    total, operands = lax.optimization_barrier((total, operands))
    result = function(*operands)
    second, result = lax.optimization_barrier((second, result))
    return [(first, total), (second, sum(second[1:], second[0]))], result


def carried_in(held, total, reverse, place):
    arrived = []
    for mask in exchange_masks():
        arrived.append(swap(total, mask))
        total = total + arrived[-1]
    single = whole(*total.shape)
    back = call(
        functools.partial(prefix_body, reverse, exchange_masks()),
        [single] * (1 + len(arrived) + GROUP),
        [single] * GROUP,
        [jax.ShapeDtypeStruct(total.shape, jnp.float32)] * GROUP,
        1 << 24,
        "prefix",
        scratch=[pltpu.VMEM((GROUP, DH, DH), jnp.float32)],
    )(place, total, *arrived, *held)
    return plane_swap(back)


def local(queries, keys, values, out_gain, grad_out):
    full = queries.shape
    flat = (full[0] * full[1], full[2])
    assert flat == (BLOCK, HEADS * DH) and lax.axis_size("seq") % GROUP == 0
    query, key, value, grad = (a.reshape(flat) for a in (queries, keys, values, grad_out))
    gain = out_gain.reshape(1, HEADS * DH)
    square = jax.ShapeDtypeStruct((DH, DH), jnp.float32)
    taller = jax.ShapeDtypeStruct((DH + GAIN_ROWS, DH), jnp.float32)
    full_float = jax.ShapeDtypeStruct(flat, jnp.float32)
    full_low = jax.ShapeDtypeStruct(flat, jnp.bfloat16)
    half_float = jax.ShapeDtypeStruct((BLOCK, WIDE), jnp.float32)
    half_low = jax.ShapeDtypeStruct((BLOCK, WIDE), jnp.bfloat16)
    short, tall, wide, half = whole(*square.shape), whole(*taller.shape), whole(*flat), whole(BLOCK, WIDE)
    unit = 2 * BLOCK * DH * DH * HEADS

    place = lax.axis_index("seq").astype(jnp.int32).reshape(1)
    deltas = call(
        delta_body,
        [pl.BlockSpec(memory_space=pltpu.HBM)] * 2,
        [short] * HEADS,
        [square] * HEADS,
        6 * unit,
        "delta",
        scratch=[pltpu.VMEM(flat, jnp.bfloat16)] * 2 + [pltpu.SemaphoreType.DMA((PARTS, 2))],
    )(place, *[pltpu.with_memory_space_constraint(a, pltpu.HBM) for a in (key, value)])
    chains = [slice(chain * GROUP, (chain + 1) * GROUP) for chain in range(CHAINS)]
    inner_call = call(
        lambda place_ref, *refs: inner_body(*refs), [wide] * 3, wide, full_float, 16 * unit, "inner"
    )
    sums, inner = beside(inner_call, (place, query, key, value), *[plane_swap(deltas[chain]) for chain in chains])
    states = [carried_in(held, total, False, place) for held, total in sums]
    attns, helds = [], []
    for chain in range(CHAINS):
        attn, *deltas = call(
            functools.partial(norm_body, chain),
            [wide, wide, wide, whole(1, HEADS * DH)] + [short] * GROUP,
            [half] + [tall] * GROUP,
            [half_low] + [taller] * GROUP,
            8 * unit,
            "norm",
        )(place, query, grad, inner, gain, *states[chain])
        attns.append(attn)
        helds.append(plane_swap(deltas))

    def partial_call(chain, *operands):
        return call(
            functools.partial(partial_body, chain),
            [wide] * 3 + [half] + [short] * GROUP + [pl.BlockSpec(memory_space=pl.ANY)] * chain,
            [pl.BlockSpec((BLOCK, WIDE), lambda step: (0, chain)), half, half],
            [full_low, half_float, half_float],
            24 * unit,
            "partial",
            aliases={5 + GROUP: 0} if chain else None,
        )(*operands)

    operands = [(place, query, key, value, attns[chain], *states[chain]) for chain in range(CHAINS)]
    sums, (grad_query, *parts) = beside(functools.partial(partial_call, 0), operands[0], *helds)
    later = [piece for held, total in sums for piece in carried_in(held, total, True, place)]
    grad_query, *rest = partial_call(1, *operands[1], grad_query)
    parts += rest
    gain_terms = call(
        gain_body, [tall] * HEADS, whole(HEADS, DH), jax.ShapeDtypeStruct((HEADS, DH), jnp.float32), unit, "gain"
    )(place, *later)
    docs, mask = lax.axis_size("dp"), 1
    while mask < docs:
        gain_terms = gain_terms + lax.ppermute(gain_terms, "dp", [(d, d ^ mask) for d in range(docs)])
        mask *= 2
    chunk = pl.BlockSpec((PART_ROWS, HEADS * DH), lambda step: (step, 0))
    grad_key, grad_value = call(
        final_body, [wide] * 2 + [half] * (2 * CHAINS) + [tall] * HEADS, [chunk] * 2, [full_low] * 2, 16 * unit, "final", steps=PARTS
    )(place, key, value, *parts, *later)
    grad_gain = gain_terms / math.sqrt(lax.axis_size("seq") * docs * BLOCK)
    return (
        grad_query.reshape(full),
        grad_key.reshape(full),
        grad_value.reshape(full),
        grad_gain.reshape(HEADS * DH),
    )


def solution(mesh):
    sharded = P("dp", "seq", None)
    return jax.shard_map(
        local,
        mesh=mesh,
        in_specs=(sharded, sharded, sharded, P(), sharded),
        out_specs=(sharded, sharded, sharded, P()),
        check_vma=False,
    )
```

```python
import functools
import math

import jax
import jax.numpy as jnp
from jax import lax
from jax.experimental import pallas as pl
from jax.experimental.pallas import tpu as pltpu
from jax.sharding import PartitionSpec as P

HEADS = 8
DH = 128
BLOCK = 256
GROUP = 4
CHAINS = HEADS // GROUP
WIDE = GROUP * DH
GAIN_ROWS = 8
ORDER = (0, 3, 2, 1)
PARTS = 2
PART_ROWS = BLOCK // PARTS
EPSILON = 1e-06

NT = (((1,), (1,)), ((), ()))
TN = (((0,), (0,)), ((), ()))
NN = (((1,), (0,)), ((), ()))


def dot(left, right, dims):
    return lax.dot_general(left, right, dims, preferred_element_type=jnp.float32)


def columns(head):
    return pl.ds(head * DH, DH)


def own_columns(place_ref, mask, chain=0):
    return pl.ds(pl.multiple_of(chain * WIDE + (place_ref[0] & (GROUP - 1) ^ mask) * DH, DH), DH)


def causal(turned=False):
    shape, first = (BLOCK, BLOCK), int(turned)
    return lax.broadcasted_iota(jnp.int32, shape, first) >= lax.broadcasted_iota(jnp.int32, shape, 1 - first)


def delta_body(place_ref, key_ref, value_ref, *refs):
    delta_refs, (key_here, value_here, sems) = refs[:HEADS], refs[HEADS:]
    copies = []
    for part in range(PARTS):
        rows = pl.ds(part * PART_ROWS, PART_ROWS)
        for side, (source, here) in enumerate(((key_ref, key_here), (value_ref, value_here))):
            copies.append(pltpu.make_async_copy(source.at[rows], here.at[rows], sems.at[part, side]))
            copies[-1].start()
    for part in range(PARTS):
        rows = pl.ds(part * PART_ROWS, PART_ROWS)
        for copy in copies[2 * part : 2 * part + 2]:
            copy.wait()
        for at_head, delta_ref in enumerate(delta_refs):
            at = own_columns(place_ref, ORDER[at_head % GROUP], at_head // GROUP)
            delta = dot(key_here[rows, at], value_here[rows, at], TN)
            delta_ref[...] = delta if part == 0 else delta_ref[...] + delta


def inner_body(query_ref, key_ref, value_ref, inner_ref):
    keep = causal()
    for head in range(HEADS):
        at = columns(head)
        scores = jnp.where(keep, dot(query_ref[:, at], key_ref[:, at], NT), 0.0).astype(jnp.bfloat16)
        inner_ref[:, at] = dot(scores, value_ref[:, at], NN)


def norm_body(chain, place_ref, query_ref, grad_ref, inner_ref, gain_ref, *refs):
    state_refs, (attn_ref, *delta_refs) = refs[:GROUP], refs[GROUP:]
    for mask, state_ref, delta_ref in zip(ORDER, state_refs, delta_refs):
        at = own_columns(place_ref, mask, chain)
        query = query_ref[:, at]
        attn = inner_ref[:, at] + dot(query, state_ref[...].astype(jnp.bfloat16), NN)
        per_root = lax.rsqrt(jnp.mean(attn * attn, axis=-1, keepdims=True) + EPSILON)
        normed = attn * per_root
        cotangent = grad_ref[:, at].astype(jnp.float32)
        product = normed * cotangent
        gain = gain_ref[:, at]
        shared = jnp.mean(product * gain, axis=-1, keepdims=True)
        grad_attn = ((gain * cotangent - normed * shared) * per_root).astype(jnp.bfloat16)
        attn_ref[:, own_columns(place_ref, mask)] = grad_attn
        delta_ref[:DH] = dot(query, grad_attn, TN)
        delta_ref[DH:] = jnp.broadcast_to(jnp.sum(product, axis=0, keepdims=True), (GAIN_ROWS, DH))


def partial_body(chain, place_ref, query_ref, key_ref, value_ref, attn_ref, *refs):
    state_refs, (grad_query_ref, key_part_ref, value_part_ref) = refs[:GROUP], refs[-3:]
    keep, kept = causal(), causal(True)
    for mask, state_ref in zip(ORDER, state_refs):
        at, here = own_columns(place_ref, mask, chain), own_columns(place_ref, mask)
        query, key, value, grad_attn = query_ref[:, at], key_ref[:, at], value_ref[:, at], attn_ref[:, here]
        turned = jnp.where(kept, dot(key, query, NT), 0.0).astype(jnp.bfloat16)
        grad_scores = jnp.where(keep, dot(grad_attn, value, NT), 0.0).astype(jnp.bfloat16)
        turned_grad = jnp.where(kept, dot(value, grad_attn, NT), 0.0).astype(jnp.bfloat16)
        carried = dot(grad_attn, state_ref[...].astype(jnp.bfloat16), NT)
        grad_query_ref[:, here] = (dot(grad_scores, key, NN) + carried).astype(jnp.bfloat16)
        key_part_ref[:, here] = dot(turned_grad, query, NN)
        value_part_ref[:, here] = dot(turned, grad_attn, NN)


def final_body(place_ref, key_ref, value_ref, *refs):
    part_refs, state_refs, (grad_key_ref, grad_value_ref) = refs[: 2 * CHAINS], refs[2 * CHAINS : -2], refs[-2:]
    rows = pl.ds(pl.multiple_of(pl.program_id(0) * PART_ROWS, PART_ROWS), PART_ROWS)
    for at_head, state_ref in enumerate(state_refs):
        chain, mask = at_head // GROUP, ORDER[at_head % GROUP]
        at, here = own_columns(place_ref, mask, chain), own_columns(place_ref, mask)
        state = state_ref[:DH].astype(jnp.bfloat16)
        key_part, value_part = part_refs[2 * chain][rows, here], part_refs[2 * chain + 1][rows, here]
        grad_key_ref[:, at] = (key_part + dot(value_ref[rows, at], state, NT)).astype(jnp.bfloat16)
        grad_value_ref[:, at] = (value_part + dot(key_ref[rows, at], state, NN)).astype(jnp.bfloat16)


def gain_body(place_ref, *refs):
    for at_head, state_ref in enumerate(refs[:-1]):
        row = (at_head // GROUP) * GROUP + (place_ref[0] & (GROUP - 1) ^ ORDER[at_head % GROUP])
        refs[-1][pl.ds(row, 1), :] = state_ref[DH : DH + 1]


def prefix_body(reverse, masks, place_ref, *refs):
    (total_ref, *arrived_refs), (*back_refs, ahead) = refs[: -2 * GROUP - 1], refs[-GROUP - 1 :]
    held_refs = refs[-2 * GROUP - 1 : -GROUP - 1]
    for mask, held_ref in zip(ORDER, held_refs):
        ahead[pl.ds(place_ref[0] & (GROUP - 1) ^ mask, 1)] = held_ref[:DH][None]
    running = jnp.zeros((DH, DH), jnp.float32)
    for mask, arrived_ref in zip(masks, arrived_refs):
        later = (place_ref[0] ^ mask < place_ref[0]) != reverse
        running = running + jnp.where(later, arrived_ref[:DH], 0.0)
    for member in reversed(range(GROUP)) if reverse else range(GROUP):
        own = ahead[member]
        ahead[member] = running
        running = running + own
    for mask, back_ref in zip(ORDER, back_refs):
        back_ref[:DH] = ahead[pl.ds(place_ref[0] & (GROUP - 1) ^ mask, 1)][0]
        if back_ref.shape[0] > DH:
            back_ref[DH:] = total_ref[DH:]


def whole(*shape):
    return pl.BlockSpec(shape, lambda step: (0,) * len(shape))


PLACE = pl.BlockSpec(memory_space=pltpu.SMEM)


def call(body, in_specs, out_specs, outs, flops, name, steps=1, scratch=(), aliases=None):
    return pl.pallas_call(
        body,
        grid=(steps,),
        in_specs=[PLACE] + in_specs,
        out_specs=out_specs,
        out_shape=outs,
        scratch_shapes=scratch,
        input_output_aliases=aliases or {},
        compiler_params=pltpu.CompilerParams(vmem_limit_bytes=16 * 1024 * 1024),
        cost_estimate=pl.CostEstimate(flops=flops, bytes_accessed=2 << 20, transcendentals=0),
        name=name,
    )


def exchange_steps():
    count, base, steps = lax.axis_size("seq"), GROUP, []
    while base < count:
        masks = [base, 2 * base, 3 * base] if 4 * base <= count else [base]
        steps.append(masks)
        base *= len(masks) + 1
    return steps


def swap(array, mask):
    if mask == 0:
        return array
    return lax.ppermute(array, "seq", [(s, s ^ mask) for s in range(lax.axis_size("seq"))])


def plane_swap(pieces):
    return [swap(piece, mask) for mask, piece in zip(ORDER, pieces)]


def beside(function, operands, first, second):
    total = sum(first[1:], first[0])
    total, operands = lax.optimization_barrier((total, operands))
    result = function(*operands)
    second, result = lax.optimization_barrier((second, result))
    return [(first, total), (second, sum(second[1:], second[0]))], result


def carried_in(held, total, reverse, place):
    arrived = []
    for masks in exchange_steps():
        arrived += [swap(total, mask) for mask in masks]
        total = sum(arrived[-len(masks) :], total)
    single = whole(*total.shape)
    back = call(
        functools.partial(prefix_body, reverse, sum(exchange_steps(), [])),
        [single] * (1 + len(arrived) + GROUP),
        [single] * GROUP,
        [jax.ShapeDtypeStruct(total.shape, jnp.float32)] * GROUP,
        1 << 24,
        "prefix",
        scratch=[pltpu.VMEM((GROUP, DH, DH), jnp.float32)],
    )(place, total, *arrived, *held)
    return plane_swap(back)


def local(queries, keys, values, out_gain, grad_out):
    full = queries.shape
    flat = (full[0] * full[1], full[2])
    assert flat == (BLOCK, HEADS * DH) and lax.axis_size("seq") % GROUP == 0
    query, key, value, grad = (a.reshape(flat) for a in (queries, keys, values, grad_out))
    gain = out_gain.reshape(1, HEADS * DH)
    square = jax.ShapeDtypeStruct((DH, DH), jnp.float32)
    taller = jax.ShapeDtypeStruct((DH + GAIN_ROWS, DH), jnp.float32)
    full_float = jax.ShapeDtypeStruct(flat, jnp.float32)
    full_low = jax.ShapeDtypeStruct(flat, jnp.bfloat16)
    half_float = jax.ShapeDtypeStruct((BLOCK, WIDE), jnp.float32)
    half_low = jax.ShapeDtypeStruct((BLOCK, WIDE), jnp.bfloat16)
    short, tall, wide, half = whole(*square.shape), whole(*taller.shape), whole(*flat), whole(BLOCK, WIDE)
    unit = 2 * BLOCK * DH * DH * HEADS

    place = lax.axis_index("seq").astype(jnp.int32).reshape(1)
    deltas = call(
        delta_body,
        [pl.BlockSpec(memory_space=pltpu.HBM)] * 2,
        [short] * HEADS,
        [square] * HEADS,
        6 * unit,
        "delta",
        scratch=[pltpu.VMEM(flat, jnp.bfloat16)] * 2 + [pltpu.SemaphoreType.DMA((PARTS, 2))],
    )(place, *[pltpu.with_memory_space_constraint(a, pltpu.HBM) for a in (key, value)])
    chains = [slice(chain * GROUP, (chain + 1) * GROUP) for chain in range(CHAINS)]
    inner_call = call(
        lambda place_ref, *refs: inner_body(*refs), [wide] * 3, wide, full_float, 16 * unit, "inner"
    )
    sums, inner = beside(inner_call, (place, query, key, value), *[plane_swap(deltas[chain]) for chain in chains])
    states = [carried_in(held, total, False, place) for held, total in sums]
    attns, helds = [], []
    for chain in range(CHAINS):
        attn, *deltas = call(
            functools.partial(norm_body, chain),
            [wide, wide, wide, whole(1, HEADS * DH)] + [short] * GROUP,
            [half] + [tall] * GROUP,
            [half_low] + [taller] * GROUP,
            8 * unit,
            "norm",
        )(place, query, grad, inner, gain, *states[chain])
        attns.append(attn)
        helds.append(plane_swap(deltas))

    def partial_call(chain, *operands):
        return call(
            functools.partial(partial_body, chain),
            [wide] * 3 + [half] + [short] * GROUP + [pl.BlockSpec(memory_space=pl.ANY)] * chain,
            [pl.BlockSpec((BLOCK, WIDE), lambda step: (0, chain)), half, half],
            [full_low, half_float, half_float],
            24 * unit,
            "partial",
            aliases={5 + GROUP: 0} if chain else None,
        )(*operands)

    operands = [(place, query, key, value, attns[chain], *states[chain]) for chain in range(CHAINS)]
    sums, (grad_query, *parts) = beside(functools.partial(partial_call, 0), operands[0], *helds)
    later = [piece for held, total in sums for piece in carried_in(held, total, True, place)]
    grad_query, *rest = partial_call(1, *operands[1], grad_query)
    parts += rest
    gain_terms = call(
        gain_body, [tall] * HEADS, whole(HEADS, DH), jax.ShapeDtypeStruct((HEADS, DH), jnp.float32), unit, "gain"
    )(place, *later)
    docs, mask = lax.axis_size("dp"), 1
    while mask < docs:
        gain_terms = gain_terms + lax.ppermute(gain_terms, "dp", [(d, d ^ mask) for d in range(docs)])
        mask *= 2
    chunk = pl.BlockSpec((PART_ROWS, HEADS * DH), lambda step: (step, 0))
    grad_key, grad_value = call(
        final_body, [wide] * 2 + [half] * (2 * CHAINS) + [tall] * HEADS, [chunk] * 2, [full_low] * 2, 16 * unit, "final", steps=PARTS
    )(place, key, value, *parts, *later)
    grad_gain = gain_terms / math.sqrt(lax.axis_size("seq") * docs * BLOCK)
    return (
        grad_query.reshape(full),
        grad_key.reshape(full),
        grad_value.reshape(full),
        grad_gain.reshape(HEADS * DH),
    )


def solution(mesh):
    sharded = P("dp", "seq", None)
    return jax.shard_map(
        local,
        mesh=mesh,
        in_specs=(sharded, sharded, sharded, P(), sharded),
        out_specs=(sharded, sharded, sharded, P()),
        check_vma=False,
    )
```

```python
import functools
import math

import jax
import jax.numpy as jnp
from jax import lax
from jax.experimental import pallas as pl
from jax.experimental.pallas import tpu as pltpu
from jax.sharding import PartitionSpec as P

HEADS = 8
DH = 128
BLOCK = 256
GROUP = 4
CHAINS = HEADS // GROUP
WIDE = GROUP * DH
GAIN_ROWS = 8
ORDER = (0, 3, 2, 1)
PARTS = 2
PART_ROWS = BLOCK // PARTS
EPSILON = 1e-06

NT = (((1,), (1,)), ((), ()))
TN = (((0,), (0,)), ((), ()))
NN = (((1,), (0,)), ((), ()))


def dot(left, right, dims):
    return lax.dot_general(left, right, dims, preferred_element_type=jnp.float32)


def columns(head):
    return pl.ds(head * DH, DH)


def own_columns(place_ref, mask, chain=0):
    return pl.ds(pl.multiple_of(chain * WIDE + (place_ref[0] & (GROUP - 1) ^ mask) * DH, DH), DH)


def causal(turned=False):
    shape, first = (BLOCK, BLOCK), int(turned)
    return lax.broadcasted_iota(jnp.int32, shape, first) >= lax.broadcasted_iota(jnp.int32, shape, 1 - first)


def delta_body(place_ref, key_ref, value_ref, *refs):
    delta_refs, (key_here, value_here, sems) = refs[:HEADS], refs[HEADS:]
    copies = []
    for part in range(PARTS):
        rows = pl.ds(part * PART_ROWS, PART_ROWS)
        for side, (source, here) in enumerate(((key_ref, key_here), (value_ref, value_here))):
            copies.append(pltpu.make_async_copy(source.at[rows], here.at[rows], sems.at[part, side]))
            copies[-1].start()
    for part in range(PARTS):
        rows = pl.ds(part * PART_ROWS, PART_ROWS)
        for copy in copies[2 * part : 2 * part + 2]:
            copy.wait()
        for at_head, delta_ref in enumerate(delta_refs):
            at = own_columns(place_ref, ORDER[at_head % GROUP], at_head // GROUP)
            delta = dot(key_here[rows, at], value_here[rows, at], TN)
            delta_ref[...] = delta if part == 0 else delta_ref[...] + delta


def inner_body(query_ref, key_ref, value_ref, inner_ref):
    keep = causal()
    for head in range(HEADS):
        at = columns(head)
        scores = jnp.where(keep, dot(query_ref[:, at], key_ref[:, at], NT), 0.0).astype(jnp.bfloat16)
        inner_ref[:, at] = dot(scores, value_ref[:, at], NN)


def norm_body(chain, place_ref, query_ref, grad_ref, inner_ref, gain_ref, *refs):
    state_refs, (attn_ref, *delta_refs) = refs[:GROUP], refs[GROUP:]
    for mask, state_ref, delta_ref in zip(ORDER, state_refs, delta_refs):
        at = own_columns(place_ref, mask, chain)
        query = query_ref[:, at]
        attn = inner_ref[:, at] + dot(query, state_ref[...].astype(jnp.bfloat16), NN)
        per_root = lax.rsqrt(jnp.mean(attn * attn, axis=-1, keepdims=True) + EPSILON)
        normed = attn * per_root
        cotangent = grad_ref[:, at].astype(jnp.float32)
        product = normed * cotangent
        gain = gain_ref[:, at]
        shared = jnp.mean(product * gain, axis=-1, keepdims=True)
        grad_attn = ((gain * cotangent - normed * shared) * per_root).astype(jnp.bfloat16)
        attn_ref[:, own_columns(place_ref, mask)] = grad_attn
        delta_ref[:DH] = dot(query, grad_attn, TN)
        delta_ref[DH:] = jnp.broadcast_to(jnp.sum(product, axis=0, keepdims=True), (GAIN_ROWS, DH))


def partial_body(place_ref, query_ref, key_ref, value_ref, *refs):
    attn_refs, state_refs = refs[:CHAINS], refs[CHAINS : CHAINS + HEADS]
    grad_query_ref, key_part_ref, value_part_ref = refs[-3:]
    keep, kept = causal(), causal(True)
    for at_head, state_ref in enumerate(state_refs):
        chain, mask = at_head // GROUP, ORDER[at_head % GROUP]
        at, here = own_columns(place_ref, mask, chain), own_columns(place_ref, mask)
        query, key, value, grad_attn = query_ref[:, at], key_ref[:, at], value_ref[:, at], attn_refs[chain][:, here]
        turned = jnp.where(kept, dot(key, query, NT), 0.0).astype(jnp.bfloat16)
        grad_scores = jnp.where(keep, dot(grad_attn, value, NT), 0.0).astype(jnp.bfloat16)
        turned_grad = jnp.where(kept, dot(value, grad_attn, NT), 0.0).astype(jnp.bfloat16)
        carried = dot(grad_attn, state_ref[...].astype(jnp.bfloat16), NT)
        grad_query_ref[:, at] = (dot(grad_scores, key, NN) + carried).astype(jnp.bfloat16)
        key_part_ref[:, at] = dot(turned_grad, query, NN)
        value_part_ref[:, at] = dot(turned, grad_attn, NN)


def final_body(place_ref, key_ref, value_ref, key_part_ref, value_part_ref, *refs):
    state_refs, (grad_key_ref, grad_value_ref) = refs[:HEADS], refs[HEADS:]
    rows = pl.ds(pl.multiple_of(pl.program_id(0) * PART_ROWS, PART_ROWS), PART_ROWS)
    for at_head, state_ref in enumerate(state_refs):
        at = own_columns(place_ref, ORDER[at_head % GROUP], at_head // GROUP)
        state = state_ref[:DH].astype(jnp.bfloat16)
        grad_key_ref[:, at] = (key_part_ref[rows, at] + dot(value_ref[rows, at], state, NT)).astype(jnp.bfloat16)
        grad_value_ref[:, at] = (value_part_ref[rows, at] + dot(key_ref[rows, at], state, NN)).astype(jnp.bfloat16)


def gain_body(place_ref, *refs):
    for at_head, state_ref in enumerate(refs[:-1]):
        row = (at_head // GROUP) * GROUP + (place_ref[0] & (GROUP - 1) ^ ORDER[at_head % GROUP])
        refs[-1][pl.ds(row, 1), :] = state_ref[DH : DH + 1]


def prefix_body(reverse, masks, place_ref, *refs):
    (total_ref, *arrived_refs), (*back_refs, ahead) = refs[: -2 * GROUP - 1], refs[-GROUP - 1 :]
    held_refs = refs[-2 * GROUP - 1 : -GROUP - 1]
    for mask, held_ref in zip(ORDER, held_refs):
        ahead[pl.ds(place_ref[0] & (GROUP - 1) ^ mask, 1)] = held_ref[:DH][None]
    running = jnp.zeros((DH, DH), jnp.float32)
    for mask, arrived_ref in zip(masks, arrived_refs):
        later = (place_ref[0] ^ mask < place_ref[0]) != reverse
        running = running + jnp.where(later, arrived_ref[:DH], 0.0)
    for member in reversed(range(GROUP)) if reverse else range(GROUP):
        own = ahead[member]
        ahead[member] = running
        running = running + own
    for mask, back_ref in zip(ORDER, back_refs):
        back_ref[:DH] = ahead[pl.ds(place_ref[0] & (GROUP - 1) ^ mask, 1)][0]
        if back_ref.shape[0] > DH:
            back_ref[DH:] = total_ref[DH:]


def whole(*shape):
    return pl.BlockSpec(shape, lambda step: (0,) * len(shape))


PLACE = pl.BlockSpec(memory_space=pltpu.SMEM)


def call(body, in_specs, out_specs, outs, flops, name, steps=1, scratch=()):
    return pl.pallas_call(
        body,
        grid=(steps,),
        in_specs=[PLACE] + in_specs,
        out_specs=out_specs,
        out_shape=outs,
        scratch_shapes=scratch,
        compiler_params=pltpu.CompilerParams(vmem_limit_bytes=16 * 1024 * 1024),
        cost_estimate=pl.CostEstimate(flops=flops, bytes_accessed=2 << 20, transcendentals=0),
        name=name,
    )


def exchange_steps():
    count, base, steps = lax.axis_size("seq"), GROUP, []
    while base < count:
        masks = [base, 3 * base, 2 * base] if 4 * base <= count else [base]
        steps.append(masks)
        base *= len(masks) + 1
    return steps


def swap(array, mask):
    if mask == 0:
        return array
    return lax.ppermute(array, "seq", [(s, s ^ mask) for s in range(lax.axis_size("seq"))])


def plane_swap(pieces):
    return lax.optimization_barrier([swap(piece, mask) for mask, piece in zip(ORDER, pieces)])


def exchange(held):
    total, arrived = sum(held[1:], held[0]), []
    for masks in exchange_steps():
        arrived += lax.optimization_barrier([swap(total, mask) for mask in masks])
        total = sum(arrived[-len(masks) :], total)
    return total, arrived


def carried_in(held, total, arrived, reverse, place):
    single = whole(*total.shape)
    back = call(
        functools.partial(prefix_body, reverse, sum(exchange_steps(), [])),
        [single] * (1 + len(arrived) + GROUP),
        [single] * GROUP,
        [jax.ShapeDtypeStruct(total.shape, jnp.float32)] * GROUP,
        1 << 24,
        "prefix",
        scratch=[pltpu.VMEM((GROUP, DH, DH), jnp.float32)],
    )(place, total, *arrived, *held)
    return plane_swap(back)


def local(queries, keys, values, out_gain, grad_out):
    full = queries.shape
    flat = (full[0] * full[1], full[2])
    assert flat == (BLOCK, HEADS * DH) and lax.axis_size("seq") % GROUP == 0
    query, key, value, grad = (a.reshape(flat) for a in (queries, keys, values, grad_out))
    gain = out_gain.reshape(1, HEADS * DH)
    square = jax.ShapeDtypeStruct((DH, DH), jnp.float32)
    taller = jax.ShapeDtypeStruct((DH + GAIN_ROWS, DH), jnp.float32)
    full_float = jax.ShapeDtypeStruct(flat, jnp.float32)
    full_low = jax.ShapeDtypeStruct(flat, jnp.bfloat16)
    half_low = jax.ShapeDtypeStruct((BLOCK, WIDE), jnp.bfloat16)
    short, tall, wide, half = whole(*square.shape), whole(*taller.shape), whole(*flat), whole(BLOCK, WIDE)
    unit = 2 * BLOCK * DH * DH * HEADS

    place = lax.axis_index("seq").astype(jnp.int32).reshape(1)
    deltas = call(
        delta_body,
        [pl.BlockSpec(memory_space=pltpu.HBM)] * 2,
        [short] * HEADS,
        [square] * HEADS,
        6 * unit,
        "delta",
        scratch=[pltpu.VMEM(flat, jnp.bfloat16)] * 2 + [pltpu.SemaphoreType.DMA((PARTS, 2))],
    )(place, *[pltpu.with_memory_space_constraint(a, pltpu.HBM) for a in (key, value)])
    chains = [slice(chain * GROUP, (chain + 1) * GROUP) for chain in range(CHAINS)]
    inner_call = call(
        lambda place_ref, *refs: inner_body(*refs), [wide] * 3, wide, full_float, 16 * unit, "inner"
    )
    helds = [plane_swap(deltas[chain]) for chain in chains]
    helds[1], operands = lax.optimization_barrier((helds[1], (place, query, key, value)))
    (total, arrived), *others = [exchange(held) for held in helds]
    arrived, inner = lax.optimization_barrier((arrived, inner_call(*operands)))
    states = [carried_in(*sums, False, place) for sums in zip(helds, *zip((total, arrived), *others))]
    attns, later = [], []
    for chain in range(CHAINS):
        attn, *deltas = call(
            functools.partial(norm_body, chain),
            [wide, wide, wide, whole(1, HEADS * DH)] + [short] * GROUP,
            [half] + [tall] * GROUP,
            [half_low] + [taller] * GROUP,
            8 * unit,
            "norm",
        )(place, query, grad, inner, gain, *states[chain])
        attns.append(attn)
        held = plane_swap(deltas)
        later += carried_in(held, *exchange(held), True, place)
    grad_query, key_part, value_part = call(
        partial_body,
        [wide] * 3 + [half] * CHAINS + [short] * HEADS,
        [wide] * 3,
        [full_low, full_float, full_float],
        48 * unit,
        "partial",
    )(place, query, key, value, *attns, *[state for chain in states for state in chain])
    gain_terms = call(
        gain_body, [tall] * HEADS, whole(HEADS, DH), jax.ShapeDtypeStruct((HEADS, DH), jnp.float32), unit, "gain"
    )(place, *later)
    docs, mask = lax.axis_size("dp"), 1
    while mask < docs:
        gain_terms = gain_terms + lax.ppermute(gain_terms, "dp", [(d, d ^ mask) for d in range(docs)])
        mask *= 2
    chunk = pl.BlockSpec((PART_ROWS, HEADS * DH), lambda step: (step, 0))
    grad_key, grad_value = call(
        final_body, [wide] * 4 + [tall] * HEADS, [chunk] * 2, [full_low] * 2, 16 * unit, "final", steps=PARTS
    )(place, key, value, key_part, value_part, *later)
    grad_gain = gain_terms / math.sqrt(lax.axis_size("seq") * docs * BLOCK)
    return (
        grad_query.reshape(full),
        grad_key.reshape(full),
        grad_value.reshape(full),
        grad_gain.reshape(HEADS * DH),
    )


def solution(mesh):
    sharded = P("dp", "seq", None)
    return jax.shard_map(
        local,
        mesh=mesh,
        in_specs=(sharded, sharded, sharded, P(), sharded),
        out_specs=(sharded, sharded, sharded, P()),
        check_vma=False,
    )
```

```python
import functools
import math

import jax
import jax.numpy as jnp
from jax import lax
from jax.experimental import pallas as pl
from jax.experimental.pallas import tpu as pltpu
from jax.sharding import PartitionSpec as P

HEADS = 8
DH = 128
BLOCK = 256
GROUP = 4
CHAINS = HEADS // GROUP
WIDE = GROUP * DH
GAIN_ROWS = 8
ORDER = (0, 3, 2, 1)
PARTS = 2
PART_ROWS = BLOCK // PARTS
EPSILON = 1e-06

NT = (((1,), (1,)), ((), ()))
TN = (((0,), (0,)), ((), ()))
NN = (((1,), (0,)), ((), ()))


def dot(left, right, dims):
    return lax.dot_general(left, right, dims, preferred_element_type=jnp.float32)


def columns(head):
    return pl.ds(head * DH, DH)


def own_columns(place_ref, mask, chain=0):
    return pl.ds(pl.multiple_of(chain * WIDE + (place_ref[0] & (GROUP - 1) ^ mask) * DH, DH), DH)


def causal(turned=False):
    shape, first = (BLOCK, BLOCK), int(turned)
    return lax.broadcasted_iota(jnp.int32, shape, first) >= lax.broadcasted_iota(jnp.int32, shape, 1 - first)


def delta_body(chain, place_ref, key_ref, value_ref, *refs):
    delta_refs, scratch = refs[:GROUP], refs[GROUP:]
    if scratch:
        copies, *heres, sems = [], *scratch
        for part in range(PARTS):
            rows = pl.ds(part * PART_ROWS, PART_ROWS)
            for side, (source, here) in enumerate(zip((key_ref, value_ref), heres)):
                chunk = source.at[rows, pl.ds(chain * WIDE, WIDE)]
                copies.append(pltpu.make_async_copy(chunk, here.at[rows], sems.at[part, side]))
                copies[-1].start()
        chain, (key_ref, value_ref) = 0, heres
    for part in range(PARTS):
        rows = pl.ds(part * PART_ROWS, PART_ROWS)
        for copy in copies[2 * part : 2 * part + 2] if scratch else ():
            copy.wait()
        for mask, delta_ref in zip(ORDER, delta_refs):
            at = own_columns(place_ref, mask, chain)
            delta = dot(key_ref[rows, at], value_ref[rows, at], TN)
            delta_ref[...] = delta if part == 0 else delta_ref[...] + delta


def inner_body(query_ref, key_ref, value_ref, inner_ref):
    keep = causal()
    for head in range(HEADS):
        at = columns(head)
        scores = jnp.where(keep, dot(query_ref[:, at], key_ref[:, at], NT), 0.0).astype(jnp.bfloat16)
        inner_ref[:, at] = dot(scores, value_ref[:, at], NN)


def norm_body(chain, place_ref, query_ref, grad_ref, inner_ref, gain_ref, *refs):
    state_refs, (attn_ref, *delta_refs) = refs[:GROUP], refs[GROUP:]
    for mask, state_ref, delta_ref in zip(ORDER, state_refs, delta_refs):
        at = own_columns(place_ref, mask, chain)
        query = query_ref[:, at]
        attn = inner_ref[:, at] + dot(query, state_ref[...].astype(jnp.bfloat16), NN)
        per_root = lax.rsqrt(jnp.mean(attn * attn, axis=-1, keepdims=True) + EPSILON)
        normed = attn * per_root
        cotangent = grad_ref[:, at].astype(jnp.float32)
        product = normed * cotangent
        gain = gain_ref[:, at]
        shared = jnp.mean(product * gain, axis=-1, keepdims=True)
        grad_attn = ((gain * cotangent - normed * shared) * per_root).astype(jnp.bfloat16)
        attn_ref[:, own_columns(place_ref, mask)] = grad_attn
        delta_ref[:DH] = dot(query, grad_attn, TN)
        delta_ref[DH:] = jnp.broadcast_to(jnp.sum(product, axis=0, keepdims=True), (GAIN_ROWS, DH))


def partial_body(chain, place_ref, query_ref, key_ref, value_ref, attn_ref, *refs):
    state_refs, (grad_query_ref, key_part_ref, value_part_ref) = refs[:GROUP], refs[-3:]
    keep, kept = causal(), causal(True)
    for mask, state_ref in zip(ORDER, state_refs):
        at, here = own_columns(place_ref, mask, chain), own_columns(place_ref, mask)
        query, key, value, grad_attn = query_ref[:, at], key_ref[:, at], value_ref[:, at], attn_ref[:, here]
        turned = jnp.where(kept, dot(key, query, NT), 0.0).astype(jnp.bfloat16)
        grad_scores = jnp.where(keep, dot(grad_attn, value, NT), 0.0).astype(jnp.bfloat16)
        turned_grad = jnp.where(kept, dot(value, grad_attn, NT), 0.0).astype(jnp.bfloat16)
        carried = dot(grad_attn, state_ref[...].astype(jnp.bfloat16), NT)
        grad_query_ref[:, here] = (dot(grad_scores, key, NN) + carried).astype(jnp.bfloat16)
        key_part_ref[:, here] = dot(turned_grad, query, NN)
        value_part_ref[:, here] = dot(turned, grad_attn, NN)


def final_body(chain, place_ref, key_ref, value_ref, key_part_ref, value_part_ref, *refs):
    state_refs, (grad_key_ref, grad_value_ref) = refs[:GROUP], refs[-2:]
    for mask, state_ref in zip(ORDER, state_refs):
        at, here = own_columns(place_ref, mask, chain), own_columns(place_ref, mask)
        state = state_ref[:DH].astype(jnp.bfloat16)
        grad_key_ref[:, here] = (key_part_ref[:, here] + dot(value_ref[:, at], state, NT)).astype(jnp.bfloat16)
        grad_value_ref[:, here] = (value_part_ref[:, here] + dot(key_ref[:, at], state, NN)).astype(jnp.bfloat16)


def gain_body(place_ref, *refs):
    for at_head, state_ref in enumerate(refs[:-1]):
        row = (at_head // GROUP) * GROUP + (place_ref[0] & (GROUP - 1) ^ ORDER[at_head % GROUP])
        refs[-1][pl.ds(row, 1), :] = state_ref[DH : DH + 1]


def prefix_body(reverse, masks, place_ref, *refs):
    (total_ref, *arrived_refs), (*back_refs, ahead) = refs[: -2 * GROUP - 1], refs[-GROUP - 1 :]
    held_refs = refs[-2 * GROUP - 1 : -GROUP - 1]
    for mask, held_ref in zip(ORDER, held_refs):
        ahead[pl.ds(place_ref[0] & (GROUP - 1) ^ mask, 1)] = held_ref[:DH][None]
    running = jnp.zeros((DH, DH), jnp.float32)
    for mask, arrived_ref in zip(masks, arrived_refs):
        later = (place_ref[0] & mask == 0) == reverse
        running = running + jnp.where(later, arrived_ref[:DH], 0.0)
    for member in reversed(range(GROUP)) if reverse else range(GROUP):
        own = ahead[member]
        ahead[member] = running
        running = running + own
    for mask, back_ref in zip(ORDER, back_refs):
        back_ref[:DH] = ahead[pl.ds(place_ref[0] & (GROUP - 1) ^ mask, 1)][0]
        if back_ref.shape[0] > DH:
            back_ref[DH:] = total_ref[DH:]


def whole(*shape):
    return pl.BlockSpec(shape, lambda step: (0,) * len(shape))


PLACE = pl.BlockSpec(memory_space=pltpu.SMEM)


def call(body, in_specs, out_specs, outs, flops, name, steps=1, scratch=(), aliases=None):
    return pl.pallas_call(
        body,
        grid=(steps,),
        in_specs=[PLACE] + in_specs,
        out_specs=out_specs,
        out_shape=outs,
        scratch_shapes=scratch,
        input_output_aliases=aliases or {},
        compiler_params=pltpu.CompilerParams(vmem_limit_bytes=16 * 1024 * 1024),
        cost_estimate=pl.CostEstimate(flops=flops, bytes_accessed=2 << 20, transcendentals=0),
        name=name,
    )


def exchange_masks():
    masks = [GROUP]
    while masks[-1] * 2 < lax.axis_size("seq"):
        masks.append(masks[-1] * 2)
    return masks if lax.axis_size("seq") > GROUP else []


def swap(array, mask):
    if mask == 0:
        return array
    return lax.ppermute(array, "seq", [(s, s ^ mask) for s in range(lax.axis_size("seq"))])


def plane_swap(pieces):
    return [swap(piece, mask) for mask, piece in zip(ORDER, pieces)]


def beside(function, operands, first, second):
    total = sum(first[1:], first[0])
    total, operands = lax.optimization_barrier((total, operands))
    result = function(*operands)
    second, result = lax.optimization_barrier((second, result))
    return [(first, total), (second, sum(second[1:], second[0]))], result


def carried_in(held, total, reverse, place):
    arrived = []
    for mask in exchange_masks():
        arrived.append(swap(total, mask))
        total = total + arrived[-1]
    single = whole(*total.shape)
    back = call(
        functools.partial(prefix_body, reverse, exchange_masks()),
        [single] * (1 + len(arrived) + GROUP),
        [single] * GROUP,
        [jax.ShapeDtypeStruct(total.shape, jnp.float32)] * GROUP,
        1 << 24,
        "prefix",
        scratch=[pltpu.VMEM((GROUP, DH, DH), jnp.float32)],
    )(place, total, *arrived, *held)
    return plane_swap(back)


def local(queries, keys, values, out_gain, grad_out):
    full = queries.shape
    flat = (full[0] * full[1], full[2])
    assert flat == (BLOCK, HEADS * DH) and lax.axis_size("seq") % GROUP == 0
    query, key, value, grad = (a.reshape(flat) for a in (queries, keys, values, grad_out))
    gain = out_gain.reshape(1, HEADS * DH)
    square = jax.ShapeDtypeStruct((DH, DH), jnp.float32)
    taller = jax.ShapeDtypeStruct((DH + GAIN_ROWS, DH), jnp.float32)
    full_float = jax.ShapeDtypeStruct(flat, jnp.float32)
    full_low = jax.ShapeDtypeStruct(flat, jnp.bfloat16)
    half_float = jax.ShapeDtypeStruct((BLOCK, WIDE), jnp.float32)
    half_low = jax.ShapeDtypeStruct((BLOCK, WIDE), jnp.bfloat16)
    short, tall, wide, half = whole(*square.shape), whole(*taller.shape), whole(*flat), whole(BLOCK, WIDE)
    unit = 2 * BLOCK * DH * DH * HEADS

    place = lax.axis_index("seq").astype(jnp.int32).reshape(1)
    near = [pltpu.with_memory_space_constraint(a, pltpu.HBM) for a in (key, value)]
    deltas = [
        call(
            functools.partial(delta_body, chain),
            [pl.BlockSpec(memory_space=pltpu.HBM) if chain == 0 else wide] * 2,
            [short] * GROUP,
            [square] * GROUP,
            3 * unit,
            "delta",
            scratch=[pltpu.VMEM((BLOCK, WIDE), jnp.bfloat16)] * 2 + [pltpu.SemaphoreType.DMA((PARTS, 2))]
            if chain == 0
            else (),
        )(place, *(near if chain == 0 else (key, value)))
        for chain in range(CHAINS)
    ]
    inner_call = call(
        lambda place_ref, *refs: inner_body(*refs), [wide] * 3, wide, full_float, 16 * unit, "inner"
    )
    sums, inner = beside(inner_call, (place, query, key, value), *[plane_swap(delta) for delta in deltas])
    states = [carried_in(held, total, False, place) for held, total in sums]
    attns, helds = [], []
    for chain in range(CHAINS):
        attn, *deltas = call(
            functools.partial(norm_body, chain),
            [wide, wide, wide, whole(1, HEADS * DH)] + [short] * GROUP,
            [half] + [tall] * GROUP,
            [half_low] + [taller] * GROUP,
            8 * unit,
            "norm",
        )(place, query, grad, inner, gain, *states[chain])
        attns.append(attn)
        helds.append(plane_swap(deltas))

    def partial_call(chain, *operands):
        return call(
            functools.partial(partial_body, chain),
            [wide] * 3 + [half] + [short] * GROUP + [pl.BlockSpec(memory_space=pl.ANY)] * chain,
            [pl.BlockSpec((BLOCK, WIDE), lambda step: (0, chain)), half, half],
            [full_low, half_float, half_float],
            24 * unit,
            "partial",
            aliases={5 + GROUP: 0} if chain else None,
        )(*operands)

    operands = [(place, query, key, value, attns[chain], *states[chain]) for chain in range(CHAINS)]
    sums, (grad_query, *parts) = beside(functools.partial(partial_call, 0), operands[0], *helds)
    later = [carried_in(held, total, True, place) for held, total in sums]
    grad_query, *other_parts = partial_call(1, *operands[1], grad_query)

    def final_call(chain, parts, grads=()):
        return call(
            functools.partial(final_body, chain),
            [wide] * 2 + [half] * 2 + [tall] * GROUP + [pl.BlockSpec(memory_space=pl.ANY)] * len(grads),
            [pl.BlockSpec((BLOCK, WIDE), lambda step: (0, chain))] * 2,
            [full_low] * 2,
            8 * unit,
            "final",
            aliases={5 + GROUP: 0, 6 + GROUP: 1} if grads else None,
        )(place, key, value, *parts, *later[chain], *grads)

    later[1], grads = lax.optimization_barrier((later[1], final_call(0, parts)))
    gain_terms = call(
        gain_body, [tall] * HEADS, whole(HEADS, DH), jax.ShapeDtypeStruct((HEADS, DH), jnp.float32), unit, "gain"
    )(place, *later[0], *later[1])
    docs, mask = lax.axis_size("dp"), 1
    while mask < docs:
        gain_terms = gain_terms + lax.ppermute(gain_terms, "dp", [(d, d ^ mask) for d in range(docs)])
        mask *= 2
    grad_key, grad_value = final_call(1, other_parts, grads)
    grad_gain = gain_terms / math.sqrt(lax.axis_size("seq") * docs * BLOCK)
    return (
        grad_query.reshape(full),
        grad_key.reshape(full),
        grad_value.reshape(full),
        grad_gain.reshape(HEADS * DH),
    )


def solution(mesh):
    sharded = P("dp", "seq", None)
    return jax.shard_map(
        local,
        mesh=mesh,
        in_specs=(sharded, sharded, sharded, P(), sharded),
        out_specs=(sharded, sharded, sharded, P()),
        check_vma=False,
    )
```

```python
import functools
import math

import jax
import jax.numpy as jnp
from jax import lax
from jax.experimental import pallas as pl
from jax.experimental.pallas import tpu as pltpu
from jax.sharding import PartitionSpec as P

HEADS = 8
DH = 128
BLOCK = 256
GROUP = 4
CHAINS = HEADS // GROUP
WIDE = GROUP * DH
GAIN_ROWS = 8
ORDER = (0, 3, 2, 1)
PARTS = 2
PART_ROWS = BLOCK // PARTS
EPSILON = 1e-06

NT = (((1,), (1,)), ((), ()))
TN = (((0,), (0,)), ((), ()))
NN = (((1,), (0,)), ((), ()))


def dot(left, right, dims):
    return lax.dot_general(left, right, dims, preferred_element_type=jnp.float32)


def columns(head):
    return pl.ds(head * DH, DH)


def own_columns(place_ref, mask, chain=0):
    return pl.ds(pl.multiple_of(chain * WIDE + (place_ref[0] & (GROUP - 1) ^ mask) * DH, DH), DH)


def causal(turned=False):
    shape, first = (BLOCK, BLOCK), int(turned)
    return lax.broadcasted_iota(jnp.int32, shape, first) >= lax.broadcasted_iota(jnp.int32, shape, 1 - first)


def delta_body(chain, place_ref, key_ref, value_ref, *refs):
    delta_refs, scratch = refs[:GROUP], refs[GROUP:]
    if scratch:
        copies, *heres, sems = [], *scratch
        for part in range(PARTS):
            rows = pl.ds(part * PART_ROWS, PART_ROWS)
            for side, (source, here) in enumerate(zip((key_ref, value_ref), heres)):
                chunk = source.at[rows, pl.ds(chain * WIDE, WIDE)]
                copies.append(pltpu.make_async_copy(chunk, here.at[rows], sems.at[part, side]))
                copies[-1].start()
        chain, (key_ref, value_ref) = 0, heres
    for part in range(PARTS):
        rows = pl.ds(part * PART_ROWS, PART_ROWS)
        for copy in copies[2 * part : 2 * part + 2] if scratch else ():
            copy.wait()
        for mask, delta_ref in zip(ORDER, delta_refs):
            at = own_columns(place_ref, mask, chain)
            delta = dot(key_ref[rows, at], value_ref[rows, at], TN)
            delta_ref[...] = delta if part == 0 else delta_ref[...] + delta


def inner_body(query_ref, key_ref, value_ref, inner_ref):
    keep = causal()
    for head in range(HEADS):
        at = columns(head)
        scores = jnp.where(keep, dot(query_ref[:, at], key_ref[:, at], NT), 0.0).astype(jnp.bfloat16)
        inner_ref[:, at] = dot(scores, value_ref[:, at], NN)


def norm_body(chain, place_ref, query_ref, grad_ref, inner_ref, gain_ref, *refs):
    state_refs, (attn_ref, *delta_refs) = refs[:GROUP], refs[-GROUP - 1 - (chain == 0) :]
    if chain == 0:
        *delta_refs, terms_ref = delta_refs
    for slot, (mask, state_ref, delta_ref) in enumerate(zip(ORDER, state_refs, delta_refs)):
        at = own_columns(place_ref, mask, chain)
        query = query_ref[:, at]
        attn = inner_ref[:, at] + dot(query, state_ref[...].astype(jnp.bfloat16), NN)
        per_root = lax.rsqrt(jnp.mean(attn * attn, axis=-1, keepdims=True) + EPSILON)
        normed = attn * per_root
        cotangent = grad_ref[:, at].astype(jnp.float32)
        product = normed * cotangent
        gain = gain_ref[:, at]
        shared = jnp.mean(product * gain, axis=-1, keepdims=True)
        grad_attn = ((gain * cotangent - normed * shared) * per_root).astype(jnp.bfloat16)
        attn_ref[:, own_columns(place_ref, mask)] = grad_attn
        delta_ref[:DH] = dot(query, grad_attn, TN)
        terms = jnp.sum(product, axis=0, keepdims=True)
        if chain == 0:
            terms_ref[slot : slot + 1] = terms
        else:
            delta_ref[DH:] = jnp.broadcast_to(terms, (GAIN_ROWS, DH))
            delta_ref[DH + 1 : DH + 2] = refs[GROUP][slot : slot + 1]


def partial_body(chain, place_ref, query_ref, key_ref, value_ref, attn_ref, *refs):
    state_refs, (grad_query_ref, key_part_ref, value_part_ref) = refs[:GROUP], refs[-3:]
    keep, kept = causal(), causal(True)
    for mask, state_ref in zip(ORDER, state_refs):
        at, here = own_columns(place_ref, mask, chain), own_columns(place_ref, mask)
        query, key, value, grad_attn = query_ref[:, at], key_ref[:, at], value_ref[:, at], attn_ref[:, here]
        turned = jnp.where(kept, dot(key, query, NT), 0.0).astype(jnp.bfloat16)
        grad_scores = jnp.where(keep, dot(grad_attn, value, NT), 0.0).astype(jnp.bfloat16)
        turned_grad = jnp.where(kept, dot(value, grad_attn, NT), 0.0).astype(jnp.bfloat16)
        carried = dot(grad_attn, state_ref[...].astype(jnp.bfloat16), NT)
        grad_query_ref[:, here] = (dot(grad_scores, key, NN) + carried).astype(jnp.bfloat16)
        key_part_ref[:, here] = dot(turned_grad, query, NN)
        value_part_ref[:, here] = dot(turned, grad_attn, NN)


def final_body(chain, place_ref, key_ref, value_ref, key_part_ref, value_part_ref, *refs):
    state_refs, (grad_key_ref, grad_value_ref) = refs[:GROUP], refs[-2:]
    for mask, state_ref in zip(ORDER, state_refs):
        at, here = own_columns(place_ref, mask, chain), own_columns(place_ref, mask)
        state = state_ref[:DH].astype(jnp.bfloat16)
        grad_key_ref[:, here] = (key_part_ref[:, here] + dot(value_ref[:, at], state, NT)).astype(jnp.bfloat16)
        grad_value_ref[:, here] = (value_part_ref[:, here] + dot(key_ref[:, at], state, NN)).astype(jnp.bfloat16)


def gain_body(place_ref, *refs):
    for mask, state_ref in zip(ORDER, refs[:-1]):
        member = place_ref[0] & (GROUP - 1) ^ mask
        for chain in range(CHAINS):
            row = DH + CHAINS - 1 - chain
            refs[-1][pl.ds(chain * GROUP + member, 1), :] = state_ref[row : row + 1]


def prefix_body(reverse, masks, place_ref, *refs):
    (total_ref, *arrived_refs), (*back_refs, ahead) = refs[: -2 * GROUP - 1], refs[-GROUP - 1 :]
    held_refs = refs[-2 * GROUP - 1 : -GROUP - 1]
    for mask, held_ref in zip(ORDER, held_refs):
        ahead[pl.ds(place_ref[0] & (GROUP - 1) ^ mask, 1)] = held_ref[:DH][None]
    running = jnp.zeros((DH, DH), jnp.float32)
    for mask, arrived_ref in zip(masks, arrived_refs):
        later = (place_ref[0] & mask == 0) == reverse
        running = running + jnp.where(later, arrived_ref[:DH], 0.0)
    for member in reversed(range(GROUP)) if reverse else range(GROUP):
        own = ahead[member]
        ahead[member] = running
        running = running + own
    for mask, back_ref in zip(ORDER, back_refs):
        back_ref[:DH] = ahead[pl.ds(place_ref[0] & (GROUP - 1) ^ mask, 1)][0]
        if back_ref.shape[0] > DH:
            back_ref[DH:] = total_ref[DH:]


def whole(*shape):
    return pl.BlockSpec(shape, lambda step: (0,) * len(shape))


PLACE = pl.BlockSpec(memory_space=pltpu.SMEM)


def call(body, in_specs, out_specs, outs, flops, name, steps=1, scratch=(), aliases=None):
    return pl.pallas_call(
        body,
        grid=(steps,),
        in_specs=[PLACE] + in_specs,
        out_specs=out_specs,
        out_shape=outs,
        scratch_shapes=scratch,
        input_output_aliases=aliases or {},
        compiler_params=pltpu.CompilerParams(vmem_limit_bytes=16 * 1024 * 1024),
        cost_estimate=pl.CostEstimate(flops=flops, bytes_accessed=2 << 20, transcendentals=0),
        name=name,
    )


def exchange_masks():
    masks = [GROUP]
    while masks[-1] * 2 < lax.axis_size("seq"):
        masks.append(masks[-1] * 2)
    return masks if lax.axis_size("seq") > GROUP else []


def swap(array, mask):
    if mask == 0:
        return array
    return lax.ppermute(array, "seq", [(s, s ^ mask) for s in range(lax.axis_size("seq"))])


def plane_swap(pieces):
    return [swap(piece, mask) for mask, piece in zip(ORDER, pieces)]


def beside(function, operands, first, second):
    total = sum(first[1:], first[0])
    total, operands = lax.optimization_barrier((total, operands))
    result = function(*operands)
    second, result = lax.optimization_barrier((second, result))
    return [(first, total), (second, sum(second[1:], second[0]))], result


def carried_in(held, total, reverse, place):
    arrived = []
    for mask in exchange_masks():
        arrived.append(swap(total, mask))
        total = total + arrived[-1]
    single = whole(*total.shape)
    back = call(
        functools.partial(prefix_body, reverse, exchange_masks()),
        [single] * (1 + len(arrived) + GROUP),
        [single] * GROUP,
        [jax.ShapeDtypeStruct(total.shape, jnp.float32)] * GROUP,
        1 << 24,
        "prefix",
        scratch=[pltpu.VMEM((GROUP, DH, DH), jnp.float32)],
    )(place, total, *arrived, *held)
    return plane_swap(back)


def local(queries, keys, values, out_gain, grad_out):
    full = queries.shape
    flat = (full[0] * full[1], full[2])
    assert flat == (BLOCK, HEADS * DH) and lax.axis_size("seq") % GROUP == 0
    query, key, value, grad = (a.reshape(flat) for a in (queries, keys, values, grad_out))
    gain = out_gain.reshape(1, HEADS * DH)
    square = jax.ShapeDtypeStruct((DH, DH), jnp.float32)
    taller = jax.ShapeDtypeStruct((DH + GAIN_ROWS, DH), jnp.float32)
    full_float = jax.ShapeDtypeStruct(flat, jnp.float32)
    full_low = jax.ShapeDtypeStruct(flat, jnp.bfloat16)
    half_float = jax.ShapeDtypeStruct((BLOCK, WIDE), jnp.float32)
    half_low = jax.ShapeDtypeStruct((BLOCK, WIDE), jnp.bfloat16)
    short, tall, wide, half = whole(*square.shape), whole(*taller.shape), whole(*flat), whole(BLOCK, WIDE)
    unit = 2 * BLOCK * DH * DH * HEADS

    place = lax.axis_index("seq").astype(jnp.int32).reshape(1)
    near = [pltpu.with_memory_space_constraint(a, pltpu.HBM) for a in (key, value)]
    deltas = [
        call(
            functools.partial(delta_body, chain),
            [pl.BlockSpec(memory_space=pltpu.HBM) if chain == 0 else wide] * 2,
            [short] * GROUP,
            [square] * GROUP,
            3 * unit,
            "delta",
            scratch=[pltpu.VMEM((BLOCK, WIDE), jnp.bfloat16)] * 2 + [pltpu.SemaphoreType.DMA((PARTS, 2))]
            if chain == 0
            else (),
        )(place, *(near if chain == 0 else (key, value)))
        for chain in range(CHAINS)
    ]
    inner_call = call(
        lambda place_ref, *refs: inner_body(*refs), [wide] * 3, wide, full_float, 16 * unit, "inner"
    )
    sums, inner = beside(inner_call, (place, query, key, value), *[plane_swap(delta) for delta in deltas])
    states = [carried_in(held, total, False, place) for held, total in sums]
    attns, helds, terms = [], [], ()
    for chain in range(CHAINS):
        size, spec = (square, short) if chain == 0 else (taller, tall)
        extra = [] if chain else [jax.ShapeDtypeStruct((GROUP, DH), jnp.float32)]
        attn, *deltas = call(
            functools.partial(norm_body, chain),
            [wide, wide, wide, whole(1, HEADS * DH)] + [short] * GROUP + [whole(GROUP, DH)] * chain,
            [half] + [spec] * GROUP + [whole(*one.shape) for one in extra],
            [half_low] + [size] * GROUP + extra,
            8 * unit,
            "norm",
        )(place, query, grad, inner, gain, *states[chain], *terms)
        attns.append(attn)
        helds.append(plane_swap(deltas[:GROUP]))
        terms = deltas[GROUP:]

    def partial_call(chain, *operands):
        return call(
            functools.partial(partial_body, chain),
            [wide] * 3 + [half] + [short] * GROUP + [pl.BlockSpec(memory_space=pl.ANY)] * chain,
            [pl.BlockSpec((BLOCK, WIDE), lambda step: (0, chain)), half, half],
            [full_low, half_float, half_float],
            24 * unit,
            "partial",
            aliases={5 + GROUP: 0} if chain else None,
        )(*operands)

    operands = [(place, query, key, value, attns[chain], *states[chain]) for chain in range(CHAINS)]
    sums, (grad_query, *parts) = beside(functools.partial(partial_call, 0), operands[0], *helds)
    later = [carried_in(held, total, True, place) for held, total in sums]
    grad_query, *other_parts = partial_call(1, *operands[1], grad_query)

    def final_call(chain, parts, grads=()):
        return call(
            functools.partial(final_body, chain),
            [wide] * 2 + [half] * 2 + [tall if chain else short] * GROUP + [pl.BlockSpec(memory_space=pl.ANY)] * len(grads),
            [pl.BlockSpec((BLOCK, WIDE), lambda step: (0, chain))] * 2,
            [full_low] * 2,
            8 * unit,
            "final",
            aliases={5 + GROUP: 0, 6 + GROUP: 1} if grads else None,
        )(place, key, value, *parts, *later[chain], *grads)

    later[1], grads = lax.optimization_barrier((later[1], final_call(0, parts)))
    gain_terms = call(
        gain_body, [tall] * GROUP, whole(HEADS, DH), jax.ShapeDtypeStruct((HEADS, DH), jnp.float32), unit, "gain"
    )(place, *later[1])
    docs, mask = lax.axis_size("dp"), 1
    while mask < docs:
        gain_terms = gain_terms + lax.ppermute(gain_terms, "dp", [(d, d ^ mask) for d in range(docs)])
        mask *= 2
    grad_key, grad_value = final_call(1, other_parts, grads)
    grad_gain = gain_terms / math.sqrt(lax.axis_size("seq") * docs * BLOCK)
    return (
        grad_query.reshape(full),
        grad_key.reshape(full),
        grad_value.reshape(full),
        grad_gain.reshape(HEADS * DH),
    )


def solution(mesh):
    sharded = P("dp", "seq", None)
    return jax.shard_map(
        local,
        mesh=mesh,
        in_specs=(sharded, sharded, sharded, P(), sharded),
        out_specs=(sharded, sharded, sharded, P()),
        check_vma=False,
    )
```

```python
import functools
import math

import jax
import jax.numpy as jnp
from jax import lax
from jax.experimental import pallas as pl
from jax.experimental.pallas import tpu as pltpu
from jax.sharding import PartitionSpec as P

HEADS = 8
DH = 128
BLOCK = 256
GROUP = 4
CHAINS = HEADS // GROUP
WIDE = GROUP * DH
GAIN_ROWS = 8
ORDER = (0, 3, 2, 1)
PARTS = 2
PART_ROWS = BLOCK // PARTS
EPSILON = 1e-06

NT = (((1,), (1,)), ((), ()))
TN = (((0,), (0,)), ((), ()))
NN = (((1,), (0,)), ((), ()))


def dot(left, right, dims):
    return lax.dot_general(left, right, dims, preferred_element_type=jnp.float32)


def columns(head):
    return pl.ds(head * DH, DH)


def own_columns(place_ref, mask, chain=0):
    return pl.ds(pl.multiple_of(chain * WIDE + (place_ref[0] & (GROUP - 1) ^ mask) * DH, DH), DH)


def causal(turned=False):
    shape, first = (BLOCK, BLOCK), int(turned)
    return lax.broadcasted_iota(jnp.int32, shape, first) >= lax.broadcasted_iota(jnp.int32, shape, 1 - first)


def delta_body(place_ref, key_ref, value_ref, *refs):
    delta_refs, (key_here, value_here, sems) = refs[:HEADS], refs[HEADS:]
    copies = []
    for part in range(PARTS):
        rows = pl.ds(part * PART_ROWS, PART_ROWS)
        for side, (source, here) in enumerate(((key_ref, key_here), (value_ref, value_here))):
            copies.append(pltpu.make_async_copy(source.at[rows], here.at[rows], sems.at[part, side]))
            copies[-1].start()
    for part in range(PARTS):
        rows = pl.ds(part * PART_ROWS, PART_ROWS)
        for copy in copies[2 * part : 2 * part + 2]:
            copy.wait()
        for at_head, delta_ref in enumerate(delta_refs):
            at = own_columns(place_ref, ORDER[at_head % GROUP], at_head // GROUP)
            delta = dot(key_here[rows, at], value_here[rows, at], TN)
            delta_ref[...] = delta if part == 0 else delta_ref[...] + delta


def inner_body(query_ref, key_ref, value_ref, inner_ref):
    keep = causal()
    for head in range(HEADS):
        at = columns(head)
        scores = jnp.where(keep, dot(query_ref[:, at], key_ref[:, at], NT), 0.0).astype(jnp.bfloat16)
        inner_ref[:, at] = dot(scores, value_ref[:, at], NN)


def norm_body(chain, place_ref, query_ref, grad_ref, inner_ref, gain_ref, *refs):
    state_refs, (attn_ref, *delta_refs) = refs[:GROUP], refs[GROUP:]
    for mask, state_ref, delta_ref in zip(ORDER, state_refs, delta_refs):
        at = own_columns(place_ref, mask, chain)
        query = query_ref[:, at]
        attn = inner_ref[:, at] + dot(query, state_ref[...].astype(jnp.bfloat16), NN)
        per_root = lax.rsqrt(jnp.mean(attn * attn, axis=-1, keepdims=True) + EPSILON)
        normed = attn * per_root
        cotangent = grad_ref[:, at].astype(jnp.float32)
        product = normed * cotangent
        gain = gain_ref[:, at]
        shared = jnp.mean(product * gain, axis=-1, keepdims=True)
        grad_attn = ((gain * cotangent - normed * shared) * per_root).astype(jnp.bfloat16)
        attn_ref[:, own_columns(place_ref, mask)] = grad_attn
        delta_ref[:DH] = dot(query, grad_attn, TN)
        delta_ref[DH:] = jnp.broadcast_to(jnp.sum(product, axis=0, keepdims=True), (GAIN_ROWS, DH))


def partial_body(place_ref, query_ref, key_ref, value_ref, *refs):
    attn_refs, state_refs = refs[:CHAINS], refs[CHAINS : CHAINS + HEADS]
    grad_query_ref, key_part_ref, value_part_ref = refs[-3:]
    keep, kept = causal(), causal(True)
    for at_head, state_ref in enumerate(state_refs):
        chain, mask = at_head // GROUP, ORDER[at_head % GROUP]
        at, here = own_columns(place_ref, mask, chain), own_columns(place_ref, mask)
        query, key, value, grad_attn = query_ref[:, at], key_ref[:, at], value_ref[:, at], attn_refs[chain][:, here]
        turned = jnp.where(kept, dot(key, query, NT), 0.0).astype(jnp.bfloat16)
        grad_scores = jnp.where(keep, dot(grad_attn, value, NT), 0.0).astype(jnp.bfloat16)
        turned_grad = jnp.where(kept, dot(value, grad_attn, NT), 0.0).astype(jnp.bfloat16)
        carried = dot(grad_attn, state_ref[...].astype(jnp.bfloat16), NT)
        grad_query_ref[:, at] = (dot(grad_scores, key, NN) + carried).astype(jnp.bfloat16)
        key_part_ref[:, at] = dot(turned_grad, query, NN)
        value_part_ref[:, at] = dot(turned, grad_attn, NN)


def final_body(place_ref, key_ref, value_ref, key_part_ref, value_part_ref, *refs):
    state_refs, (grad_key_ref, grad_value_ref) = refs[:HEADS], refs[HEADS:]
    rows = pl.ds(pl.multiple_of(pl.program_id(0) * PART_ROWS, PART_ROWS), PART_ROWS)
    for at_head, state_ref in enumerate(state_refs):
        at = own_columns(place_ref, ORDER[at_head % GROUP], at_head // GROUP)
        state = state_ref[:DH].astype(jnp.bfloat16)
        grad_key_ref[:, at] = (key_part_ref[rows, at] + dot(value_ref[rows, at], state, NT)).astype(jnp.bfloat16)
        grad_value_ref[:, at] = (value_part_ref[rows, at] + dot(key_ref[rows, at], state, NN)).astype(jnp.bfloat16)


def gain_body(place_ref, *refs):
    for at_head, state_ref in enumerate(refs[:-1]):
        row = (at_head // GROUP) * GROUP + (place_ref[0] & (GROUP - 1) ^ ORDER[at_head % GROUP])
        refs[-1][pl.ds(row, 1), :] = state_ref[DH : DH + 1]


def prefix_body(reverse, masks, place_ref, *refs):
    (total_ref, *arrived_refs), (*back_refs, ahead) = refs[: -2 * GROUP - 1], refs[-GROUP - 1 :]
    held_refs = refs[-2 * GROUP - 1 : -GROUP - 1]
    for mask, held_ref in zip(ORDER, held_refs):
        ahead[pl.ds(place_ref[0] & (GROUP - 1) ^ mask, 1)] = held_ref[:DH][None]
    running = jnp.zeros((DH, DH), jnp.float32)
    for mask, arrived_ref in zip(masks, arrived_refs):
        later = (place_ref[0] ^ mask < place_ref[0]) != reverse
        running = running + jnp.where(later, arrived_ref[:DH], 0.0)
    for member in reversed(range(GROUP)) if reverse else range(GROUP):
        own = ahead[member]
        ahead[member] = running
        running = running + own
    for mask, back_ref in zip(ORDER, back_refs):
        back_ref[:DH] = ahead[pl.ds(place_ref[0] & (GROUP - 1) ^ mask, 1)][0]
        if back_ref.shape[0] > DH:
            back_ref[DH:] = total_ref[DH:]


def whole(*shape):
    return pl.BlockSpec(shape, lambda step: (0,) * len(shape))


PLACE = pl.BlockSpec(memory_space=pltpu.SMEM)


def call(body, in_specs, out_specs, outs, flops, name, steps=1, scratch=()):
    return pl.pallas_call(
        body,
        grid=(steps,),
        in_specs=[PLACE] + in_specs,
        out_specs=out_specs,
        out_shape=outs,
        scratch_shapes=scratch,
        compiler_params=pltpu.CompilerParams(vmem_limit_bytes=16 * 1024 * 1024),
        cost_estimate=pl.CostEstimate(flops=flops, bytes_accessed=2 << 20, transcendentals=0),
        name=name,
    )


def exchange_steps(direct):
    count, base, steps = lax.axis_size("seq"), GROUP, []
    while base < count:
        masks = [base, 3 * base, 2 * base] if direct and 4 * base <= count else [base]
        steps.append(masks)
        base *= len(masks) + 1
    return steps


def swap(array, mask):
    if mask == 0:
        return array
    return lax.ppermute(array, "seq", [(s, s ^ mask) for s in range(lax.axis_size("seq"))])


def plane_swap(pieces):
    return [swap(piece, mask) for mask, piece in zip(ORDER, pieces)]


def plane_sum(held):
    return sum(held[1:], held[0])


def carried_in(held, reverse, place, beside=None, operands=()):
    total, arrived, steps, result = plane_sum(held), [], exchange_steps(reverse), None
    for masks in steps:
        if beside and masks == steps[-1]:
            total, operands = lax.optimization_barrier((total, operands))
            result = beside(*operands)
        got = [swap(total, mask) for mask in masks]
        if result is not None:
            got, result = lax.optimization_barrier((got, result))
        elif len(masks) > 1:
            got = lax.optimization_barrier(got)
        arrived += got
        total = sum(got, total)
    single = whole(*total.shape)
    back = call(
        functools.partial(prefix_body, reverse, sum(steps, [])),
        [single] * (1 + len(arrived) + GROUP),
        [single] * GROUP,
        [jax.ShapeDtypeStruct(total.shape, jnp.float32)] * GROUP,
        1 << 24,
        "prefix",
        scratch=[pltpu.VMEM((GROUP, DH, DH), jnp.float32)],
    )(place, total, *arrived, *held)
    return plane_swap(back), result


def local(queries, keys, values, out_gain, grad_out):
    full = queries.shape
    flat = (full[0] * full[1], full[2])
    assert flat == (BLOCK, HEADS * DH) and lax.axis_size("seq") % GROUP == 0
    query, key, value, grad = (a.reshape(flat) for a in (queries, keys, values, grad_out))
    gain = out_gain.reshape(1, HEADS * DH)
    square = jax.ShapeDtypeStruct((DH, DH), jnp.float32)
    taller = jax.ShapeDtypeStruct((DH + GAIN_ROWS, DH), jnp.float32)
    full_float = jax.ShapeDtypeStruct(flat, jnp.float32)
    full_low = jax.ShapeDtypeStruct(flat, jnp.bfloat16)
    half_low = jax.ShapeDtypeStruct((BLOCK, WIDE), jnp.bfloat16)
    short, tall, wide, half = whole(*square.shape), whole(*taller.shape), whole(*flat), whole(BLOCK, WIDE)
    unit = 2 * BLOCK * DH * DH * HEADS

    place = lax.axis_index("seq").astype(jnp.int32).reshape(1)
    deltas = call(
        delta_body,
        [pl.BlockSpec(memory_space=pltpu.HBM)] * 2,
        [short] * HEADS,
        [square] * HEADS,
        6 * unit,
        "delta",
        scratch=[pltpu.VMEM(flat, jnp.bfloat16)] * 2 + [pltpu.SemaphoreType.DMA((PARTS, 2))],
    )(place, *[pltpu.with_memory_space_constraint(a, pltpu.HBM) for a in (key, value)])
    chains = [slice(chain * GROUP, (chain + 1) * GROUP) for chain in range(CHAINS)]
    inner_call = call(
        lambda place_ref, *refs: inner_body(*refs), [wide] * 3, wide, full_float, 16 * unit, "inner"
    )
    first, second = [lax.optimization_barrier(plane_swap(deltas[chain])) for chain in chains]
    state, inner = carried_in(first, False, place, inner_call, (place, query, key, value))
    states = [state, carried_in(second, False, place)[0]]
    attns, later = [], []
    for chain in range(CHAINS):
        attn, *deltas = call(
            functools.partial(norm_body, chain),
            [wide, wide, wide, whole(1, HEADS * DH)] + [short] * GROUP,
            [half] + [tall] * GROUP,
            [half_low] + [taller] * GROUP,
            8 * unit,
            "norm",
        )(place, query, grad, inner, gain, *states[chain])
        attns.append(attn)
        held = lax.optimization_barrier(plane_swap(deltas))
        later += carried_in(held, True, place)[0]
    grad_query, key_part, value_part = call(
        partial_body,
        [wide] * 3 + [half] * CHAINS + [short] * HEADS,
        [wide] * 3,
        [full_low, full_float, full_float],
        48 * unit,
        "partial",
    )(place, query, key, value, *attns, *[state for chain in states for state in chain])
    gain_terms = call(
        gain_body, [tall] * HEADS, whole(HEADS, DH), jax.ShapeDtypeStruct((HEADS, DH), jnp.float32), unit, "gain"
    )(place, *later)
    docs, mask = lax.axis_size("dp"), 1
    while mask < docs:
        gain_terms = gain_terms + lax.ppermute(gain_terms, "dp", [(d, d ^ mask) for d in range(docs)])
        mask *= 2
    chunk = pl.BlockSpec((PART_ROWS, HEADS * DH), lambda step: (step, 0))
    grad_key, grad_value = call(
        final_body, [wide] * 4 + [tall] * HEADS, [chunk] * 2, [full_low] * 2, 16 * unit, "final", steps=PARTS
    )(place, key, value, key_part, value_part, *later)
    grad_gain = gain_terms / math.sqrt(lax.axis_size("seq") * docs * BLOCK)
    return (
        grad_query.reshape(full),
        grad_key.reshape(full),
        grad_value.reshape(full),
        grad_gain.reshape(HEADS * DH),
    )


def solution(mesh):
    sharded = P("dp", "seq", None)
    return jax.shard_map(
        local,
        mesh=mesh,
        in_specs=(sharded, sharded, sharded, P(), sharded),
        out_specs=(sharded, sharded, sharded, P()),
        check_vma=False,
    )
```

```python
import functools
import math

import jax
import jax.numpy as jnp
from jax import lax
from jax.experimental import pallas as pl
from jax.experimental.pallas import tpu as pltpu
from jax.sharding import PartitionSpec as P

HEADS = 8
DH = 128
BLOCK = 256
GROUP = 4
CHAINS = HEADS // GROUP
WIDE = GROUP * DH
GAIN_ROWS = 8
ORDER = (0, 3, 2, 1)
PARTS = 2
PART_ROWS = BLOCK // PARTS
EPSILON = 1e-06

NT = (((1,), (1,)), ((), ()))
TN = (((0,), (0,)), ((), ()))
NN = (((1,), (0,)), ((), ()))


def dot(left, right, dims):
    return lax.dot_general(left, right, dims, preferred_element_type=jnp.float32)


def columns(head):
    return pl.ds(head * DH, DH)


def own_columns(place_ref, mask, chain=0):
    return pl.ds(pl.multiple_of(chain * WIDE + (place_ref[0] & (GROUP - 1) ^ mask) * DH, DH), DH)


def causal(turned=False):
    shape, first = (BLOCK, BLOCK), int(turned)
    return lax.broadcasted_iota(jnp.int32, shape, first) >= lax.broadcasted_iota(jnp.int32, shape, 1 - first)


def delta_body(place_ref, key_ref, value_ref, *refs):
    delta_refs, (key_here, value_here, sems) = refs[:HEADS], refs[HEADS:]
    copies = []
    for part in range(PARTS):
        rows = pl.ds(part * PART_ROWS, PART_ROWS)
        for side, (source, here) in enumerate(((key_ref, key_here), (value_ref, value_here))):
            copies.append(pltpu.make_async_copy(source.at[rows], here.at[rows], sems.at[part, side]))
            copies[-1].start()
    for part in range(PARTS):
        rows = pl.ds(part * PART_ROWS, PART_ROWS)
        for copy in copies[2 * part : 2 * part + 2]:
            copy.wait()
        for at_head, delta_ref in enumerate(delta_refs):
            at = own_columns(place_ref, ORDER[at_head % GROUP], at_head // GROUP)
            delta = dot(key_here[rows, at], value_here[rows, at], TN)
            delta_ref[...] = delta if part == 0 else delta_ref[...] + delta


def inner_body(query_ref, key_ref, value_ref, inner_ref):
    keep = causal()
    for head in range(HEADS):
        at = columns(head)
        scores = jnp.where(keep, dot(query_ref[:, at], key_ref[:, at], NT), 0.0).astype(jnp.bfloat16)
        inner_ref[:, at] = dot(scores, value_ref[:, at], NN)


def norm_body(chain, place_ref, query_ref, grad_ref, inner_ref, gain_ref, *refs):
    state_refs, (attn_ref, *delta_refs) = refs[:GROUP], refs[-GROUP - 1 - (chain == 0) :]
    if chain == 0:
        *delta_refs, terms_ref = delta_refs
    for slot, (mask, state_ref, delta_ref) in enumerate(zip(ORDER, state_refs, delta_refs)):
        at = own_columns(place_ref, mask, chain)
        query = query_ref[:, at]
        attn = inner_ref[:, at] + dot(query, state_ref[...].astype(jnp.bfloat16), NN)
        per_root = lax.rsqrt(jnp.mean(attn * attn, axis=-1, keepdims=True) + EPSILON)
        normed = attn * per_root
        cotangent = grad_ref[:, at].astype(jnp.float32)
        product = normed * cotangent
        gain = gain_ref[:, at]
        shared = jnp.mean(product * gain, axis=-1, keepdims=True)
        grad_attn = ((gain * cotangent - normed * shared) * per_root).astype(jnp.bfloat16)
        attn_ref[:, own_columns(place_ref, mask)] = grad_attn
        delta_ref[:DH] = dot(query, grad_attn, TN)
        terms = jnp.sum(product, axis=0, keepdims=True)
        if chain == 0:
            terms_ref[slot : slot + 1] = terms
        else:
            delta_ref[DH:] = jnp.broadcast_to(terms, (GAIN_ROWS, DH))
            delta_ref[DH + 1 : DH + 2] = refs[GROUP][slot : slot + 1]


def partial_body(place_ref, query_ref, key_ref, value_ref, *refs):
    attn_refs, state_refs = refs[:CHAINS], refs[CHAINS : CHAINS + HEADS]
    grad_query_ref, key_part_ref, value_part_ref = refs[-3:]
    keep, kept = causal(), causal(True)
    for at_head, state_ref in enumerate(state_refs):
        chain, mask = at_head // GROUP, ORDER[at_head % GROUP]
        at, here = own_columns(place_ref, mask, chain), own_columns(place_ref, mask)
        query, key, value, grad_attn = query_ref[:, at], key_ref[:, at], value_ref[:, at], attn_refs[chain][:, here]
        turned = jnp.where(kept, dot(key, query, NT), 0.0).astype(jnp.bfloat16)
        grad_scores = jnp.where(keep, dot(grad_attn, value, NT), 0.0).astype(jnp.bfloat16)
        turned_grad = jnp.where(kept, dot(value, grad_attn, NT), 0.0).astype(jnp.bfloat16)
        carried = dot(grad_attn, state_ref[...].astype(jnp.bfloat16), NT)
        grad_query_ref[:, at] = (dot(grad_scores, key, NN) + carried).astype(jnp.bfloat16)
        key_part_ref[:, at] = dot(turned_grad, query, NN)
        value_part_ref[:, at] = dot(turned, grad_attn, NN)


def final_body(place_ref, key_ref, value_ref, key_part_ref, value_part_ref, *refs):
    state_refs, (grad_key_ref, grad_value_ref) = refs[:HEADS], refs[HEADS:]
    rows = pl.ds(pl.multiple_of(pl.program_id(0) * PART_ROWS, PART_ROWS), PART_ROWS)
    for at_head, state_ref in enumerate(state_refs):
        at = own_columns(place_ref, ORDER[at_head % GROUP], at_head // GROUP)
        state = state_ref[:DH].astype(jnp.bfloat16)
        grad_key_ref[:, at] = (key_part_ref[rows, at] + dot(value_ref[rows, at], state, NT)).astype(jnp.bfloat16)
        grad_value_ref[:, at] = (value_part_ref[rows, at] + dot(key_ref[rows, at], state, NN)).astype(jnp.bfloat16)


def gain_body(place_ref, *refs):
    for mask, state_ref in zip(ORDER, refs[GROUP:-1]):
        member = place_ref[0] & (GROUP - 1) ^ mask
        for chain in range(CHAINS):
            row = DH + CHAINS - 1 - chain
            refs[-1][pl.ds(chain * GROUP + member, 1), :] = state_ref[row : row + 1]


def prefix_body(reverse, masks, place_ref, *refs):
    (total_ref, *arrived_refs), (*back_refs, ahead) = refs[: -2 * GROUP - 1], refs[-GROUP - 1 :]
    held_refs = refs[-2 * GROUP - 1 : -GROUP - 1]
    for mask, held_ref in zip(ORDER, held_refs):
        ahead[pl.ds(place_ref[0] & (GROUP - 1) ^ mask, 1)] = held_ref[:DH][None]
    running = jnp.zeros((DH, DH), jnp.float32)
    for mask, arrived_ref in zip(masks, arrived_refs):
        later = (place_ref[0] ^ mask < place_ref[0]) != reverse
        running = running + jnp.where(later, arrived_ref[:DH], 0.0)
    for member in reversed(range(GROUP)) if reverse else range(GROUP):
        own = ahead[member]
        ahead[member] = running
        running = running + own
    for mask, back_ref in zip(ORDER, back_refs):
        back_ref[:DH] = ahead[pl.ds(place_ref[0] & (GROUP - 1) ^ mask, 1)][0]
        if back_ref.shape[0] > DH:
            back_ref[DH:] = total_ref[DH:]


def whole(*shape):
    return pl.BlockSpec(shape, lambda step: (0,) * len(shape))


PLACE = pl.BlockSpec(memory_space=pltpu.SMEM)


def call(body, in_specs, out_specs, outs, flops, name, steps=1, scratch=()):
    return pl.pallas_call(
        body,
        grid=(steps,),
        in_specs=[PLACE] + in_specs,
        out_specs=out_specs,
        out_shape=outs,
        scratch_shapes=scratch,
        compiler_params=pltpu.CompilerParams(vmem_limit_bytes=16 * 1024 * 1024),
        cost_estimate=pl.CostEstimate(flops=flops, bytes_accessed=2 << 20, transcendentals=0),
        name=name,
    )


def exchange_steps(direct):
    count, base, steps = lax.axis_size("seq"), GROUP, []
    while base < count:
        masks = [base, 3 * base, 2 * base] if direct and 4 * base <= count else [base]
        steps.append(masks)
        base *= len(masks) + 1
    return steps


def swap(array, mask):
    if mask == 0:
        return array
    return lax.ppermute(array, "seq", [(s, s ^ mask) for s in range(lax.axis_size("seq"))])


def plane_swap(pieces):
    return [swap(piece, mask) for mask, piece in zip(ORDER, pieces)]


def plane_sum(held):
    return sum(held[1:], held[0])


def carried_in(held, reverse, place, beside=None, operands=()):
    total, arrived, steps, result = plane_sum(held), [], exchange_steps(reverse), None
    for masks in steps:
        if beside and masks == steps[-1]:
            total, operands = lax.optimization_barrier((total, operands))
            result = beside(*operands)
        got = [swap(total, mask) for mask in masks]
        if result is not None:
            got, result = lax.optimization_barrier((got, result))
        elif len(masks) > 1:
            got = lax.optimization_barrier(got)
        arrived += got
        total = sum(got, total)
    single = whole(*total.shape)
    back = call(
        functools.partial(prefix_body, reverse, sum(steps, [])),
        [single] * (1 + len(arrived) + GROUP),
        [single] * GROUP,
        [jax.ShapeDtypeStruct(total.shape, jnp.float32)] * GROUP,
        1 << 24,
        "prefix",
        scratch=[pltpu.VMEM((GROUP, DH, DH), jnp.float32)],
    )(place, total, *arrived, *held)
    return plane_swap(back), result


def local(queries, keys, values, out_gain, grad_out):
    full = queries.shape
    flat = (full[0] * full[1], full[2])
    assert flat == (BLOCK, HEADS * DH) and lax.axis_size("seq") % GROUP == 0
    query, key, value, grad = (a.reshape(flat) for a in (queries, keys, values, grad_out))
    gain = out_gain.reshape(1, HEADS * DH)
    square = jax.ShapeDtypeStruct((DH, DH), jnp.float32)
    taller = jax.ShapeDtypeStruct((DH + GAIN_ROWS, DH), jnp.float32)
    full_float = jax.ShapeDtypeStruct(flat, jnp.float32)
    full_low = jax.ShapeDtypeStruct(flat, jnp.bfloat16)
    half_low = jax.ShapeDtypeStruct((BLOCK, WIDE), jnp.bfloat16)
    short, tall, wide, half = whole(*square.shape), whole(*taller.shape), whole(*flat), whole(BLOCK, WIDE)
    unit = 2 * BLOCK * DH * DH * HEADS

    place = lax.axis_index("seq").astype(jnp.int32).reshape(1)
    deltas = call(
        delta_body,
        [pl.BlockSpec(memory_space=pltpu.HBM)] * 2,
        [short] * HEADS,
        [square] * HEADS,
        6 * unit,
        "delta",
        scratch=[pltpu.VMEM(flat, jnp.bfloat16)] * 2 + [pltpu.SemaphoreType.DMA((PARTS, 2))],
    )(place, *[pltpu.with_memory_space_constraint(a, pltpu.HBM) for a in (key, value)])
    chains = [slice(chain * GROUP, (chain + 1) * GROUP) for chain in range(CHAINS)]
    inner_call = call(
        lambda place_ref, *refs: inner_body(*refs), [wide] * 3, wide, full_float, 16 * unit, "inner"
    )
    first, second = [lax.optimization_barrier(plane_swap(deltas[chain])) for chain in chains]
    state, inner = carried_in(first, False, place, inner_call, (place, query, key, value))
    states = [state, carried_in(second, False, place)[0]]
    attns, later, terms = [], [], ()
    for chain in range(CHAINS):
        size, spec = (square, short) if chain == 0 else (taller, tall)
        extra = [] if chain else [jax.ShapeDtypeStruct((GROUP, DH), jnp.float32)]
        attn, *deltas = call(
            functools.partial(norm_body, chain),
            [wide, wide, wide, whole(1, HEADS * DH)] + [short] * GROUP + [whole(GROUP, DH)] * chain,
            [half] + [spec] * GROUP + [whole(*one.shape) for one in extra],
            [half_low] + [size] * GROUP + extra,
            8 * unit,
            "norm",
        )(place, query, grad, inner, gain, *states[chain], *terms)
        attns.append(attn)
        held, terms = lax.optimization_barrier(plane_swap(deltas[:GROUP])), deltas[GROUP:]
        later += carried_in(held, True, place)[0]
    grad_query, key_part, value_part = call(
        partial_body,
        [wide] * 3 + [half] * CHAINS + [short] * HEADS,
        [wide] * 3,
        [full_low, full_float, full_float],
        48 * unit,
        "partial",
    )(place, query, key, value, *attns, *[state for chain in states for state in chain])
    gain_terms = call(
        gain_body, [short] * GROUP + [tall] * GROUP, whole(HEADS, DH), jax.ShapeDtypeStruct((HEADS, DH), jnp.float32), unit, "gain"
    )(place, *later)
    docs, mask = lax.axis_size("dp"), 1
    while mask < docs:
        gain_terms = gain_terms + lax.ppermute(gain_terms, "dp", [(d, d ^ mask) for d in range(docs)])
        mask *= 2
    chunk = pl.BlockSpec((PART_ROWS, HEADS * DH), lambda step: (step, 0))
    grad_key, grad_value = call(
        final_body, [wide] * 4 + [short] * GROUP + [tall] * GROUP, [chunk] * 2, [full_low] * 2, 16 * unit, "final", steps=PARTS
    )(place, key, value, key_part, value_part, *later)
    grad_gain = gain_terms / math.sqrt(lax.axis_size("seq") * docs * BLOCK)
    return (
        grad_query.reshape(full),
        grad_key.reshape(full),
        grad_value.reshape(full),
        grad_gain.reshape(HEADS * DH),
    )


def solution(mesh):
    sharded = P("dp", "seq", None)
    return jax.shard_map(
        local,
        mesh=mesh,
        in_specs=(sharded, sharded, sharded, P(), sharded),
        out_specs=(sharded, sharded, sharded, P()),
        check_vma=False,
    )
```

```python
import functools
import math

import jax
import jax.numpy as jnp
from jax import lax
from jax.experimental import pallas as pl
from jax.experimental.pallas import tpu as pltpu
from jax.sharding import PartitionSpec as P

HEADS = 8
DH = 128
BLOCK = 256
GROUP = 4
CHAINS = HEADS // GROUP
WIDE = GROUP * DH
GAIN_ROWS = 8
ORDER = (0, 3, 2, 1)
PARTS = 2
PART_ROWS = BLOCK // PARTS
EPSILON = 1e-06

NT = (((1,), (1,)), ((), ()))
TN = (((0,), (0,)), ((), ()))
NN = (((1,), (0,)), ((), ()))


def dot(left, right, dims):
    return lax.dot_general(left, right, dims, preferred_element_type=jnp.float32)


def columns(head):
    return pl.ds(head * DH, DH)


def own_columns(place_ref, mask, chain=0):
    return pl.ds(pl.multiple_of(chain * WIDE + (place_ref[0] & (GROUP - 1) ^ mask) * DH, DH), DH)


def causal(turned=False):
    shape, first = (BLOCK, BLOCK), int(turned)
    return lax.broadcasted_iota(jnp.int32, shape, first) >= lax.broadcasted_iota(jnp.int32, shape, 1 - first)


def delta_body(place_ref, key_ref, value_ref, *refs):
    delta_refs, (key_here, value_here, sems) = refs[:HEADS], refs[HEADS:]
    copies = []
    for part in range(PARTS):
        rows = pl.ds(part * PART_ROWS, PART_ROWS)
        for side, (source, here) in enumerate(((key_ref, key_here), (value_ref, value_here))):
            copies.append(pltpu.make_async_copy(source.at[rows], here.at[rows], sems.at[part, side]))
            copies[-1].start()
    for part in range(PARTS):
        rows = pl.ds(part * PART_ROWS, PART_ROWS)
        for copy in copies[2 * part : 2 * part + 2]:
            copy.wait()
        for at_head, delta_ref in enumerate(delta_refs):
            at = own_columns(place_ref, ORDER[at_head % GROUP], at_head // GROUP)
            delta = dot(key_here[rows, at], value_here[rows, at], TN)
            delta_ref[...] = delta if part == 0 else delta_ref[...] + delta


def inner_body(query_ref, key_ref, value_ref, inner_ref):
    keep = causal()
    for head in range(HEADS):
        at = columns(head)
        scores = jnp.where(keep, dot(query_ref[:, at], key_ref[:, at], NT), 0.0).astype(jnp.bfloat16)
        inner_ref[:, at] = dot(scores, value_ref[:, at], NN)


def norm_body(chain, place_ref, query_ref, grad_ref, inner_ref, gain_ref, *refs):
    state_refs, (attn_ref, *delta_refs) = refs[:GROUP], refs[GROUP:]
    for mask, state_ref, delta_ref in zip(ORDER, state_refs, delta_refs):
        at = own_columns(place_ref, mask, chain)
        query = query_ref[:, at]
        attn = inner_ref[:, at] + dot(query, state_ref[...].astype(jnp.bfloat16), NN)
        per_root = lax.rsqrt(jnp.mean(attn * attn, axis=-1, keepdims=True) + EPSILON)
        normed = attn * per_root
        cotangent = grad_ref[:, at].astype(jnp.float32)
        product = normed * cotangent
        gain = gain_ref[:, at]
        shared = jnp.mean(product * gain, axis=-1, keepdims=True)
        grad_attn = ((gain * cotangent - normed * shared) * per_root).astype(jnp.bfloat16)
        attn_ref[:, own_columns(place_ref, mask)] = grad_attn
        delta_ref[:DH] = dot(query, grad_attn, TN)
        delta_ref[DH:] = jnp.broadcast_to(jnp.sum(product, axis=0, keepdims=True), (GAIN_ROWS, DH))


def partial_body(place_ref, query_ref, key_ref, value_ref, *refs):
    attn_refs, state_refs = refs[:CHAINS], refs[CHAINS : CHAINS + HEADS]
    grad_query_ref, key_part_ref, value_part_ref = refs[-3:]
    keep, kept = causal(), causal(True)
    for at_head, state_ref in enumerate(state_refs):
        chain, mask = at_head // GROUP, ORDER[at_head % GROUP]
        at, here = own_columns(place_ref, mask, chain), own_columns(place_ref, mask)
        query, key, value, grad_attn = query_ref[:, at], key_ref[:, at], value_ref[:, at], attn_refs[chain][:, here]
        turned = jnp.where(kept, dot(key, query, NT), 0.0).astype(jnp.bfloat16)
        grad_scores = jnp.where(keep, dot(grad_attn, value, NT), 0.0).astype(jnp.bfloat16)
        turned_grad = jnp.where(kept, dot(value, grad_attn, NT), 0.0).astype(jnp.bfloat16)
        carried = dot(grad_attn, state_ref[...].astype(jnp.bfloat16), NT)
        grad_query_ref[:, at] = (dot(grad_scores, key, NN) + carried).astype(jnp.bfloat16)
        key_part_ref[:, at] = dot(turned_grad, query, NN)
        value_part_ref[:, at] = dot(turned, grad_attn, NN)


def final_body(place_ref, key_ref, value_ref, key_part_ref, value_part_ref, *refs):
    state_refs, (grad_key_ref, grad_value_ref) = refs[:HEADS], refs[HEADS:]
    rows = pl.ds(pl.multiple_of(pl.program_id(0) * PART_ROWS, PART_ROWS), PART_ROWS)
    for at_head, state_ref in enumerate(state_refs):
        at = own_columns(place_ref, ORDER[at_head % GROUP], at_head // GROUP)
        state = state_ref[:DH].astype(jnp.bfloat16)
        grad_key_ref[:, at] = (key_part_ref[rows, at] + dot(value_ref[rows, at], state, NT)).astype(jnp.bfloat16)
        grad_value_ref[:, at] = (value_part_ref[rows, at] + dot(key_ref[rows, at], state, NN)).astype(jnp.bfloat16)


def gain_body(place_ref, *refs):
    for at_head, state_ref in enumerate(refs[:-1]):
        row = (at_head // GROUP) * GROUP + (place_ref[0] & (GROUP - 1) ^ ORDER[at_head % GROUP])
        refs[-1][pl.ds(row, 1), :] = state_ref[DH : DH + 1]


def prefix_body(reverse, masks, place_ref, *refs):
    (total_ref, *arrived_refs), (*back_refs, ahead) = refs[: -2 * GROUP - 1], refs[-GROUP - 1 :]
    held_refs = refs[-2 * GROUP - 1 : -GROUP - 1]
    for mask, held_ref in zip(ORDER, held_refs):
        ahead[pl.ds(place_ref[0] & (GROUP - 1) ^ mask, 1)] = held_ref[:DH][None]
    running = jnp.zeros((DH, DH), jnp.float32)
    for mask, arrived_ref in zip(masks, arrived_refs):
        later = (place_ref[0] ^ mask < place_ref[0]) != reverse
        running = running + jnp.where(later, arrived_ref[:DH], 0.0)
    for member in reversed(range(GROUP)) if reverse else range(GROUP):
        own = ahead[member]
        ahead[member] = running
        running = running + own
    for mask, back_ref in zip(ORDER, back_refs):
        back_ref[:DH] = ahead[pl.ds(place_ref[0] & (GROUP - 1) ^ mask, 1)][0]
        if back_ref.shape[0] > DH:
            back_ref[DH:] = total_ref[DH:]


def whole(*shape):
    return pl.BlockSpec(shape, lambda step: (0,) * len(shape))


PLACE = pl.BlockSpec(memory_space=pltpu.SMEM)


def call(body, in_specs, out_specs, outs, flops, name, steps=1, scratch=()):
    return pl.pallas_call(
        body,
        grid=(steps,),
        in_specs=[PLACE] + in_specs,
        out_specs=out_specs,
        out_shape=outs,
        scratch_shapes=scratch,
        compiler_params=pltpu.CompilerParams(vmem_limit_bytes=16 * 1024 * 1024),
        cost_estimate=pl.CostEstimate(flops=flops, bytes_accessed=2 << 20, transcendentals=0),
        name=name,
    )


def exchange_steps(near_first):
    count, base, steps = lax.axis_size("seq"), GROUP, []
    while base < count:
        masks = [base, 3 * base, 2 * base] if near_first else [3 * base, 2 * base, base]
        masks = masks if 4 * base <= count else [base]
        steps.append(masks)
        base *= len(masks) + 1
    return steps


def swap(array, mask):
    if mask == 0:
        return array
    return lax.ppermute(array, "seq", [(s, s ^ mask) for s in range(lax.axis_size("seq"))])


def plane_swap(pieces):
    return [swap(piece, mask) for mask, piece in zip(ORDER, pieces)]


def plane_sum(held):
    return sum(held[1:], held[0])


def carried_in(held, reverse, place, beside=None, operands=()):
    total, arrived, steps, result = plane_sum(held), [], exchange_steps(reverse), None
    for masks in steps:
        if beside and masks == steps[-1]:
            result = beside(*operands)
        got = [swap(total, mask) for mask in masks]
        if result is not None:
            got, result = lax.optimization_barrier((got, result))
        elif len(masks) > 1:
            got = lax.optimization_barrier(got)
        arrived += got
        total = sum(got, total)
    single = whole(*total.shape)
    back = call(
        functools.partial(prefix_body, reverse, sum(steps, [])),
        [single] * (1 + len(arrived) + GROUP),
        [single] * GROUP,
        [jax.ShapeDtypeStruct(total.shape, jnp.float32)] * GROUP,
        1 << 24,
        "prefix",
        scratch=[pltpu.VMEM((GROUP, DH, DH), jnp.float32)],
    )(place, total, *arrived, *held)
    return plane_swap(back), result


def local(queries, keys, values, out_gain, grad_out):
    full = queries.shape
    flat = (full[0] * full[1], full[2])
    assert flat == (BLOCK, HEADS * DH) and lax.axis_size("seq") % GROUP == 0
    query, key, value, grad = (a.reshape(flat) for a in (queries, keys, values, grad_out))
    gain = out_gain.reshape(1, HEADS * DH)
    square = jax.ShapeDtypeStruct((DH, DH), jnp.float32)
    taller = jax.ShapeDtypeStruct((DH + GAIN_ROWS, DH), jnp.float32)
    full_float = jax.ShapeDtypeStruct(flat, jnp.float32)
    full_low = jax.ShapeDtypeStruct(flat, jnp.bfloat16)
    half_low = jax.ShapeDtypeStruct((BLOCK, WIDE), jnp.bfloat16)
    short, tall, wide, half = whole(*square.shape), whole(*taller.shape), whole(*flat), whole(BLOCK, WIDE)
    unit = 2 * BLOCK * DH * DH * HEADS

    place = lax.axis_index("seq").astype(jnp.int32).reshape(1)
    deltas = call(
        delta_body,
        [pl.BlockSpec(memory_space=pltpu.HBM)] * 2,
        [short] * HEADS,
        [square] * HEADS,
        6 * unit,
        "delta",
        scratch=[pltpu.VMEM(flat, jnp.bfloat16)] * 2 + [pltpu.SemaphoreType.DMA((PARTS, 2))],
    )(place, *[pltpu.with_memory_space_constraint(a, pltpu.HBM) for a in (key, value)])
    chains = [slice(chain * GROUP, (chain + 1) * GROUP) for chain in range(CHAINS)]
    inner_call = call(
        lambda place_ref, *refs: inner_body(*refs), [wide] * 3, wide, full_float, 16 * unit, "inner"
    )
    first, second = [lax.optimization_barrier(plane_swap(deltas[chain])) for chain in chains]
    second, operands = lax.optimization_barrier((second, (place, query, key, value)))
    state, inner = carried_in(first, False, place, inner_call, operands)
    states = [state, carried_in(second, False, place)[0]]
    attns, later = [], []
    for chain in range(CHAINS):
        attn, *deltas = call(
            functools.partial(norm_body, chain),
            [wide, wide, wide, whole(1, HEADS * DH)] + [short] * GROUP,
            [half] + [tall] * GROUP,
            [half_low] + [taller] * GROUP,
            8 * unit,
            "norm",
        )(place, query, grad, inner, gain, *states[chain])
        attns.append(attn)
        held = lax.optimization_barrier(plane_swap(deltas))
        later += carried_in(held, True, place)[0]
    grad_query, key_part, value_part = call(
        partial_body,
        [wide] * 3 + [half] * CHAINS + [short] * HEADS,
        [wide] * 3,
        [full_low, full_float, full_float],
        48 * unit,
        "partial",
    )(place, query, key, value, *attns, *[state for chain in states for state in chain])
    gain_terms = call(
        gain_body, [tall] * HEADS, whole(HEADS, DH), jax.ShapeDtypeStruct((HEADS, DH), jnp.float32), unit, "gain"
    )(place, *later)
    docs, mask = lax.axis_size("dp"), 1
    while mask < docs:
        gain_terms = gain_terms + lax.ppermute(gain_terms, "dp", [(d, d ^ mask) for d in range(docs)])
        mask *= 2
    chunk = pl.BlockSpec((PART_ROWS, HEADS * DH), lambda step: (step, 0))
    grad_key, grad_value = call(
        final_body, [wide] * 4 + [tall] * HEADS, [chunk] * 2, [full_low] * 2, 16 * unit, "final", steps=PARTS
    )(place, key, value, key_part, value_part, *later)
    grad_gain = gain_terms / math.sqrt(lax.axis_size("seq") * docs * BLOCK)
    return (
        grad_query.reshape(full),
        grad_key.reshape(full),
        grad_value.reshape(full),
        grad_gain.reshape(HEADS * DH),
    )


def solution(mesh):
    sharded = P("dp", "seq", None)
    return jax.shard_map(
        local,
        mesh=mesh,
        in_specs=(sharded, sharded, sharded, P(), sharded),
        out_specs=(sharded, sharded, sharded, P()),
        check_vma=False,
    )
```

```python
import functools
import math

import jax
import jax.numpy as jnp
from jax import lax
from jax.experimental import pallas as pl
from jax.experimental.pallas import tpu as pltpu
from jax.sharding import PartitionSpec as P

HEADS = 8
DH = 128
BLOCK = 256
GROUP = 4
CHAINS = HEADS // GROUP
WIDE = GROUP * DH
GAIN_ROWS = 8
ORDER = (0, 3, 2, 1)
PARTS = 2
PART_ROWS = BLOCK // PARTS
EPSILON = 1e-06

NT = (((1,), (1,)), ((), ()))
TN = (((0,), (0,)), ((), ()))
NN = (((1,), (0,)), ((), ()))


def dot(left, right, dims):
    return lax.dot_general(left, right, dims, preferred_element_type=jnp.float32)


def columns(head):
    return pl.ds(head * DH, DH)


def own_columns(place_ref, mask, chain=0):
    return pl.ds(pl.multiple_of(chain * WIDE + (place_ref[0] & (GROUP - 1) ^ mask) * DH, DH), DH)


def causal(turned=False):
    shape, first = (BLOCK, BLOCK), int(turned)
    return lax.broadcasted_iota(jnp.int32, shape, first) >= lax.broadcasted_iota(jnp.int32, shape, 1 - first)


def delta_body(place_ref, key_ref, value_ref, *refs):
    delta_refs, (key_here, value_here, sems) = refs[:HEADS], refs[HEADS:]
    copies = []
    for part in range(PARTS):
        rows = pl.ds(part * PART_ROWS, PART_ROWS)
        for side, (source, here) in enumerate(((key_ref, key_here), (value_ref, value_here))):
            copies.append(pltpu.make_async_copy(source.at[rows], here.at[rows], sems.at[part, side]))
            copies[-1].start()
    for part in range(PARTS):
        rows = pl.ds(part * PART_ROWS, PART_ROWS)
        for copy in copies[2 * part : 2 * part + 2]:
            copy.wait()
        for at_head, delta_ref in enumerate(delta_refs):
            at = own_columns(place_ref, ORDER[at_head % GROUP], at_head // GROUP)
            delta = dot(key_here[rows, at], value_here[rows, at], TN)
            delta_ref[...] = delta if part == 0 else delta_ref[...] + delta


def inner_body(query_ref, key_ref, value_ref, inner_ref, turned_ref):
    keep = causal()
    for head in range(HEADS):
        at = columns(head)
        query = query_ref[:, at]
        scores = jnp.where(keep, dot(query, key_ref[:, at], NT), 0.0).astype(jnp.bfloat16)
        inner_ref[:, at] = dot(scores, value_ref[:, at], NN)
        turned_ref[at, :] = query.T


def norm_body(chain, place_ref, query_ref, turned_ref, grad_ref, inner_ref, gain_ref, *refs):
    state_refs, (attn_ref, *delta_refs) = refs[:GROUP], refs[GROUP:]
    for mask, state_ref, delta_ref in zip(ORDER, state_refs, delta_refs):
        at = own_columns(place_ref, mask, chain)
        query = query_ref[:, at]
        attn = inner_ref[:, at] + dot(query, state_ref[...].astype(jnp.bfloat16), NN)
        per_root = lax.rsqrt(jnp.mean(attn * attn, axis=-1, keepdims=True) + EPSILON)
        normed = attn * per_root
        cotangent = grad_ref[:, at].astype(jnp.float32)
        product = normed * cotangent
        gain = gain_ref[:, at]
        shared = jnp.mean(product * gain, axis=-1, keepdims=True)
        grad_attn = ((gain * cotangent - normed * shared) * per_root).astype(jnp.bfloat16)
        attn_ref[:, own_columns(place_ref, mask)] = grad_attn
        delta_ref[:DH] = dot(turned_ref[at, :], grad_attn, NN)
        delta_ref[DH:] = jnp.broadcast_to(jnp.sum(product, axis=0, keepdims=True), (GAIN_ROWS, DH))


def partial_body(place_ref, query_ref, key_ref, value_ref, *refs):
    attn_refs, state_refs = refs[:CHAINS], refs[CHAINS : CHAINS + HEADS]
    grad_query_ref, key_part_ref, value_part_ref = refs[-3:]
    keep, kept = causal(), causal(True)
    for at_head, state_ref in enumerate(state_refs):
        chain, mask = at_head // GROUP, ORDER[at_head % GROUP]
        at, here = own_columns(place_ref, mask, chain), own_columns(place_ref, mask)
        query, key, value, grad_attn = query_ref[:, at], key_ref[:, at], value_ref[:, at], attn_refs[chain][:, here]
        turned = jnp.where(kept, dot(key, query, NT), 0.0).astype(jnp.bfloat16)
        grad_scores = jnp.where(keep, dot(grad_attn, value, NT), 0.0).astype(jnp.bfloat16)
        turned_grad = jnp.where(kept, dot(value, grad_attn, NT), 0.0).astype(jnp.bfloat16)
        carried = dot(grad_attn, state_ref[...].astype(jnp.bfloat16), NT)
        grad_query_ref[:, at] = (dot(grad_scores, key, NN) + carried).astype(jnp.bfloat16)
        key_part_ref[:, at] = dot(turned_grad, query, NN)
        value_part_ref[:, at] = dot(turned, grad_attn, NN)


def final_body(place_ref, key_ref, value_ref, key_part_ref, value_part_ref, *refs):
    state_refs, (grad_key_ref, grad_value_ref) = refs[:HEADS], refs[HEADS:]
    rows = pl.ds(pl.multiple_of(pl.program_id(0) * PART_ROWS, PART_ROWS), PART_ROWS)
    for at_head, state_ref in enumerate(state_refs):
        at = own_columns(place_ref, ORDER[at_head % GROUP], at_head // GROUP)
        state = state_ref[:DH].astype(jnp.bfloat16)
        grad_key_ref[:, at] = (key_part_ref[rows, at] + dot(value_ref[rows, at], state, NT)).astype(jnp.bfloat16)
        grad_value_ref[:, at] = (value_part_ref[rows, at] + dot(key_ref[rows, at], state, NN)).astype(jnp.bfloat16)


def gain_body(place_ref, *refs):
    for at_head, state_ref in enumerate(refs[:-1]):
        row = (at_head // GROUP) * GROUP + (place_ref[0] & (GROUP - 1) ^ ORDER[at_head % GROUP])
        refs[-1][pl.ds(row, 1), :] = state_ref[DH : DH + 1]


def prefix_body(reverse, masks, place_ref, *refs):
    (total_ref, *arrived_refs), (*back_refs, ahead) = refs[: -2 * GROUP - 1], refs[-GROUP - 1 :]
    held_refs = refs[-2 * GROUP - 1 : -GROUP - 1]
    for mask, held_ref in zip(ORDER, held_refs):
        ahead[pl.ds(place_ref[0] & (GROUP - 1) ^ mask, 1)] = held_ref[:DH][None]
    running = jnp.zeros((DH, DH), jnp.float32)
    for mask, arrived_ref in zip(masks, arrived_refs):
        later = (place_ref[0] ^ mask < place_ref[0]) != reverse
        running = running + jnp.where(later, arrived_ref[:DH], 0.0)
    for member in reversed(range(GROUP)) if reverse else range(GROUP):
        own = ahead[member]
        ahead[member] = running
        running = running + own
    for mask, back_ref in zip(ORDER, back_refs):
        back_ref[:DH] = ahead[pl.ds(place_ref[0] & (GROUP - 1) ^ mask, 1)][0]
        if back_ref.shape[0] > DH:
            back_ref[DH:] = total_ref[DH:]


def whole(*shape):
    return pl.BlockSpec(shape, lambda step: (0,) * len(shape))


PLACE = pl.BlockSpec(memory_space=pltpu.SMEM)


def call(body, in_specs, out_specs, outs, flops, name, steps=1, scratch=()):
    return pl.pallas_call(
        body,
        grid=(steps,),
        in_specs=[PLACE] + in_specs,
        out_specs=out_specs,
        out_shape=outs,
        scratch_shapes=scratch,
        compiler_params=pltpu.CompilerParams(vmem_limit_bytes=16 * 1024 * 1024),
        cost_estimate=pl.CostEstimate(flops=flops, bytes_accessed=2 << 20, transcendentals=0),
        name=name,
    )


def exchange_steps(near_first):
    count, base, steps = lax.axis_size("seq"), GROUP, []
    while base < count:
        masks = [base, 3 * base, 2 * base] if near_first else [3 * base, 2 * base, base]
        masks = masks if 4 * base <= count else [base]
        steps.append(masks)
        base *= len(masks) + 1
    return steps


def swap(array, mask):
    if mask == 0:
        return array
    return lax.ppermute(array, "seq", [(s, s ^ mask) for s in range(lax.axis_size("seq"))])


def plane_swap(pieces):
    return [swap(piece, mask) for mask, piece in zip(ORDER, pieces)]


def plane_sum(held):
    return sum(held[1:], held[0])


def carried_in(held, reverse, place, beside=None, operands=()):
    total, arrived, steps, result = plane_sum(held), [], exchange_steps(reverse), None
    for masks in steps:
        if beside and masks == steps[-1]:
            result = beside(*operands)
        got = [swap(total, mask) for mask in masks]
        if result is not None:
            got, result = lax.optimization_barrier((got, result))
        elif len(masks) > 1:
            got = lax.optimization_barrier(got)
        arrived += got
        total = sum(got, total)
    single = whole(*total.shape)
    back = call(
        functools.partial(prefix_body, reverse, sum(steps, [])),
        [single] * (1 + len(arrived) + GROUP),
        [single] * GROUP,
        [jax.ShapeDtypeStruct(total.shape, jnp.float32)] * GROUP,
        1 << 24,
        "prefix",
        scratch=[pltpu.VMEM((GROUP, DH, DH), jnp.float32)],
    )(place, total, *arrived, *held)
    return plane_swap(back), result


def local(queries, keys, values, out_gain, grad_out):
    full = queries.shape
    flat = (full[0] * full[1], full[2])
    assert flat == (BLOCK, HEADS * DH) and lax.axis_size("seq") % GROUP == 0
    query, key, value, grad = (a.reshape(flat) for a in (queries, keys, values, grad_out))
    gain = out_gain.reshape(1, HEADS * DH)
    square = jax.ShapeDtypeStruct((DH, DH), jnp.float32)
    taller = jax.ShapeDtypeStruct((DH + GAIN_ROWS, DH), jnp.float32)
    full_float = jax.ShapeDtypeStruct(flat, jnp.float32)
    full_low = jax.ShapeDtypeStruct(flat, jnp.bfloat16)
    turned_low = jax.ShapeDtypeStruct(flat[::-1], jnp.bfloat16)
    half_low = jax.ShapeDtypeStruct((BLOCK, WIDE), jnp.bfloat16)
    short, tall, wide, half = whole(*square.shape), whole(*taller.shape), whole(*flat), whole(BLOCK, WIDE)
    unit = 2 * BLOCK * DH * DH * HEADS

    place = lax.axis_index("seq").astype(jnp.int32).reshape(1)
    deltas = call(
        delta_body,
        [pl.BlockSpec(memory_space=pltpu.HBM)] * 2,
        [short] * HEADS,
        [square] * HEADS,
        6 * unit,
        "delta",
        scratch=[pltpu.VMEM(flat, jnp.bfloat16)] * 2 + [pltpu.SemaphoreType.DMA((PARTS, 2))],
    )(place, *[pltpu.with_memory_space_constraint(a, pltpu.HBM) for a in (key, value)])
    chains = [slice(chain * GROUP, (chain + 1) * GROUP) for chain in range(CHAINS)]
    inner_call = call(
        lambda place_ref, *refs: inner_body(*refs),
        [wide] * 3,
        [wide, whole(*turned_low.shape)],
        [full_float, turned_low],
        16 * unit,
        "inner",
    )
    first, second = [lax.optimization_barrier(plane_swap(deltas[chain])) for chain in chains]
    second, operands = lax.optimization_barrier((second, (place, query, key, value)))
    state, (inner, turned) = carried_in(first, False, place, inner_call, operands)
    states = [state, carried_in(second, False, place)[0]]
    attns, later = [], []
    for chain in range(CHAINS):
        attn, *deltas = call(
            functools.partial(norm_body, chain),
            [wide, whole(*turned_low.shape), wide, wide, whole(1, HEADS * DH)] + [short] * GROUP,
            [half] + [tall] * GROUP,
            [half_low] + [taller] * GROUP,
            8 * unit,
            "norm",
        )(place, query, turned, grad, inner, gain, *states[chain])
        attns.append(attn)
        held = lax.optimization_barrier(plane_swap(deltas))
        later += carried_in(held, True, place)[0]
    grad_query, key_part, value_part = call(
        partial_body,
        [wide] * 3 + [half] * CHAINS + [short] * HEADS,
        [wide] * 3,
        [full_low, full_float, full_float],
        48 * unit,
        "partial",
    )(place, query, key, value, *attns, *[state for chain in states for state in chain])
    gain_terms = call(
        gain_body, [tall] * HEADS, whole(HEADS, DH), jax.ShapeDtypeStruct((HEADS, DH), jnp.float32), unit, "gain"
    )(place, *later)
    docs, mask = lax.axis_size("dp"), 1
    while mask < docs:
        gain_terms = gain_terms + lax.ppermute(gain_terms, "dp", [(d, d ^ mask) for d in range(docs)])
        mask *= 2
    chunk = pl.BlockSpec((PART_ROWS, HEADS * DH), lambda step: (step, 0))
    grad_key, grad_value = call(
        final_body, [wide] * 4 + [tall] * HEADS, [chunk] * 2, [full_low] * 2, 16 * unit, "final", steps=PARTS
    )(place, key, value, key_part, value_part, *later)
    grad_gain = gain_terms / math.sqrt(lax.axis_size("seq") * docs * BLOCK)
    return (
        grad_query.reshape(full),
        grad_key.reshape(full),
        grad_value.reshape(full),
        grad_gain.reshape(HEADS * DH),
    )


def solution(mesh):
    sharded = P("dp", "seq", None)
    return jax.shard_map(
        local,
        mesh=mesh,
        in_specs=(sharded, sharded, sharded, P(), sharded),
        out_specs=(sharded, sharded, sharded, P()),
        check_vma=False,
    )
```

```python
import functools
import math

import jax
import jax.numpy as jnp
from jax import lax
from jax.experimental import pallas as pl
from jax.experimental.pallas import tpu as pltpu
from jax.sharding import PartitionSpec as P

HEADS = 8
DH = 128
BLOCK = 256
GROUP = 4
CHAINS = HEADS // GROUP
WIDE = GROUP * DH
GAIN_ROWS = 8
ORDER = (0, 3, 2, 1)
PARTS = 2
PART_ROWS = BLOCK // PARTS
EPSILON = 1e-06

NT = (((1,), (1,)), ((), ()))
TN = (((0,), (0,)), ((), ()))
NN = (((1,), (0,)), ((), ()))


def dot(left, right, dims):
    return lax.dot_general(left, right, dims, preferred_element_type=jnp.float32)


def columns(head):
    return pl.ds(head * DH, DH)


def own_columns(place_ref, mask, chain=0):
    return pl.ds(pl.multiple_of(chain * WIDE + (place_ref[0] & (GROUP - 1) ^ mask) * DH, DH), DH)


def causal(turned=False):
    shape, first = (BLOCK, BLOCK), int(turned)
    return lax.broadcasted_iota(jnp.int32, shape, first) >= lax.broadcasted_iota(jnp.int32, shape, 1 - first)


def delta_body(place_ref, key_ref, value_ref, *refs):
    delta_refs, (key_here, value_here, sems) = refs[:HEADS], refs[HEADS:]
    copies = []
    for part in range(PARTS):
        rows = pl.ds(part * PART_ROWS, PART_ROWS)
        for side, (source, here) in enumerate(((key_ref, key_here), (value_ref, value_here))):
            copies.append(pltpu.make_async_copy(source.at[rows], here.at[rows], sems.at[part, side]))
            copies[-1].start()
    for part in range(PARTS):
        rows = pl.ds(part * PART_ROWS, PART_ROWS)
        for copy in copies[2 * part : 2 * part + 2]:
            copy.wait()
        for at_head, delta_ref in enumerate(delta_refs):
            at = own_columns(place_ref, ORDER[at_head % GROUP], at_head // GROUP)
            delta = dot(key_here[rows, at], value_here[rows, at], TN)
            delta_ref[...] = delta if part == 0 else delta_ref[...] + delta


def inner_body(query_ref, key_ref, value_ref, inner_ref, turned_ref, scores_ref):
    keep, kept = causal(), causal(True)
    for head in range(HEADS):
        at = columns(head)
        query = query_ref[:, at]
        scores = jnp.where(keep, dot(query, key_ref[:, at], NT), 0.0).astype(jnp.bfloat16)
        inner_ref[:, at] = dot(scores, value_ref[:, at], NN)
        turned = query.T
        turned_ref[at, :] = turned
        scores_ref[head] = jnp.where(kept, dot(key_ref[:, at], turned, NN), 0.0).astype(jnp.bfloat16)


def norm_body(chain, place_ref, query_ref, turned_ref, grad_ref, inner_ref, gain_ref, *refs):
    state_refs, (attn_ref, *delta_refs) = refs[:GROUP], refs[GROUP:]
    for mask, state_ref, delta_ref in zip(ORDER, state_refs, delta_refs):
        at = own_columns(place_ref, mask, chain)
        query = query_ref[:, at]
        attn = inner_ref[:, at] + dot(query, state_ref[...].astype(jnp.bfloat16), NN)
        per_root = lax.rsqrt(jnp.mean(attn * attn, axis=-1, keepdims=True) + EPSILON)
        normed = attn * per_root
        cotangent = grad_ref[:, at].astype(jnp.float32)
        product = normed * cotangent
        gain = gain_ref[:, at]
        shared = jnp.mean(product * gain, axis=-1, keepdims=True)
        grad_attn = ((gain * cotangent - normed * shared) * per_root).astype(jnp.bfloat16)
        attn_ref[:, own_columns(place_ref, mask)] = grad_attn
        delta_ref[:DH] = dot(turned_ref[at, :], grad_attn, NN)
        delta_ref[DH:] = jnp.broadcast_to(jnp.sum(product, axis=0, keepdims=True), (GAIN_ROWS, DH))


def partial_body(place_ref, query_ref, key_ref, value_ref, scores_ref, *refs):
    attn_refs, state_refs = refs[:CHAINS], refs[CHAINS : CHAINS + HEADS]
    later_refs, (grad_query_ref, *out_refs) = refs[CHAINS + HEADS : -5], refs[-5:]
    keep, kept = causal(), causal(True)
    for at_head, state_ref in enumerate(state_refs):
        chain, mask = at_head // GROUP, ORDER[at_head % GROUP]
        at, here = own_columns(place_ref, mask, chain), own_columns(place_ref, mask)
        query, key, value, grad_attn = query_ref[:, at], key_ref[:, at], value_ref[:, at], attn_refs[chain][:, here]
        turned = scores_ref[chain * GROUP + (place_ref[0] & (GROUP - 1) ^ mask)]
        grad_scores = jnp.where(keep, dot(grad_attn, value, NT), 0.0).astype(jnp.bfloat16)
        turned_grad = jnp.where(kept, dot(value, grad_attn, NT), 0.0).astype(jnp.bfloat16)
        carried = dot(grad_attn, state_ref[...].astype(jnp.bfloat16), NT)
        grad_query_ref[:, at] = (dot(grad_scores, key, NN) + carried).astype(jnp.bfloat16)
        parts = [dot(turned_grad, query, NN), dot(turned, grad_attn, NN)]
        if chain == 0:
            state = later_refs[at_head][:DH].astype(jnp.bfloat16)
            parts = [parts[0] + dot(value, state, NT), parts[1] + dot(key, state, NN)]
        for part, out_ref in zip(parts, out_refs[2 * chain :]):
            out_ref[:, here] = part.astype(out_ref.dtype)


def final_body(place_ref, key_ref, value_ref, key_part_ref, value_part_ref, *refs):
    state_refs, (grad_key_ref, grad_value_ref) = refs[:GROUP], refs[-2:]
    for mask, state_ref in zip(ORDER, state_refs):
        at, here = own_columns(place_ref, mask, 1), own_columns(place_ref, mask)
        state = state_ref[:DH].astype(jnp.bfloat16)
        grad_key_ref[:, here] = (key_part_ref[:, here] + dot(value_ref[:, at], state, NT)).astype(jnp.bfloat16)
        grad_value_ref[:, here] = (value_part_ref[:, here] + dot(key_ref[:, at], state, NN)).astype(jnp.bfloat16)


def gain_body(place_ref, *refs):
    for at_head, state_ref in enumerate(refs[:-1]):
        row = (at_head // GROUP) * GROUP + (place_ref[0] & (GROUP - 1) ^ ORDER[at_head % GROUP])
        refs[-1][pl.ds(row, 1), :] = state_ref[DH : DH + 1]


def prefix_body(reverse, masks, place_ref, *refs):
    (total_ref, *arrived_refs), (*back_refs, ahead) = refs[: -2 * GROUP - 1], refs[-GROUP - 1 :]
    held_refs = refs[-2 * GROUP - 1 : -GROUP - 1]
    for mask, held_ref in zip(ORDER, held_refs):
        ahead[pl.ds(place_ref[0] & (GROUP - 1) ^ mask, 1)] = held_ref[:DH][None]
    running = jnp.zeros((DH, DH), jnp.float32)
    for mask, arrived_ref in zip(masks, arrived_refs):
        later = (place_ref[0] ^ mask < place_ref[0]) != reverse
        running = running + jnp.where(later, arrived_ref[:DH], 0.0)
    for member in reversed(range(GROUP)) if reverse else range(GROUP):
        own = ahead[member]
        ahead[member] = running
        running = running + own
    for mask, back_ref in zip(ORDER, back_refs):
        back_ref[:DH] = ahead[pl.ds(place_ref[0] & (GROUP - 1) ^ mask, 1)][0]
        if back_ref.shape[0] > DH:
            back_ref[DH:] = total_ref[DH:]


def whole(*shape):
    return pl.BlockSpec(shape, lambda step: (0,) * len(shape))


PLACE = pl.BlockSpec(memory_space=pltpu.SMEM)


def call(body, in_specs, out_specs, outs, flops, name, steps=1, scratch=(), aliases=None):
    return pl.pallas_call(
        body,
        grid=(steps,),
        in_specs=[PLACE] + in_specs,
        out_specs=out_specs,
        out_shape=outs,
        scratch_shapes=scratch,
        input_output_aliases=aliases or {},
        compiler_params=pltpu.CompilerParams(vmem_limit_bytes=16 * 1024 * 1024),
        cost_estimate=pl.CostEstimate(flops=flops, bytes_accessed=2 << 20, transcendentals=0),
        name=name,
    )


def exchange_steps(near_first):
    count, base, steps = lax.axis_size("seq"), GROUP, []
    while base < count:
        masks = [base, 3 * base, 2 * base] if near_first else [3 * base, 2 * base, base]
        masks = masks if 4 * base <= count else [base]
        steps.append(masks)
        base *= len(masks) + 1
    return steps


def swap(array, mask):
    if mask == 0:
        return array
    return lax.ppermute(array, "seq", [(s, s ^ mask) for s in range(lax.axis_size("seq"))])


def plane_swap(pieces):
    return [swap(piece, mask) for mask, piece in zip(ORDER, pieces)]


def plane_sum(held):
    return sum(held[1:], held[0])


def carried_in(held, reverse, place, beside=None, operands=()):
    total, arrived, steps, result = plane_sum(held), [], exchange_steps(reverse), None
    for masks in steps:
        if beside and masks == steps[-1]:
            result = beside(*operands)
        got = [swap(total, mask) for mask in masks]
        if result is not None:
            got, result = lax.optimization_barrier((got, result))
        elif len(masks) > 1:
            got = lax.optimization_barrier(got)
        arrived += got
        total = sum(got, total)
    single = whole(*total.shape)
    back = call(
        functools.partial(prefix_body, reverse, sum(steps, [])),
        [single] * (1 + len(arrived) + GROUP),
        [single] * GROUP,
        [jax.ShapeDtypeStruct(total.shape, jnp.float32)] * GROUP,
        1 << 24,
        "prefix",
        scratch=[pltpu.VMEM((GROUP, DH, DH), jnp.float32)],
    )(place, total, *arrived, *held)
    return plane_swap(back), result


def local(queries, keys, values, out_gain, grad_out):
    full = queries.shape
    flat = (full[0] * full[1], full[2])
    assert flat == (BLOCK, HEADS * DH) and lax.axis_size("seq") % GROUP == 0
    query, key, value, grad = (a.reshape(flat) for a in (queries, keys, values, grad_out))
    gain = out_gain.reshape(1, HEADS * DH)
    square = jax.ShapeDtypeStruct((DH, DH), jnp.float32)
    taller = jax.ShapeDtypeStruct((DH + GAIN_ROWS, DH), jnp.float32)
    full_float = jax.ShapeDtypeStruct(flat, jnp.float32)
    full_low = jax.ShapeDtypeStruct(flat, jnp.bfloat16)
    scores_low = jax.ShapeDtypeStruct((HEADS, BLOCK, BLOCK), jnp.bfloat16)
    turned_low = jax.ShapeDtypeStruct(flat[::-1], jnp.bfloat16)
    half_float = jax.ShapeDtypeStruct((BLOCK, WIDE), jnp.float32)
    half_low = jax.ShapeDtypeStruct((BLOCK, WIDE), jnp.bfloat16)
    short, tall, wide, half = whole(*square.shape), whole(*taller.shape), whole(*flat), whole(BLOCK, WIDE)
    unit = 2 * BLOCK * DH * DH * HEADS

    place = lax.axis_index("seq").astype(jnp.int32).reshape(1)
    deltas = call(
        delta_body,
        [pl.BlockSpec(memory_space=pltpu.HBM)] * 2,
        [short] * HEADS,
        [square] * HEADS,
        6 * unit,
        "delta",
        scratch=[pltpu.VMEM(flat, jnp.bfloat16)] * 2 + [pltpu.SemaphoreType.DMA((PARTS, 2))],
    )(place, *[pltpu.with_memory_space_constraint(a, pltpu.HBM) for a in (key, value)])
    chains = [slice(chain * GROUP, (chain + 1) * GROUP) for chain in range(CHAINS)]
    inner_call = call(
        lambda place_ref, *refs: inner_body(*refs),
        [wide] * 3,
        [wide, whole(*turned_low.shape), whole(*scores_low.shape)],
        [full_float, turned_low, scores_low],
        16 * unit,
        "inner",
    )
    first, second = [lax.optimization_barrier(plane_swap(deltas[chain])) for chain in chains]
    second, operands = lax.optimization_barrier((second, (place, query, key, value)))
    state, (inner, turned, scores) = carried_in(first, False, place, inner_call, operands)
    states = [state, carried_in(second, False, place)[0]]
    attns, later = [], []
    for chain in range(CHAINS):
        attn, *deltas = call(
            functools.partial(norm_body, chain),
            [wide, whole(*turned_low.shape), wide, wide, whole(1, HEADS * DH)] + [short] * GROUP,
            [half] + [tall] * GROUP,
            [half_low] + [taller] * GROUP,
            8 * unit,
            "norm",
        )(place, query, turned, grad, inner, gain, *states[chain])
        attns.append(attn)
        held = lax.optimization_barrier(plane_swap(deltas))
        later += carried_in(held, True, place)[0]
    chunks = [pl.BlockSpec((BLOCK, WIDE), lambda step, chain=chain: (0, chain)) for chain in range(CHAINS)]
    grad_query, grad_key, grad_value, key_part, value_part = call(
        partial_body,
        [wide] * 3 + [whole(*scores_low.shape)] + [half] * CHAINS + [short] * HEADS + [tall] * GROUP,
        [wide] + [chunks[0]] * 2 + [half] * 2,
        [full_low] * 3 + [half_float] * 2,
        48 * unit,
        "partial",
    )(place, query, key, value, scores, *attns, *[state for chain in states for state in chain], *later[:GROUP])
    gain_terms = call(
        gain_body, [tall] * HEADS, whole(HEADS, DH), jax.ShapeDtypeStruct((HEADS, DH), jnp.float32), unit, "gain"
    )(place, *later)
    gain_terms, value_part = lax.optimization_barrier((gain_terms, value_part))
    docs, mask = lax.axis_size("dp"), 1
    while mask < docs:
        gain_terms = gain_terms + lax.ppermute(gain_terms, "dp", [(d, d ^ mask) for d in range(docs)])
        mask *= 2
    grad_key, grad_value = call(
        final_body,
        [wide] * 2 + [half] * 2 + [tall] * GROUP + [pl.BlockSpec(memory_space=pl.ANY)] * 2,
        [chunks[1]] * 2,
        [full_low] * 2,
        8 * unit,
        "final",
        aliases={5 + GROUP: 0, 6 + GROUP: 1},
    )(place, key, value, key_part, value_part, *later[GROUP:], grad_key, grad_value)
    grad_gain = gain_terms / math.sqrt(lax.axis_size("seq") * docs * BLOCK)
    return (
        grad_query.reshape(full),
        grad_key.reshape(full),
        grad_value.reshape(full),
        grad_gain.reshape(HEADS * DH),
    )


def solution(mesh):
    sharded = P("dp", "seq", None)
    return jax.shard_map(
        local,
        mesh=mesh,
        in_specs=(sharded, sharded, sharded, P(), sharded),
        out_specs=(sharded, sharded, sharded, P()),
        check_vma=False,
    )
```

```python
import functools
import math

import jax
import jax.numpy as jnp
from jax import lax
from jax.experimental import pallas as pl
from jax.experimental.pallas import tpu as pltpu
from jax.sharding import PartitionSpec as P

HEADS = 8
DH = 128
BLOCK = 256
GROUP = 4
CHAINS = HEADS // GROUP
WIDE = GROUP * DH
GAIN_ROWS = 8
ORDER = (0, 3, 2, 1)
PARTS = 2
PART_ROWS = BLOCK // PARTS
EPSILON = 1e-06

NT = (((1,), (1,)), ((), ()))
TN = (((0,), (0,)), ((), ()))
NN = (((1,), (0,)), ((), ()))


def dot(left, right, dims):
    return lax.dot_general(left, right, dims, preferred_element_type=jnp.float32)


def columns(head):
    return pl.ds(head * DH, DH)


def own_columns(place_ref, mask, chain=0):
    return pl.ds(pl.multiple_of(chain * WIDE + (place_ref[0] & (GROUP - 1) ^ mask) * DH, DH), DH)


def causal(turned=False):
    shape, first = (BLOCK, BLOCK), int(turned)
    return lax.broadcasted_iota(jnp.int32, shape, first) >= lax.broadcasted_iota(jnp.int32, shape, 1 - first)


def delta_body(place_ref, key_ref, value_ref, *refs):
    delta_refs, (key_here, value_here, sems) = refs[:HEADS], refs[HEADS:]
    copies = []
    for part in range(PARTS):
        rows = pl.ds(part * PART_ROWS, PART_ROWS)
        for side, (source, here) in enumerate(((key_ref, key_here), (value_ref, value_here))):
            copies.append(pltpu.make_async_copy(source.at[rows], here.at[rows], sems.at[part, side]))
            copies[-1].start()
    for part in range(PARTS):
        rows = pl.ds(part * PART_ROWS, PART_ROWS)
        for copy in copies[2 * part : 2 * part + 2]:
            copy.wait()
        for at_head, delta_ref in enumerate(delta_refs):
            at = own_columns(place_ref, ORDER[at_head % GROUP], at_head // GROUP)
            delta = dot(key_here[rows, at], value_here[rows, at], TN)
            delta_ref[...] = delta if part == 0 else delta_ref[...] + delta


def inner_body(query_ref, key_ref, value_ref, inner_ref, turned_ref):
    keep = causal()
    for head in range(HEADS):
        at = columns(head)
        query = query_ref[:, at]
        scores = jnp.where(keep, dot(query, key_ref[:, at], NT), 0.0).astype(jnp.bfloat16)
        inner_ref[:, at] = dot(scores, value_ref[:, at], NN)
        turned_ref[at, :] = query.T


def norm_body(chain, place_ref, query_ref, turned_ref, grad_ref, inner_ref, gain_ref, *refs):
    state_refs, (attn_ref, *delta_refs) = refs[:GROUP], refs[GROUP:]
    for mask, state_ref, delta_ref in zip(ORDER, state_refs, delta_refs):
        at = own_columns(place_ref, mask, chain)
        query = query_ref[:, at]
        attn = inner_ref[:, at] + dot(query, state_ref[...].astype(jnp.bfloat16), NN)
        per_root = lax.rsqrt(jnp.mean(attn * attn, axis=-1, keepdims=True) + EPSILON)
        normed = attn * per_root
        cotangent = grad_ref[:, at].astype(jnp.float32)
        product = normed * cotangent
        gain = gain_ref[:, at]
        shared = jnp.mean(product * gain, axis=-1, keepdims=True)
        grad_attn = ((gain * cotangent - normed * shared) * per_root).astype(jnp.bfloat16)
        attn_ref[:, own_columns(place_ref, mask)] = grad_attn
        delta_ref[:DH] = dot(turned_ref[at, :], grad_attn, NN)
        delta_ref[DH:] = jnp.broadcast_to(jnp.sum(product, axis=0, keepdims=True), (GAIN_ROWS, DH))


def partial_body(place_ref, query_ref, key_ref, value_ref, turned_ref, *refs):
    attn_refs, state_refs = refs[:CHAINS], refs[CHAINS : CHAINS + HEADS]
    later_refs, (grad_query_ref, *out_refs) = refs[CHAINS + HEADS : -5], refs[-5:]
    keep, kept = causal(), causal(True)
    for at_head, state_ref in enumerate(state_refs):
        chain, mask = at_head // GROUP, ORDER[at_head % GROUP]
        at, here = own_columns(place_ref, mask, chain), own_columns(place_ref, mask)
        query, key, value, grad_attn = query_ref[:, at], key_ref[:, at], value_ref[:, at], attn_refs[chain][:, here]
        turned = jnp.where(kept, dot(key, turned_ref[at, :], NN), 0.0).astype(jnp.bfloat16)
        grad_scores = jnp.where(keep, dot(grad_attn, value, NT), 0.0).astype(jnp.bfloat16)
        turned_grad = jnp.where(kept, dot(value, grad_attn, NT), 0.0).astype(jnp.bfloat16)
        carried = dot(grad_attn, state_ref[...].astype(jnp.bfloat16), NT)
        grad_query_ref[:, at] = (dot(grad_scores, key, NN) + carried).astype(jnp.bfloat16)
        parts = [dot(turned_grad, query, NN), dot(turned, grad_attn, NN)]
        if chain == 0:
            state = later_refs[at_head][:DH].astype(jnp.bfloat16)
            parts = [parts[0] + dot(value, state, NT), parts[1] + dot(key, state, NN)]
        for part, out_ref in zip(parts, out_refs[2 * chain :]):
            out_ref[:, here] = part.astype(out_ref.dtype)


def final_body(place_ref, key_ref, value_ref, key_part_ref, value_part_ref, *refs):
    state_refs, (grad_key_ref, grad_value_ref) = refs[:GROUP], refs[-2:]
    for mask, state_ref in zip(ORDER, state_refs):
        at, here = own_columns(place_ref, mask, 1), own_columns(place_ref, mask)
        state = state_ref[:DH].astype(jnp.bfloat16)
        grad_key_ref[:, here] = (key_part_ref[:, here] + dot(value_ref[:, at], state, NT)).astype(jnp.bfloat16)
        grad_value_ref[:, here] = (value_part_ref[:, here] + dot(key_ref[:, at], state, NN)).astype(jnp.bfloat16)


def gain_body(place_ref, *refs):
    for at_head, state_ref in enumerate(refs[:-1]):
        row = (at_head // GROUP) * GROUP + (place_ref[0] & (GROUP - 1) ^ ORDER[at_head % GROUP])
        refs[-1][pl.ds(row, 1), :] = state_ref[DH : DH + 1]


def prefix_body(reverse, masks, place_ref, *refs):
    (total_ref, *arrived_refs), (*back_refs, ahead) = refs[: -2 * GROUP - 1], refs[-GROUP - 1 :]
    held_refs = refs[-2 * GROUP - 1 : -GROUP - 1]
    for mask, held_ref in zip(ORDER, held_refs):
        ahead[pl.ds(place_ref[0] & (GROUP - 1) ^ mask, 1)] = held_ref[:DH][None]
    running = jnp.zeros((DH, DH), jnp.float32)
    for mask, arrived_ref in zip(masks, arrived_refs):
        later = (place_ref[0] ^ mask < place_ref[0]) != reverse
        running = running + jnp.where(later, arrived_ref[:DH], 0.0)
    for member in reversed(range(GROUP)) if reverse else range(GROUP):
        own = ahead[member]
        ahead[member] = running
        running = running + own
    for mask, back_ref in zip(ORDER, back_refs):
        back_ref[:DH] = ahead[pl.ds(place_ref[0] & (GROUP - 1) ^ mask, 1)][0]
        if back_ref.shape[0] > DH:
            back_ref[DH:] = total_ref[DH:]


def whole(*shape):
    return pl.BlockSpec(shape, lambda step: (0,) * len(shape))


PLACE = pl.BlockSpec(memory_space=pltpu.SMEM)


def call(body, in_specs, out_specs, outs, flops, name, steps=1, scratch=(), aliases=None):
    return pl.pallas_call(
        body,
        grid=(steps,),
        in_specs=[PLACE] + in_specs,
        out_specs=out_specs,
        out_shape=outs,
        scratch_shapes=scratch,
        input_output_aliases=aliases or {},
        compiler_params=pltpu.CompilerParams(vmem_limit_bytes=16 * 1024 * 1024),
        cost_estimate=pl.CostEstimate(flops=flops, bytes_accessed=2 << 20, transcendentals=0),
        name=name,
    )


def exchange_steps(near_first):
    count, base, steps = lax.axis_size("seq"), GROUP, []
    while base < count:
        masks = [base, 3 * base, 2 * base] if near_first else [3 * base, 2 * base, base]
        masks = masks if 4 * base <= count else [base]
        steps.append(masks)
        base *= len(masks) + 1
    return steps


def swap(array, mask):
    if mask == 0:
        return array
    return lax.ppermute(array, "seq", [(s, s ^ mask) for s in range(lax.axis_size("seq"))])


def plane_swap(pieces):
    return [swap(piece, mask) for mask, piece in zip(ORDER, pieces)]


def plane_sum(held):
    return sum(held[1:], held[0])


def carried_in(held, reverse, place, beside=None, operands=()):
    total, arrived, steps, result = plane_sum(held), [], exchange_steps(reverse), None
    for masks in steps:
        if beside and masks == steps[-1]:
            result = beside(*operands)
        got = [swap(total, mask) for mask in masks]
        if result is not None:
            got, result = lax.optimization_barrier((got, result))
        elif len(masks) > 1:
            got = lax.optimization_barrier(got)
        arrived += got
        total = sum(got, total)
    single = whole(*total.shape)
    back = call(
        functools.partial(prefix_body, reverse, sum(steps, [])),
        [single] * (1 + len(arrived) + GROUP),
        [single] * GROUP,
        [jax.ShapeDtypeStruct(total.shape, jnp.float32)] * GROUP,
        1 << 24,
        "prefix",
        scratch=[pltpu.VMEM((GROUP, DH, DH), jnp.float32)],
    )(place, total, *arrived, *held)
    return plane_swap(back), result


def local(queries, keys, values, out_gain, grad_out):
    full = queries.shape
    flat = (full[0] * full[1], full[2])
    assert flat == (BLOCK, HEADS * DH) and lax.axis_size("seq") % GROUP == 0
    query, key, value, grad = (a.reshape(flat) for a in (queries, keys, values, grad_out))
    gain = out_gain.reshape(1, HEADS * DH)
    square = jax.ShapeDtypeStruct((DH, DH), jnp.float32)
    taller = jax.ShapeDtypeStruct((DH + GAIN_ROWS, DH), jnp.float32)
    full_float = jax.ShapeDtypeStruct(flat, jnp.float32)
    full_low = jax.ShapeDtypeStruct(flat, jnp.bfloat16)
    turned_low = jax.ShapeDtypeStruct(flat[::-1], jnp.bfloat16)
    half_float = jax.ShapeDtypeStruct((BLOCK, WIDE), jnp.float32)
    half_low = jax.ShapeDtypeStruct((BLOCK, WIDE), jnp.bfloat16)
    short, tall, wide, half = whole(*square.shape), whole(*taller.shape), whole(*flat), whole(BLOCK, WIDE)
    unit = 2 * BLOCK * DH * DH * HEADS

    place = lax.axis_index("seq").astype(jnp.int32).reshape(1)
    deltas = call(
        delta_body,
        [pl.BlockSpec(memory_space=pltpu.HBM)] * 2,
        [short] * HEADS,
        [square] * HEADS,
        6 * unit,
        "delta",
        scratch=[pltpu.VMEM(flat, jnp.bfloat16)] * 2 + [pltpu.SemaphoreType.DMA((PARTS, 2))],
    )(place, *[pltpu.with_memory_space_constraint(a, pltpu.HBM) for a in (key, value)])
    chains = [slice(chain * GROUP, (chain + 1) * GROUP) for chain in range(CHAINS)]
    inner_call = call(
        lambda place_ref, *refs: inner_body(*refs),
        [wide] * 3,
        [wide, whole(*turned_low.shape)],
        [full_float, turned_low],
        16 * unit,
        "inner",
    )
    first, second = [lax.optimization_barrier(plane_swap(deltas[chain])) for chain in chains]
    second, operands = lax.optimization_barrier((second, (place, query, key, value)))
    state, (inner, turned) = carried_in(first, False, place, inner_call, operands)
    states = [state, carried_in(second, False, place)[0]]
    attns, later = [], []
    for chain in range(CHAINS):
        attn, *deltas = call(
            functools.partial(norm_body, chain),
            [wide, whole(*turned_low.shape), wide, wide, whole(1, HEADS * DH)] + [short] * GROUP,
            [half] + [tall] * GROUP,
            [half_low] + [taller] * GROUP,
            8 * unit,
            "norm",
        )(place, query, turned, grad, inner, gain, *states[chain])
        attns.append(attn)
        held = lax.optimization_barrier(plane_swap(deltas))
        later += carried_in(held, True, place)[0]
    chunks = [pl.BlockSpec((BLOCK, WIDE), lambda step, chain=chain: (0, chain)) for chain in range(CHAINS)]
    grad_query, grad_key, grad_value, key_part, value_part = call(
        partial_body,
        [wide] * 3 + [whole(*turned_low.shape)] + [half] * CHAINS + [short] * HEADS + [tall] * GROUP,
        [wide] + [chunks[0]] * 2 + [half] * 2,
        [full_low] * 3 + [half_float] * 2,
        48 * unit,
        "partial",
    )(place, query, key, value, turned, *attns, *[state for chain in states for state in chain], *later[:GROUP])
    gain_terms = call(
        gain_body, [tall] * HEADS, whole(HEADS, DH), jax.ShapeDtypeStruct((HEADS, DH), jnp.float32), unit, "gain"
    )(place, *later)
    gain_terms, value_part = lax.optimization_barrier((gain_terms, value_part))
    docs, mask = lax.axis_size("dp"), 1
    while mask < docs:
        gain_terms = gain_terms + lax.ppermute(gain_terms, "dp", [(d, d ^ mask) for d in range(docs)])
        mask *= 2
    grad_key, grad_value = call(
        final_body,
        [wide] * 2 + [half] * 2 + [tall] * GROUP + [pl.BlockSpec(memory_space=pl.ANY)] * 2,
        [chunks[1]] * 2,
        [full_low] * 2,
        8 * unit,
        "final",
        aliases={5 + GROUP: 0, 6 + GROUP: 1},
    )(place, key, value, key_part, value_part, *later[GROUP:], grad_key, grad_value)
    grad_gain = gain_terms / math.sqrt(lax.axis_size("seq") * docs * BLOCK)
    return (
        grad_query.reshape(full),
        grad_key.reshape(full),
        grad_value.reshape(full),
        grad_gain.reshape(HEADS * DH),
    )


def solution(mesh):
    sharded = P("dp", "seq", None)
    return jax.shard_map(
        local,
        mesh=mesh,
        in_specs=(sharded, sharded, sharded, P(), sharded),
        out_specs=(sharded, sharded, sharded, P()),
        check_vma=False,
    )
```

```python
import functools
import math

import jax
import jax.numpy as jnp
from jax import lax
from jax.experimental import pallas as pl
from jax.experimental.pallas import tpu as pltpu
from jax.sharding import PartitionSpec as P

HEADS = 8
DH = 128
BLOCK = 256
GROUP = 4
CHAINS = HEADS // GROUP
WIDE = GROUP * DH
GAIN_ROWS = 8
ORDER = (0, 3, 2, 1)
PARTS = 2
PART_ROWS = BLOCK // PARTS
EPSILON = 1e-06

NT = (((1,), (1,)), ((), ()))
TN = (((0,), (0,)), ((), ()))
NN = (((1,), (0,)), ((), ()))


def dot(left, right, dims):
    return lax.dot_general(left, right, dims, preferred_element_type=jnp.float32)


def columns(head):
    return pl.ds(head * DH, DH)


def own_columns(place_ref, mask, chain=0):
    return pl.ds(pl.multiple_of(chain * WIDE + (place_ref[0] & (GROUP - 1) ^ mask) * DH, DH), DH)


def causal(turned=False):
    shape, first = (BLOCK, BLOCK), int(turned)
    return lax.broadcasted_iota(jnp.int32, shape, first) >= lax.broadcasted_iota(jnp.int32, shape, 1 - first)


def delta_body(place_ref, key_ref, value_ref, *refs):
    delta_refs, (key_here, value_here, sems) = refs[:HEADS], refs[HEADS:]
    copies = []
    for part in range(PARTS):
        rows = pl.ds(part * PART_ROWS, PART_ROWS)
        for side, (source, here) in enumerate(((key_ref, key_here), (value_ref, value_here))):
            copies.append(pltpu.make_async_copy(source.at[rows], here.at[rows], sems.at[part, side]))
            copies[-1].start()
    for part in range(PARTS):
        rows = pl.ds(part * PART_ROWS, PART_ROWS)
        for copy in copies[2 * part : 2 * part + 2]:
            copy.wait()
        for at_head, delta_ref in enumerate(delta_refs):
            at = own_columns(place_ref, ORDER[at_head % GROUP], at_head // GROUP)
            delta = dot(key_here[rows, at], value_here[rows, at], TN)
            delta_ref[...] = delta if part == 0 else delta_ref[...] + delta


def inner_body(query_ref, key_ref, value_ref, inner_ref, turned_ref):
    keep = causal()
    for head in range(HEADS):
        at = columns(head)
        query = query_ref[:, at]
        scores = jnp.where(keep, dot(query, key_ref[:, at], NT), 0.0).astype(jnp.bfloat16)
        inner_ref[:, at] = dot(scores, value_ref[:, at], NN)
        turned_ref[at, :] = query.T


def norm_body(chain, place_ref, query_ref, turned_ref, grad_ref, inner_ref, gain_ref, *refs):
    state_refs, (attn_ref, *delta_refs) = refs[:GROUP], refs[GROUP:]
    for mask, state_ref, delta_ref in zip(ORDER, state_refs, delta_refs):
        at = own_columns(place_ref, mask, chain)
        query = query_ref[:, at]
        attn = inner_ref[:, at] + dot(query, state_ref[...].astype(jnp.bfloat16), NN)
        per_root = lax.rsqrt(jnp.mean(attn * attn, axis=-1, keepdims=True) + EPSILON)
        normed = attn * per_root
        cotangent = grad_ref[:, at].astype(jnp.float32)
        product = normed * cotangent
        gain = gain_ref[:, at]
        shared = jnp.mean(product * gain, axis=-1, keepdims=True)
        grad_attn = ((gain * cotangent - normed * shared) * per_root).astype(jnp.bfloat16)
        attn_ref[:, own_columns(place_ref, mask)] = grad_attn
        delta_ref[:DH] = dot(turned_ref[at, :], grad_attn, NN)
        delta_ref[DH:] = jnp.broadcast_to(jnp.sum(product, axis=0, keepdims=True), (GAIN_ROWS, DH))


def partial_body(place_ref, query_ref, key_ref, value_ref, turned_ref, *refs):
    attn_refs, state_refs = refs[:CHAINS], refs[CHAINS : CHAINS + HEADS]
    later_refs, (grad_query_ref, *out_refs) = refs[CHAINS + HEADS : -5], refs[-5:]
    keep, kept = causal(), causal(True)
    for at_head, state_ref in enumerate(state_refs):
        chain, mask = at_head // GROUP, ORDER[at_head % GROUP]
        at, here = own_columns(place_ref, mask, chain), own_columns(place_ref, mask)
        query, key, value, grad_attn = query_ref[:, at], key_ref[:, at], value_ref[:, at], attn_refs[chain][:, here]
        turned = jnp.where(kept, dot(key, turned_ref[at, :], NN), 0.0).astype(jnp.bfloat16)
        grad_scores = jnp.where(keep, dot(grad_attn, value, NT), 0.0).astype(jnp.bfloat16)
        turned_grad = jnp.where(kept, dot(value, grad_attn, NT), 0.0).astype(jnp.bfloat16)
        carried = dot(grad_attn, state_ref[...].astype(jnp.bfloat16), NT)
        grad_query_ref[:, at] = (dot(grad_scores, key, NN) + carried).astype(jnp.bfloat16)
        parts = [dot(turned_grad, query, NN), dot(turned, grad_attn, NN)]
        if chain == 0:
            state = later_refs[at_head][:DH].astype(jnp.bfloat16)
            parts = [parts[0] + dot(value, state, NT), parts[1] + dot(key, state, NN)]
        for part, out_ref in zip(parts, out_refs[2 * chain :]):
            out_ref[:, here] = part.astype(out_ref.dtype)


def final_body(place_ref, key_ref, value_ref, key_part_ref, value_part_ref, *refs):
    state_refs, (grad_key_ref, grad_value_ref) = refs[:GROUP], refs[-2:]
    for mask, state_ref in zip(ORDER, state_refs):
        at, here = own_columns(place_ref, mask, 1), own_columns(place_ref, mask)
        state = state_ref[:DH].astype(jnp.bfloat16)
        grad_key_ref[:, here] = (key_part_ref[:, here] + dot(value_ref[:, at], state, NT)).astype(jnp.bfloat16)
        grad_value_ref[:, here] = (value_part_ref[:, here] + dot(key_ref[:, at], state, NN)).astype(jnp.bfloat16)


def gain_body(place_ref, *refs):
    for at_head, state_ref in enumerate(refs[:-1]):
        row = (at_head // GROUP) * GROUP + (place_ref[0] & (GROUP - 1) ^ ORDER[at_head % GROUP])
        refs[-1][pl.ds(row, 1), :] = state_ref[DH : DH + 1]


def prefix_body(reverse, masks, place_ref, *refs):
    (total_ref, *arrived_refs), (*back_refs, ahead) = refs[: -2 * GROUP - 1], refs[-GROUP - 1 :]
    held_refs = refs[-2 * GROUP - 1 : -GROUP - 1]
    for mask, held_ref in zip(ORDER, held_refs):
        ahead[pl.ds(place_ref[0] & (GROUP - 1) ^ mask, 1)] = held_ref[:DH][None]
    running = jnp.zeros((DH, DH), jnp.float32)
    for mask, arrived_ref in zip(masks, arrived_refs):
        later = (place_ref[0] ^ mask < place_ref[0]) != reverse
        running = running + jnp.where(later, arrived_ref[:DH], 0.0)
    for member in reversed(range(GROUP)) if reverse else range(GROUP):
        own = ahead[member]
        ahead[member] = running
        running = running + own
    for mask, back_ref in zip(ORDER, back_refs):
        back_ref[:DH] = ahead[pl.ds(place_ref[0] & (GROUP - 1) ^ mask, 1)][0]
        if back_ref.shape[0] > DH:
            back_ref[DH:] = total_ref[DH:]


def whole(*shape):
    return pl.BlockSpec(shape, lambda step: (0,) * len(shape))


PLACE = pl.BlockSpec(memory_space=pltpu.SMEM)


def call(body, in_specs, out_specs, outs, flops, name, steps=1, scratch=(), aliases=None):
    return pl.pallas_call(
        body,
        grid=(steps,),
        in_specs=[PLACE] + in_specs,
        out_specs=out_specs,
        out_shape=outs,
        scratch_shapes=scratch,
        input_output_aliases=aliases or {},
        compiler_params=pltpu.CompilerParams(vmem_limit_bytes=16 * 1024 * 1024),
        cost_estimate=pl.CostEstimate(flops=flops, bytes_accessed=2 << 20, transcendentals=0),
        name=name,
    )


def exchange_steps(near_first):
    count, base, steps = lax.axis_size("seq"), GROUP, []
    while base < count:
        masks = [base, 3 * base, 2 * base] if near_first else [2 * base, 3 * base, base]
        masks = masks if 4 * base <= count else [base]
        steps.append(masks)
        base *= len(masks) + 1
    return steps


def swap(array, mask):
    if mask == 0:
        return array
    return lax.ppermute(array, "seq", [(s, s ^ mask) for s in range(lax.axis_size("seq"))])


def plane_swap(pieces):
    return [swap(piece, mask) for mask, piece in zip(ORDER, pieces)]


def plane_sum(held):
    return sum(held[1:], held[0])


def carried_in(held, reverse, place, beside=None, operands=()):
    total, arrived, steps, result = plane_sum(held), [], exchange_steps(reverse), None
    for masks in steps:
        if beside and masks == steps[-1]:
            result = beside(*operands)
        got = [swap(total, mask) for mask in masks]
        if result is not None:
            got, result = lax.optimization_barrier((got, result))
        elif len(masks) > 1:
            got = lax.optimization_barrier(got)
        arrived += got
        total = sum(got, total)
    single = whole(*total.shape)
    back = call(
        functools.partial(prefix_body, reverse, sum(steps, [])),
        [single] * (1 + len(arrived) + GROUP),
        [single] * GROUP,
        [jax.ShapeDtypeStruct(total.shape, jnp.float32)] * GROUP,
        1 << 24,
        "prefix",
        scratch=[pltpu.VMEM((GROUP, DH, DH), jnp.float32)],
    )(place, total, *arrived, *held)
    return plane_swap(back), result


def local(queries, keys, values, out_gain, grad_out):
    full = queries.shape
    flat = (full[0] * full[1], full[2])
    assert flat == (BLOCK, HEADS * DH) and lax.axis_size("seq") % GROUP == 0
    query, key, value, grad = (a.reshape(flat) for a in (queries, keys, values, grad_out))
    gain = out_gain.reshape(1, HEADS * DH)
    square = jax.ShapeDtypeStruct((DH, DH), jnp.float32)
    taller = jax.ShapeDtypeStruct((DH + GAIN_ROWS, DH), jnp.float32)
    full_float = jax.ShapeDtypeStruct(flat, jnp.float32)
    full_low = jax.ShapeDtypeStruct(flat, jnp.bfloat16)
    turned_low = jax.ShapeDtypeStruct(flat[::-1], jnp.bfloat16)
    half_float = jax.ShapeDtypeStruct((BLOCK, WIDE), jnp.float32)
    half_low = jax.ShapeDtypeStruct((BLOCK, WIDE), jnp.bfloat16)
    short, tall, wide, half = whole(*square.shape), whole(*taller.shape), whole(*flat), whole(BLOCK, WIDE)
    unit = 2 * BLOCK * DH * DH * HEADS

    place = lax.axis_index("seq").astype(jnp.int32).reshape(1)
    deltas = call(
        delta_body,
        [pl.BlockSpec(memory_space=pltpu.HBM)] * 2,
        [short] * HEADS,
        [square] * HEADS,
        6 * unit,
        "delta",
        scratch=[pltpu.VMEM(flat, jnp.bfloat16)] * 2 + [pltpu.SemaphoreType.DMA((PARTS, 2))],
    )(place, *[pltpu.with_memory_space_constraint(a, pltpu.HBM) for a in (key, value)])
    chains = [slice(chain * GROUP, (chain + 1) * GROUP) for chain in range(CHAINS)]
    inner_call = call(
        lambda place_ref, *refs: inner_body(*refs),
        [wide] * 3,
        [wide, whole(*turned_low.shape)],
        [full_float, turned_low],
        16 * unit,
        "inner",
    )
    first, second = [lax.optimization_barrier(plane_swap(deltas[chain])) for chain in chains]
    second, operands = lax.optimization_barrier((second, (place, query, key, value)))
    state, (inner, turned) = carried_in(first, False, place, inner_call, operands)
    states = [state, carried_in(second, False, place)[0]]
    attns, later = [], []
    for chain in range(CHAINS):
        attn, *deltas = call(
            functools.partial(norm_body, chain),
            [wide, whole(*turned_low.shape), wide, wide, whole(1, HEADS * DH)] + [short] * GROUP,
            [half] + [tall] * GROUP,
            [half_low] + [taller] * GROUP,
            8 * unit,
            "norm",
        )(place, query, turned, grad, inner, gain, *states[chain])
        attns.append(attn)
        held = lax.optimization_barrier(plane_swap(deltas))
        later += carried_in(held, True, place)[0]
    chunks = [pl.BlockSpec((BLOCK, WIDE), lambda step, chain=chain: (0, chain)) for chain in range(CHAINS)]
    grad_query, grad_key, grad_value, key_part, value_part = call(
        partial_body,
        [wide] * 3 + [whole(*turned_low.shape)] + [half] * CHAINS + [short] * HEADS + [tall] * GROUP,
        [wide] + [chunks[0]] * 2 + [half] * 2,
        [full_low] * 3 + [half_float] * 2,
        48 * unit,
        "partial",
    )(place, query, key, value, turned, *attns, *[state for chain in states for state in chain], *later[:GROUP])
    gain_terms = call(
        gain_body, [tall] * HEADS, whole(HEADS, DH), jax.ShapeDtypeStruct((HEADS, DH), jnp.float32), unit, "gain"
    )(place, *later)
    gain_terms, value_part = lax.optimization_barrier((gain_terms, value_part))
    docs, mask = lax.axis_size("dp"), 1
    while mask < docs:
        gain_terms = gain_terms + lax.ppermute(gain_terms, "dp", [(d, d ^ mask) for d in range(docs)])
        mask *= 2
    grad_key, grad_value = call(
        final_body,
        [wide] * 2 + [half] * 2 + [tall] * GROUP + [pl.BlockSpec(memory_space=pl.ANY)] * 2,
        [chunks[1]] * 2,
        [full_low] * 2,
        8 * unit,
        "final",
        aliases={5 + GROUP: 0, 6 + GROUP: 1},
    )(place, key, value, key_part, value_part, *later[GROUP:], grad_key, grad_value)
    grad_gain = gain_terms / math.sqrt(lax.axis_size("seq") * docs * BLOCK)
    return (
        grad_query.reshape(full),
        grad_key.reshape(full),
        grad_value.reshape(full),
        grad_gain.reshape(HEADS * DH),
    )


def solution(mesh):
    sharded = P("dp", "seq", None)
    return jax.shard_map(
        local,
        mesh=mesh,
        in_specs=(sharded, sharded, sharded, P(), sharded),
        out_specs=(sharded, sharded, sharded, P()),
        check_vma=False,
    )
```

```python
import functools
import math

import jax
import jax.numpy as jnp
from jax import lax
from jax.experimental import pallas as pl
from jax.experimental.pallas import tpu as pltpu
from jax.sharding import PartitionSpec as P

HEADS = 8
DH = 128
BLOCK = 256
GROUP = 4
CHAINS = HEADS // GROUP
WIDE = GROUP * DH
GAIN_ROWS = 8
ORDER = (0, 3, 2, 1)
PARTS = 2
PART_ROWS = BLOCK // PARTS
EPSILON = 1e-06

NT = (((1,), (1,)), ((), ()))
TN = (((0,), (0,)), ((), ()))
NN = (((1,), (0,)), ((), ()))


def dot(left, right, dims):
    return lax.dot_general(left, right, dims, preferred_element_type=jnp.float32)


def columns(head):
    return pl.ds(head * DH, DH)


def own_columns(place_ref, mask, chain=0):
    return pl.ds(pl.multiple_of(chain * WIDE + (place_ref[0] & (GROUP - 1) ^ mask) * DH, DH), DH)


def causal(turned=False):
    shape, first = (BLOCK, BLOCK), int(turned)
    return lax.broadcasted_iota(jnp.int32, shape, first) >= lax.broadcasted_iota(jnp.int32, shape, 1 - first)


def delta_body(place_ref, key_ref, value_ref, *refs):
    delta_refs, (key_here, value_here, sems) = refs[:HEADS], refs[HEADS:]
    copies = []
    for part in range(PARTS):
        rows = pl.ds(part * PART_ROWS, PART_ROWS)
        for side, (source, here) in enumerate(((key_ref, key_here), (value_ref, value_here))):
            copies.append(pltpu.make_async_copy(source.at[rows], here.at[rows], sems.at[part, side]))
            copies[-1].start()
    for part in range(PARTS):
        rows = pl.ds(part * PART_ROWS, PART_ROWS)
        for copy in copies[2 * part : 2 * part + 2]:
            copy.wait()
        for at_head, delta_ref in enumerate(delta_refs):
            at = own_columns(place_ref, ORDER[at_head % GROUP], at_head // GROUP)
            delta = dot(key_here[rows, at], value_here[rows, at], TN)
            delta_ref[...] = delta if part == 0 else delta_ref[...] + delta


def inner_body(query_ref, key_ref, value_ref, inner_ref, turned_ref):
    keep = causal()
    for head in range(HEADS):
        at = columns(head)
        query = query_ref[:, at]
        scores = jnp.where(keep, dot(query, key_ref[:, at], NT), 0.0).astype(jnp.bfloat16)
        inner_ref[:, at] = dot(scores, value_ref[:, at], NN)
        turned_ref[at, :] = query.T


def norm_body(chain, place_ref, query_ref, turned_ref, grad_ref, inner_ref, gain_ref, *refs):
    state_refs, (attn_ref, *delta_refs) = refs[:GROUP], refs[GROUP:]
    for mask, state_ref, delta_ref in zip(ORDER, state_refs, delta_refs):
        at = own_columns(place_ref, mask, chain)
        query = query_ref[:, at]
        attn = inner_ref[:, at] + dot(query, state_ref[...].astype(jnp.bfloat16), NN)
        per_root = lax.rsqrt(jnp.mean(attn * attn, axis=-1, keepdims=True) + EPSILON)
        normed = attn * per_root
        cotangent = grad_ref[:, at].astype(jnp.float32)
        product = normed * cotangent
        gain = gain_ref[:, at]
        shared = jnp.mean(product * gain, axis=-1, keepdims=True)
        grad_attn = ((gain * cotangent - normed * shared) * per_root).astype(jnp.bfloat16)
        attn_ref[:, own_columns(place_ref, mask)] = grad_attn
        delta_ref[:DH] = dot(turned_ref[at, :], grad_attn, NN)
        delta_ref[DH:] = jnp.broadcast_to(jnp.sum(product, axis=0, keepdims=True), (GAIN_ROWS, DH))


def partial_body(place_ref, query_ref, key_ref, value_ref, turned_ref, *refs):
    attn_refs, state_refs = refs[:CHAINS], refs[CHAINS : CHAINS + HEADS]
    later_refs, (grad_query_ref, *out_refs) = refs[CHAINS + HEADS : -5], refs[-5:]
    keep, kept = causal(), causal(True)
    for at_head, state_ref in enumerate(state_refs):
        chain, mask = at_head // GROUP, ORDER[at_head % GROUP]
        at, here = own_columns(place_ref, mask, chain), own_columns(place_ref, mask)
        query, key, value, grad_attn = query_ref[:, at], key_ref[:, at], value_ref[:, at], attn_refs[chain][:, here]
        turned = jnp.where(kept, dot(key, turned_ref[at, :], NN), 0.0).astype(jnp.bfloat16)
        grad_scores = jnp.where(keep, dot(grad_attn, value, NT), 0.0).astype(jnp.bfloat16)
        turned_grad = jnp.where(kept, dot(value, grad_attn, NT), 0.0).astype(jnp.bfloat16)
        carried = dot(grad_attn, state_ref[...].astype(jnp.bfloat16), NT)
        grad_query_ref[:, at] = (dot(grad_scores, key, NN) + carried).astype(jnp.bfloat16)
        parts = [dot(turned_grad, query, NN), dot(turned, grad_attn, NN)]
        if chain == 0:
            state = later_refs[at_head][:DH].astype(jnp.bfloat16)
            parts = [parts[0] + dot(value, state, NT), parts[1] + dot(key, state, NN)]
        for part, out_ref in zip(parts, out_refs[2 * chain :]):
            out_ref[:, here] = part.astype(out_ref.dtype)


def final_body(place_ref, key_ref, value_ref, key_part_ref, value_part_ref, *refs):
    state_refs, (grad_key_ref, grad_value_ref) = refs[:GROUP], refs[-2:]
    for mask, state_ref in zip(ORDER, state_refs):
        at, here = own_columns(place_ref, mask, 1), own_columns(place_ref, mask)
        state = state_ref[:DH].astype(jnp.bfloat16)
        grad_key_ref[:, here] = (key_part_ref[:, here] + dot(value_ref[:, at], state, NT)).astype(jnp.bfloat16)
        grad_value_ref[:, here] = (value_part_ref[:, here] + dot(key_ref[:, at], state, NN)).astype(jnp.bfloat16)


def gain_body(place_ref, *refs):
    for at_head, state_ref in enumerate(refs[:-1]):
        row = (at_head // GROUP) * GROUP + (place_ref[0] & (GROUP - 1) ^ ORDER[at_head % GROUP])
        refs[-1][pl.ds(row, 1), :] = state_ref[DH : DH + 1]


def prefix_body(reverse, masks, place_ref, *refs):
    (total_ref, *arrived_refs), (*back_refs, ahead) = refs[: -2 * GROUP - 1], refs[-GROUP - 1 :]
    held_refs = refs[-2 * GROUP - 1 : -GROUP - 1]
    for mask, held_ref in zip(ORDER, held_refs):
        ahead[pl.ds(place_ref[0] & (GROUP - 1) ^ mask, 1)] = held_ref[:DH][None]
    running = jnp.zeros((DH, DH), jnp.float32)
    for mask, arrived_ref in zip(masks, arrived_refs):
        later = (place_ref[0] ^ mask < place_ref[0]) != reverse
        running = running + jnp.where(later, arrived_ref[:DH], 0.0)
    for member in reversed(range(GROUP)) if reverse else range(GROUP):
        own = ahead[member]
        ahead[member] = running
        running = running + own
    for mask, back_ref in zip(ORDER, back_refs):
        back_ref[:DH] = ahead[pl.ds(place_ref[0] & (GROUP - 1) ^ mask, 1)][0]
        if back_ref.shape[0] > DH:
            back_ref[DH:] = total_ref[DH:]


def whole(*shape):
    return pl.BlockSpec(shape, lambda step: (0,) * len(shape))


PLACE = pl.BlockSpec(memory_space=pltpu.SMEM)


def call(body, in_specs, out_specs, outs, flops, name, steps=1, scratch=(), aliases=None):
    return pl.pallas_call(
        body,
        grid=(steps,),
        in_specs=[PLACE] + in_specs,
        out_specs=out_specs,
        out_shape=outs,
        scratch_shapes=scratch,
        input_output_aliases=aliases or {},
        compiler_params=pltpu.CompilerParams(vmem_limit_bytes=16 * 1024 * 1024),
        cost_estimate=pl.CostEstimate(flops=flops, bytes_accessed=2 << 20, transcendentals=0),
        name=name,
    )


def exchange_steps(near_first):
    count, base, steps = lax.axis_size("seq"), GROUP, []
    while base < count:
        masks = [3 * base, base, 2 * base] if near_first else [3 * base, 2 * base, base]
        masks = masks if 4 * base <= count else [base]
        steps.append(masks)
        base *= len(masks) + 1
    return steps


def swap(array, mask):
    if mask == 0:
        return array
    return lax.ppermute(array, "seq", [(s, s ^ mask) for s in range(lax.axis_size("seq"))])


def plane_swap(pieces):
    return [swap(piece, mask) for mask, piece in zip(ORDER, pieces)]


def plane_sum(held):
    return sum(held[1:], held[0])


def carried_in(held, reverse, place, beside=None, operands=()):
    total, arrived, steps, result = plane_sum(held), [], exchange_steps(reverse), None
    for masks in steps:
        if beside and masks == steps[-1]:
            result = beside(*operands)
        got = [swap(total, mask) for mask in masks]
        if result is not None:
            got, result = lax.optimization_barrier((got, result))
        elif len(masks) > 1:
            got = lax.optimization_barrier(got)
        arrived += got
        total = sum(got, total)
    single = whole(*total.shape)
    back = call(
        functools.partial(prefix_body, reverse, sum(steps, [])),
        [single] * (1 + len(arrived) + GROUP),
        [single] * GROUP,
        [jax.ShapeDtypeStruct(total.shape, jnp.float32)] * GROUP,
        1 << 24,
        "prefix",
        scratch=[pltpu.VMEM((GROUP, DH, DH), jnp.float32)],
    )(place, total, *arrived, *held)
    return plane_swap(back), result


def local(queries, keys, values, out_gain, grad_out):
    full = queries.shape
    flat = (full[0] * full[1], full[2])
    assert flat == (BLOCK, HEADS * DH) and lax.axis_size("seq") % GROUP == 0
    query, key, value, grad = (a.reshape(flat) for a in (queries, keys, values, grad_out))
    gain = out_gain.reshape(1, HEADS * DH)
    square = jax.ShapeDtypeStruct((DH, DH), jnp.float32)
    taller = jax.ShapeDtypeStruct((DH + GAIN_ROWS, DH), jnp.float32)
    full_float = jax.ShapeDtypeStruct(flat, jnp.float32)
    full_low = jax.ShapeDtypeStruct(flat, jnp.bfloat16)
    turned_low = jax.ShapeDtypeStruct(flat[::-1], jnp.bfloat16)
    half_float = jax.ShapeDtypeStruct((BLOCK, WIDE), jnp.float32)
    half_low = jax.ShapeDtypeStruct((BLOCK, WIDE), jnp.bfloat16)
    short, tall, wide, half = whole(*square.shape), whole(*taller.shape), whole(*flat), whole(BLOCK, WIDE)
    unit = 2 * BLOCK * DH * DH * HEADS

    place = lax.axis_index("seq").astype(jnp.int32).reshape(1)
    deltas = call(
        delta_body,
        [pl.BlockSpec(memory_space=pltpu.HBM)] * 2,
        [short] * HEADS,
        [square] * HEADS,
        6 * unit,
        "delta",
        scratch=[pltpu.VMEM(flat, jnp.bfloat16)] * 2 + [pltpu.SemaphoreType.DMA((PARTS, 2))],
    )(place, *[pltpu.with_memory_space_constraint(a, pltpu.HBM) for a in (key, value)])
    chains = [slice(chain * GROUP, (chain + 1) * GROUP) for chain in range(CHAINS)]
    inner_call = call(
        lambda place_ref, *refs: inner_body(*refs),
        [wide] * 3,
        [wide, whole(*turned_low.shape)],
        [full_float, turned_low],
        16 * unit,
        "inner",
    )
    first, second = [lax.optimization_barrier(plane_swap(deltas[chain])) for chain in chains]
    second, operands = lax.optimization_barrier((second, (place, query, key, value)))
    state, (inner, turned) = carried_in(first, False, place, inner_call, operands)
    states = [state, carried_in(second, False, place)[0]]
    attns, later = [], []
    for chain in range(CHAINS):
        attn, *deltas = call(
            functools.partial(norm_body, chain),
            [wide, whole(*turned_low.shape), wide, wide, whole(1, HEADS * DH)] + [short] * GROUP,
            [half] + [tall] * GROUP,
            [half_low] + [taller] * GROUP,
            8 * unit,
            "norm",
        )(place, query, turned, grad, inner, gain, *states[chain])
        attns.append(attn)
        held = lax.optimization_barrier(plane_swap(deltas))
        later += carried_in(held, True, place)[0]
    chunks = [pl.BlockSpec((BLOCK, WIDE), lambda step, chain=chain: (0, chain)) for chain in range(CHAINS)]
    grad_query, grad_key, grad_value, key_part, value_part = call(
        partial_body,
        [wide] * 3 + [whole(*turned_low.shape)] + [half] * CHAINS + [short] * HEADS + [tall] * GROUP,
        [wide] + [chunks[0]] * 2 + [half] * 2,
        [full_low] * 3 + [half_float] * 2,
        48 * unit,
        "partial",
    )(place, query, key, value, turned, *attns, *[state for chain in states for state in chain], *later[:GROUP])
    gain_terms = call(
        gain_body, [tall] * HEADS, whole(HEADS, DH), jax.ShapeDtypeStruct((HEADS, DH), jnp.float32), unit, "gain"
    )(place, *later)
    gain_terms, value_part = lax.optimization_barrier((gain_terms, value_part))
    docs, mask = lax.axis_size("dp"), 1
    while mask < docs:
        gain_terms = gain_terms + lax.ppermute(gain_terms, "dp", [(d, d ^ mask) for d in range(docs)])
        mask *= 2
    grad_key, grad_value = call(
        final_body,
        [wide] * 2 + [half] * 2 + [tall] * GROUP + [pl.BlockSpec(memory_space=pl.ANY)] * 2,
        [chunks[1]] * 2,
        [full_low] * 2,
        8 * unit,
        "final",
        aliases={5 + GROUP: 0, 6 + GROUP: 1},
    )(place, key, value, key_part, value_part, *later[GROUP:], grad_key, grad_value)
    grad_gain = gain_terms / math.sqrt(lax.axis_size("seq") * docs * BLOCK)
    return (
        grad_query.reshape(full),
        grad_key.reshape(full),
        grad_value.reshape(full),
        grad_gain.reshape(HEADS * DH),
    )


def solution(mesh):
    sharded = P("dp", "seq", None)
    return jax.shard_map(
        local,
        mesh=mesh,
        in_specs=(sharded, sharded, sharded, P(), sharded),
        out_specs=(sharded, sharded, sharded, P()),
        check_vma=False,
    )
```
